32 devices in a mesh: section: 2 (over core), dp: 4 (over z), tensor: 4 (over y, x).
Axes of the slice: x: 2, y: 2, z: 4, core: 2. Of those that a mesh axis runs over, the one named last changes fastest.
Arguments:
- inputs: bfloat16 [4, 2048, 768], P(None, 'dp'), may hold values from -6 to 6
- out_grad: bfloat16 [4, 2048, 768], P(None, 'dp'), may hold values from -6 to 6
- items: int32 [2, 4, 2048], P('section', None, 'dp'), may hold values from 0 to 5, never falling along the last dimension, each value on 1 to 1024 neighbouring positions
- send_order: int32 [2, 4, 4, 512], P('section', None, 'dp'), may hold values from 0 to 511, each once within a row
- recv_order: int32 [2, 4, 4, 512], P('section', None, 'dp'), may hold values from 0 to 511, each once within a row
- attn_weight: bfloat16 [2, 768, 3, 768], P('section', None, None, 'tensor'), may hold values from -0.21875 to 0.21875
- qv_bias: float32 [2, 2, 768], P('section', None, 'tensor'), may hold values from -3 to 3
- out_weight: bfloat16 [2, 768, 768], P('section', 'tensor'), may hold values from -0.625 to 0.625
- out_bias: float32 [2, 768], P('section'), may hold values from -3 to 3
- norm_first: float32 [2, 2, 768], P('section'), may hold values from 0.25 to 1.75
- up_weight: bfloat16 [2, 768, 3072], P('section', None, 'tensor'), may hold values from -0.21875 to 0.21875
- up_bias: float32 [2, 3072], P('section', 'tensor'), may hold values from -3 to 3
- down_weight: bfloat16 [2, 3072, 768], P('section', 'tensor'), may hold values from -0.109375 to 0.109375
- down_bias: float32 [2, 768], P('section'), may hold values from -3 to 3
- norm_second: float32 [2, 2, 768], P('section'), may hold values from 0.25 to 1.75
Outputs:
- activations: bfloat16 [2, 4, 2048, 768], P('section', None, 'dp')
- input_grads: float32 [2, 4, 2048, 768], P('section', None, 'dp')
- entropy_log: float32 [2, 4, 16, 12], P('section', None, 'dp', 'tensor')
- occupancy_log: float32 [2, 4, 16, 6], P('section', None, 'dp')
- attn_weight_grad: float32 [2, 768, 3, 768], P('section', 'dp', None, 'tensor')
- qv_bias_grad: float32 [2, 2, 768], P('section', None, 'tensor')
- out_weight_grad: float32 [2, 768, 768], P('section', 'tensor', 'dp')
- out_bias_grad: float32 [2, 768], P('section')
- norm_first_grad: float32 [2, 2, 768], P('section')
- up_weight_grad: float32 [2, 768, 3072], P('section', 'dp', 'tensor')
- up_bias_grad: float32 [2, 3072], P('section', 'tensor')
- down_weight_grad: float32 [2, 3072, 768], P('section', 'tensor', 'dp')
- down_bias_grad: float32 [2, 768], P('section')
- norm_second_grad: float32 [2, 2, 768], P('section')
The draws below stay inside these ranges and needn't reach their ends.
Inputs may be any that keep to these rules, and one draw needn't show every extreme that they name: Each row of items[s, m] numbers the items of the cluster slots and never falls. `send_order`: each row holds every position of one device's 512 tokens once. `recv_order`: each row holds every received position of one device once.
All inputs are finite; a program needn't handle non-finite values.
Results may differ from the reference program's by a relative error of at most 0.034.
Values may be sent and summed in bfloat16 or wider, within the bound.
A program may use at most 256 MiB of HBM per device.

```python
import math
import jax
import jax.numpy as jnp
import numpy as np
from jax import lax

D = 768
HEADS = 12
HEAD_DIM = 64
FF = 3072
CLUSTER = 128
MB = 4
ITEMS = 6
ROWS = 512
TOKENS = 2048
CLUSTERS = 16
LONGEST = 1024
N_SECTION = 2
N_DP = 4


def spiked(drawn, key, source, target, blocks, factor):
    def block_of(dim):
        return (jnp.arange(drawn.shape[dim]) // (drawn.shape[dim] // blocks)).reshape((-1,) + (1,) * (drawn.ndim - 1 - dim))

    near = jax.random.permutation(key, blocks)[block_of(target)]
    second = (block_of(target) + blocks // 2) % blocks
    return jnp.where((block_of(source) == near) | (block_of(source) == second), factor * drawn, drawn)


def levels(rng, shape, pieces, low, top_value):
    level, own = 1.0, jax.random.fold_in(rng, 6)
    for axis_at, blocks in pieces:
        steps = jnp.exp(jax.random.uniform(jax.random.fold_in(own, axis_at), (blocks,), jnp.float32, low / len(pieces), top_value / len(pieces)))
        level = level * jnp.repeat(steps, shape[axis_at] // blocks).reshape([-1 if axis == axis_at else 1 for axis in range(len(shape))])
    return level


def split_up(amount, total, limit, slope):
    portions = [(1 << 20) // math.isqrt(grade ** slope) + 1 for grade in range(2, amount + 1)]
    spare, given = total - limit - (amount - 1), [1] * (amount - 1)
    while spare > 0:
        candidates = [i for i in range(amount - 1) if given[i] < limit]
        pool, left = sum([portions[i] for i in candidates]), spare
        for i in candidates:
            more = min(limit - given[i], max(1, left * portions[i] // pool), spare)
            given[i] = given[i] + more
            spare = spare - more
    return np.array([limit] + given)


def uneven_parts(key, number_of, total, most, slope):
    if number_of == 2:
        one = jax.random.randint(key, (), max(1, total - most), min(most, total - 1) + 1)
        return jnp.stack([one, total - one])
    sizes = jnp.asarray(split_up(number_of, total, most, slope), jnp.int32)
    couples = (number_of - 1) // 2
    donor, taker = sizes[1:1 + 2 * couples:2], sizes[2:2 + 2 * couples:2]
    margin = jnp.minimum(donor - 1, most - taker)
    passed = jax.random.randint(jax.random.fold_in(key, 1), (couples,), 0, 1 << 20) % (margin + 1)
    sizes = sizes.at[1:1 + 2 * couples:2].set(donor - passed).at[2:2 + 2 * couples:2].set(taker + passed)
    return sizes[jax.random.permutation(jax.random.fold_in(key, 2), number_of)]


def centred(key, extent, scale, reach, shards=(), held_as=jnp.bfloat16):
    values = scale * jax.random.normal(key, extent, jnp.float32)
    if shards:
        values = values * levels(key, extent, shards, -0.22, 0.18)
    return jnp.clip(values, -reach, reach).astype(held_as)


def gaussian_with(stream_key, extent, scale, bound, shards, heavy, kind=jnp.bfloat16):
    values = scale * jax.random.normal(stream_key, extent, jnp.float32)
    if shards:
        values = values * levels(stream_key, extent, shards, -0.22, 0.18)
    return jnp.clip(spiked(values, jax.random.fold_in(stream_key, 3), *heavy), -bound, bound).astype(kind)


def setup_inputs(seed: int = 0) -> dict:
    key_of = jax.random.split(jax.random.key(seed), 16)
    inputs = centred(key_of[0], (MB, TOKENS, D), 1.0, 6.0, ((1, 4),))
    out_grad = gaussian_with(key_of[1], (MB, TOKENS, D), 1.0, 6.0, ((1, 4),), (1, 2, 4, 2.0))
    items = jax.vmap(lambda own: jnp.searchsorted(jnp.cumsum(uneven_parts(own, ITEMS, TOKENS, LONGEST, 1)), jnp.arange(TOKENS), side="right"))(jax.random.split(key_of[2], N_SECTION * MB)).reshape((N_SECTION, MB, TOKENS)).astype(jnp.int32)
    send_order = jax.vmap(lambda own: jax.random.permutation(own, ROWS))(jax.random.split(key_of[3], N_SECTION * MB * N_DP)).reshape((N_SECTION, MB, N_DP, ROWS)).astype(jnp.int32)
    recv_order = jax.vmap(lambda own: jax.random.permutation(own, ROWS))(jax.random.split(key_of[4], N_SECTION * MB * N_DP)).reshape((N_SECTION, MB, N_DP, ROWS)).astype(jnp.int32)
    attn_weight = centred(key_of[5], (N_SECTION, D, 3, D), D ** -0.5, 0.21875, ((0, 2), (3, 4)))
    qv_bias = centred(key_of[6], (N_SECTION, 2, D), 0.5, 3.0, ((0, 2), (2, 4)), jnp.float32)
    out_weight = centred(key_of[7], (N_SECTION, D, D), (D // 8) ** -0.5, 0.625, ((0, 2), (1, 4)))
    out_bias = centred(key_of[8], (N_SECTION, D), 0.5, 3.0, ((0, 2),), jnp.float32)
    norm_first = jnp.clip(1.0 + 0.15 * jax.random.normal(key_of[9], (N_SECTION, 2, D), jnp.float32), 0.25, 1.75)
    up_weight = centred(key_of[10], (N_SECTION, D, FF), D ** -0.5, 0.21875, ((0, 2), (2, 4)))
    up_bias = centred(key_of[11], (N_SECTION, FF), 0.5, 3.0, ((0, 2), (1, 4)), jnp.float32)
    down_weight = centred(key_of[12], (N_SECTION, FF, D), FF ** -0.5, 0.109375, ((0, 2), (1, 4)))
    down_bias = centred(key_of[13], (N_SECTION, D), 0.5, 3.0, ((0, 2),), jnp.float32)
    norm_second = jnp.clip(1.0 + 0.15 * jax.random.normal(key_of[14], (N_SECTION, 2, D), jnp.float32), 0.25, 1.75)
    return dict(inputs=inputs, out_grad=out_grad, items=items, send_order=send_order, recv_order=recv_order, attn_weight=attn_weight, qv_bias=qv_bias, out_weight=out_weight, out_bias=out_bias, norm_first=norm_first, up_weight=up_weight, up_bias=up_bias, down_weight=down_weight, down_bias=down_bias, norm_second=norm_second)


@jax.custom_vjp
def low(v):
    return lax.optimization_barrier(v.astype(jnp.bfloat16)).astype(jnp.float32)

@jax.custom_vjp
def low_back(v):
    return v

def low_keep(v):
    return (low(v), None)

def low_pass(kept, grad):
    return (grad,)

def back_keep(v):
    return (v, None)

def back_low(kept, grad):
    return (low(grad),)
low.defvjp(low_keep, low_pass)
low_back.defvjp(back_keep, back_low)
PRECISE = lax.Precision.HIGHEST
EPSILON = 1e-06

def norm_rows(values, gain, shift):
    centre = lax.optimization_barrier(jnp.mean(values, axis=-1, keepdims=True))
    spread = values - centre
    second = lax.optimization_barrier(jnp.mean(spread * spread, axis=-1, keepdims=True))
    return spread * lax.rsqrt(second + EPSILON) * gain + shift

def slot_tokens(send_rows, recv_rows):
    piece_rows = ROWS // N_DP
    owners = jnp.arange(N_DP, dtype=jnp.int32)[:, None]
    source = recv_rows // piece_rows
    offset = recv_rows % piece_rows
    local_row = send_rows[source, owners * piece_rows + offset]
    return (source * ROWS + local_row).reshape(-1).astype(jnp.int32)

def occupancy_of(item_ids):
    labels = item_ids.reshape(CLUSTERS, CLUSTER)
    numbers = jnp.arange(ITEMS, dtype=jnp.int32)
    return lax.optimization_barrier(jnp.sum((labels[:, :, None] == numbers[None, None, :]).astype(jnp.float32), axis=1))

def cluster_attention(queries, keys_all, values, item_ids):
    blocks = (CLUSTERS, CLUSTER, HEADS, HEAD_DIM)
    query_c = queries.reshape(blocks)
    key_c = keys_all.reshape(blocks)
    value_c = values.reshape(blocks)
    scores = low_back(jnp.einsum('cqhe,ckhe->chqk', query_c, key_c, precision=PRECISE) * HEAD_DIM ** (-0.5))
    labels = item_ids.reshape(CLUSTERS, CLUSTER)
    same_item = labels[:, None, :, None] == labels[:, None, None, :]
    masked = jnp.where(same_item, scores, -1e+30)
    row_peak = lax.optimization_barrier(jnp.max(masked, axis=-1, keepdims=True))
    shifted = jnp.exp(masked - row_peak)
    row_total = lax.optimization_barrier(jnp.sum(shifted, axis=-1, keepdims=True))
    attn_prob = shifted / row_total
    inner = lax.optimization_barrier(jnp.sum(jnp.where(same_item, attn_prob * (masked - row_peak), 0.0), axis=-1))
    entropy = lax.optimization_barrier(jnp.mean(jnp.log(row_total[..., 0]) - inner, axis=-1))
    mixed_rows = jnp.einsum('chqk,ckhe->cqhe', low(attn_prob), value_c, precision=PRECISE)
    return (mixed_rows.reshape(TOKENS, HEADS * HEAD_DIM), entropy)

def run_layer(params, rows_in, item_ids, slots):
    attn_weight, qv_bias, out_weight, out_bias, norm_first, up_weight, up_bias, down_weight, down_bias, norm_second = params
    bias_three = jnp.stack([qv_bias[0], jnp.zeros_like(qv_bias[0]), qv_bias[1]])
    projected = jnp.einsum('td,dsf->tsf', rows_in, attn_weight, precision=PRECISE) + bias_three[None]
    projected = low_back(low(projected))
    grouped = projected[slots].reshape(TOKENS, 3, HEADS, HEAD_DIM)
    mixed_rows, entropy = cluster_attention(grouped[:, 0], grouped[:, 1], grouped[:, 2], item_ids)
    mixed_rows = low_back(low(mixed_rows))
    restored = jnp.zeros_like(mixed_rows).at[slots].set(mixed_rows)
    attended = low_back(jnp.dot(restored, out_weight, precision=PRECISE) + out_bias)
    hidden = norm_rows(rows_in + attended, norm_first[0], norm_first[1])
    upward = low_back(jnp.dot(low(hidden), up_weight, precision=PRECISE) + up_bias)
    active = low(jax.nn.gelu(upward))
    branch = low_back(jnp.dot(active, down_weight, precision=PRECISE) + down_bias)
    return (norm_rows(hidden + branch, norm_second[0], norm_second[1]), entropy)

def reference(inputs, out_grad, items, send_order, recv_order, attn_weight, qv_bias, out_weight, out_bias, norm_first, up_weight, up_bias, down_weight, down_bias, norm_second):
    weights_all = (attn_weight, qv_bias, out_weight, out_bias, norm_first, up_weight, up_bias, down_weight, down_bias, norm_second)
    params = [tuple((weight[layer_no].astype(jnp.float32) for weight in weights_all)) for layer_no in range(N_SECTION)]
    totals = [jax.tree.map(jnp.zeros_like, params[layer_no]) for layer_no in range(N_SECTION)]
    acts_first, acts_second, grads_first, grads_second, ent_first, ent_second = ([], [], [], [], [], [])
    occ_first, occ_second = ([], [])
    for micro_no in range(MB):
        slots_first = slot_tokens(send_order[0, micro_no], recv_order[0, micro_no])
        slots_second = slot_tokens(send_order[1, micro_no], recv_order[1, micro_no])
        items_first = items[0, micro_no]
        items_second = items[1, micro_no]

        def run_first(layer_params, rows_in):
            return run_layer(layer_params, rows_in, items_first, slots_first)

        def run_second(layer_params, rows_in):
            return run_layer(layer_params, rows_in, items_second, slots_second)
        out_first, back_first, entropy_first = jax.vjp(run_first, params[0], inputs[micro_no].astype(jnp.float32), has_aux=True)
        middle = low(out_first)
        out_second, back_second, entropy_second = jax.vjp(run_second, params[1], middle, has_aux=True)
        param_second, grad_middle = back_second(out_grad[micro_no].astype(jnp.float32))
        param_first, grad_input = back_first(low(grad_middle))
        totals[0] = jax.tree.map(jnp.add, totals[0], param_first)
        totals[1] = jax.tree.map(jnp.add, totals[1], param_second)
        acts_first.append(middle.astype(jnp.bfloat16))
        acts_second.append(out_second.astype(jnp.bfloat16))
        grads_first.append(grad_input)
        grads_second.append(grad_middle)
        ent_first.append(entropy_first)
        ent_second.append(entropy_second)
        occ_first.append(occupancy_of(items_first))
        occ_second.append(occupancy_of(items_second))
    activations = jnp.stack([jnp.stack(acts_first), jnp.stack(acts_second)])
    input_grads = jnp.stack([jnp.stack(grads_first), jnp.stack(grads_second)])
    entropy_log = jnp.stack([jnp.stack(ent_first), jnp.stack(ent_second)])
    occupancy_log = jnp.stack([jnp.stack(occ_first), jnp.stack(occ_second)])
    stacked = [jnp.stack([totals[0][index], totals[1][index]]) for index in range(10)]
    return (activations, input_grads, entropy_log, occupancy_log, stacked[0], stacked[1], stacked[2], stacked[3], stacked[4], stacked[5], stacked[6], stacked[7], stacked[8], stacked[9])
```

```python
import functools

import jax
import jax.numpy as jnp
from jax import lax
from jax.experimental import pallas as pl
from jax.experimental.pallas import tpu as pltpu
from jax.sharding import PartitionSpec as P

HEAD_DIM = 64
CLUSTER = 128
ITEMS = 6
EPSILON = 1e-06
MESH = pl.DeviceIdType.MESH
VMEM_LIMIT = 60 * 1024 * 1024
bf16 = jnp.bfloat16
f32 = jnp.float32


def nn(a, b):
    return lax.dot_general(a, b, (((1,), (0,)), ((), ())), preferred_element_type=f32)


def nt(a, b):
    return lax.dot_general(a, b, (((1,), (1,)), ((), ())), preferred_element_type=f32)


def tn(a, b):
    return lax.dot_general(a, b, (((0,), (0,)), ((), ())), preferred_element_type=f32)


def loop(count, body):
    def step(index, carry):
        body(index)
        return carry

    lax.fori_loop(0, count, step, 0)


def rows_at(index, size):
    return pl.ds(pl.multiple_of(index * size, size), size)


class Place:
    def __init__(self, n_z, n_t, rows):
        self.n_z, self.n_t, self.rows = n_z, n_t, rows
        self.z, self.t = lax.axis_index("dp"), lax.axis_index("tensor")
        self.piece = rows // n_z
        self.own = rows // n_t
        self.chunk = max(self.piece, 128)
        self.chunks = rows // self.chunk
        self.per_chunk = self.chunk // self.piece

    def greet(self):
        barrier = pltpu.get_barrier_semaphore()

        def greet_z(k):
            peer = lax.rem(self.z + 1 + k, self.n_z)
            pl.semaphore_signal(barrier, inc=1, device_id={"dp": peer}, device_id_type=MESH)

        def greet_t(k):
            peer = lax.rem(self.t + 1 + k, self.n_t)
            pl.semaphore_signal(barrier, inc=1, device_id={"tensor": peer}, device_id_type=MESH)

        loop(self.n_z - 1, greet_z)
        loop(self.n_t - 1, greet_t)
        pl.semaphore_wait(barrier, self.n_z + self.n_t - 2)

    def own_rows(self):
        return rows_at(self.t, self.own)

    def z_copy(self, m, k, src, dst, sems):
        peer = lax.rem(self.z + k, self.n_z)
        return pltpu.make_async_remote_copy(
            src_ref=src.at[m, rows_at(peer, self.piece)],
            dst_ref=dst.at[m, rows_at(self.z, self.piece)],
            send_sem=sems[0].at[m, k - 1],
            recv_sem=sems[1].at[m, k - 1],
            device_id={"dp": peer},
            device_id_type=MESH,
        )

    def z_chunk(self, kk):
        return lax.rem(self.z // self.per_chunk + 1 + kk, self.chunks)

    def z_send_chunk(self, m, cc, src, dst, sems):
        def one(j):
            peer = cc * self.per_chunk + j
            k = lax.rem(peer - self.z + self.n_z, self.n_z)

            @pl.when(k > 0)
            def _():
                self.z_copy(m, k, src, dst, sems).start()

        loop(self.per_chunk, one)

    def z_keep_own(self, m, src, dst):
        mine = rows_at(self.z, self.piece)
        dst[m, mine] = src[m, mine]

    def z_wait(self, m, src, dst, sems):
        loop(self.n_z - 1, lambda k: self.z_copy(m, k + 1, src, dst, sems).wait())

    def sum_copy(self, m, k, src, dst, sems):
        peer = lax.rem(self.t + k, self.n_t)
        return pltpu.make_async_remote_copy(
            src_ref=src.at[m, k - 1],
            dst_ref=dst.at[m, k - 1],
            send_sem=sems[0].at[m, k - 1],
            recv_sem=sems[1].at[m, k - 1],
            device_id={"tensor": peer},
            device_id_type=MESH,
        )

    def sum_put(self, m, k, part, src, dst, sems, mine):
        @pl.when(k > 0)
        def _():
            src[m, k - 1] = part.astype(bf16)
            self.sum_copy(m, k, src, dst, sems).start()

        @pl.when(k == 0)
        def _():
            mine[m] = part

    def sum_take(self, m, src, dst, sems, mine):
        total = mine[m]
        for k in range(1, self.n_t):
            self.sum_copy(m, k, src, dst, sems).wait()
        for k in range(1, self.n_t):
            total = total + dst[m, k - 1].astype(f32)
        return total

    def gather_copy(self, m, k, buf, sems):
        peer = lax.rem(self.t + k, self.n_t)
        return pltpu.make_async_remote_copy(
            src_ref=buf.at[m, self.own_rows()],
            dst_ref=buf.at[m, self.own_rows()],
            send_sem=sems[0].at[m, k - 1],
            recv_sem=sems[1].at[m, k - 1],
            device_id={"tensor": peer},
            device_id_type=MESH,
        )

    def gather_start(self, m, buf, sems):
        loop(self.n_t - 1, lambda k: self.gather_copy(m, k + 1, buf, sems).start())

    def gather_wait_from(self, m, k, buf, sems):
        @pl.when(k > 0)
        def _():
            self.gather_copy(m, self.n_t - k, buf, sems).wait_recv()

    def gather_wait_sent(self, m, buf, sems):
        loop(self.n_t - 1, lambda k: self.gather_copy(m, k + 1, buf, sems).wait_send())

    def gather_wait(self, m, buf, sems):
        loop(self.n_t - 1, lambda k: self.gather_copy(m, k + 1, buf, sems).wait())


def pick_rows(column, count):
    return (lax.broadcasted_iota(jnp.int32, (column.shape[0], count), 1) == column).astype(bf16)


def place_rows(row, first, count):
    numbers = lax.broadcasted_iota(jnp.int32, (count, row.shape[1]), 0) + first
    return (numbers == row).astype(bf16)


def by_head(block, heads):
    lane = lax.broadcasted_iota(jnp.int32, block.shape, 1) // HEAD_DIM
    return jnp.concatenate([jnp.where(lane == h, block, jnp.zeros_like(block)) for h in range(heads)])


def fold_heads(stacked, heads):
    count = stacked.shape[0] // heads
    lane = lax.broadcasted_iota(jnp.int32, (count, stacked.shape[1]), 1) // HEAD_DIM
    total = jnp.where(lane == 0, stacked[:count], 0.0)
    for h in range(1, heads):
        total = jnp.where(lane == h, stacked[h * count : (h + 1) * count], total)
    return total


def softmax_parts(scores, same):
    masked = jnp.where(same, scores, -1e30)
    centred = masked - jnp.max(masked, axis=-1, keepdims=True)
    grown = jnp.exp(centred)
    total = jnp.sum(grown, axis=-1, keepdims=True)
    return grown / total, centred, total


def normalise(values):
    centre = jnp.mean(values, axis=-1, keepdims=True)
    spread = values - centre
    second = jnp.mean(spread * spread, axis=-1, keepdims=True)
    inverse = lax.rsqrt(second + EPSILON)
    return spread * inverse, inverse


def norm_backward(grad, normed, inverse, gain):
    scaled = grad * gain
    first = jnp.mean(scaled, axis=-1, keepdims=True)
    second = jnp.mean(scaled * normed, axis=-1, keepdims=True)
    return inverse * (scaled - first - normed * second)


def forward_kernel(
    n_z, n_t, heads,
    x, send_col, send_row, recv_col, recv_row, label_col, label_row,
    wa, ba, wo, bo, norm1, wu, bu, wd, bd, norm2,
    xp, grouped, ms, n1, inv1, hfull, act, gprime, n2, inv2, ent, x_next,
    zsend, zrecv, mixc, msend, rs1_src, rs1_dst, mine1, hid, rs2_src, rs2_dst, mine2, out_sent,
    q_s, q_r, m_s, m_r, r1_s, r1_r, g1_s, g1_r, r2_s, r2_r, g2_s, g2_r,
):
    rows = x.shape[1]
    at = Place(n_z, n_t, rows)
    width = heads * HEAD_DIM
    scale = HEAD_DIM**-0.5
    q_sems, m_sems, r1_sems, g1_sems, r2_sems, g2_sems = (
        (q_s, q_r), (m_s, m_r), (r1_s, r1_r), (g1_s, g1_r), (r2_s, r2_r), (g2_s, g2_r),
    )
    at.greet()

    def project(m):
        def chunk(kk):
            cc = at.z_chunk(kk)
            here = rows_at(cc, at.chunk)
            moved = nn(pick_rows(send_col[m, here], rows), x[m]).astype(bf16)
            xp[m, here] = moved
            zsend[m, here] = (nn(moved, wa[...]) + ba[...]).astype(bf16)
            at.z_send_chunk(m, cc, zsend, zrecv, q_sems)

        loop(at.chunks, chunk)
        at.z_keep_own(m, zsend, zrecv)

    def attend(m):
        at.z_wait(m, zsend, zrecv, q_sems)
        ent[m] = jnp.zeros(ent.shape[1:], f32)

        def cluster(c):
            here = rows_at(c, CLUSTER)
            block = nn(pick_rows(recv_col[m, here], rows), zrecv[m]).astype(bf16)
            grouped[m, here] = block
            queries, keys, values = (block[:, i * width : (i + 1) * width] for i in range(3))
            scores = nt(queries, by_head(keys, heads)) * scale
            same = label_col[m, here] == label_row[m, :, here]
            probs = []
            lane = lax.broadcasted_iota(jnp.int32, (1, 128), 1)
            log_row = jnp.zeros((1, 128), f32)
            for h in range(heads):
                prob, centred, total = softmax_parts(
                    scores[:, h * CLUSTER : (h + 1) * CLUSTER], same
                )
                inner = jnp.sum(jnp.where(same, prob * centred, 0.0), axis=-1, keepdims=True)
                entropy = jnp.mean(jnp.log(total) - inner, axis=0, keepdims=True)
                log_row = jnp.where(lane == h, entropy, log_row)
                probs.append(prob.astype(bf16))
            ent[m, pl.ds(c, 1)] = log_row
            mixed = nn(jnp.concatenate(probs, axis=1), by_head(values, heads))
            mixc[m, here] = mixed.astype(bf16)

        loop(rows // CLUSTER, cluster)

        def home(kk):
            cc = at.z_chunk(kk)
            here = rows_at(cc, at.chunk)
            one_hot = place_rows(recv_row[m], cc * at.chunk, at.chunk)
            msend[m, here] = nn(one_hot, mixc[m]).astype(bf16)
            at.z_send_chunk(m, cc, msend, ms, m_sems)

        loop(at.chunks, home)
        at.z_keep_own(m, msend, ms)

    def out_project(m):
        at.z_wait(m, msend, ms, m_sems)

        def part(kk):
            k = lax.rem(kk + 1, n_t)
            here = rows_at(lax.rem(at.t + k, n_t), at.own)
            at.sum_put(m, k, nn(ms[m, here], wo[...]), rs1_src, rs1_dst, r1_sems, mine1)

        loop(n_t, part)

    def first_norm(m):
        total = at.sum_take(m, rs1_src, rs1_dst, r1_sems, mine1) + bo[...]
        here = at.own_rows()
        normed, inverse = normalise(xp[m, here].astype(f32) + total)
        hidden = normed * norm1[0:1] + norm1[1:2]
        n1[m] = normed
        inv1[m] = jnp.broadcast_to(inverse, inv1.shape[1:])
        hid[m] = hidden
        hfull[m, here] = hidden.astype(bf16)
        at.gather_start(m, hfull, g1_sems)

    def feed(m):
        def part(k):
            at.gather_wait_from(m, k, hfull, g1_sems)
            here = rows_at(lax.rem(at.t + k, n_t), at.own)
            up = nn(hfull[m, here], wu[...]) + bu[...]
            square = up * up
            tanh = jnp.tanh(0.7978845608028654 * up * (1.0 + 0.044715 * square))
            half = 0.5 * (1.0 + tanh)
            slope = 0.7978845608028654 * (1.0 + 3 * 0.044715 * square)
            gprime[m, here] = (half + 0.5 * up * (1.0 - tanh * tanh) * slope).astype(bf16)
            active = (up * half).astype(bf16)
            act[m, here] = active
            at.sum_put(m, k, nn(active, wd[...]), rs2_src, rs2_dst, r2_sems, mine2)

        loop(n_t, part)

    def second_norm(m):
        total = at.sum_take(m, rs2_src, rs2_dst, r2_sems, mine2) + bd[...]
        here = at.own_rows()
        normed, inverse = normalise(hid[m] + total)
        n2[m] = normed
        inv2[m] = jnp.broadcast_to(inverse, inv2.shape[1:])
        out_sent[m, here] = (normed * norm2[0:1] + norm2[1:2]).astype(bf16)
        at.gather_start(m, out_sent, g2_sems)

    def back_to_tokens(m):
        at.gather_wait(m, out_sent, g2_sems)

        def chunk(cc):
            one_hot = place_rows(send_row[m], cc * 128, 128)
            x_next[m, rows_at(cc, 128)] = nn(one_hot, out_sent[m]).astype(bf16)

        loop(rows // 128, chunk)
        at.gather_wait_sent(m, hfull, g1_sems)

    project(0)
    project(1)
    attend(0)
    out_project(0)
    attend(1)
    first_norm(0)
    feed(0)
    out_project(1)
    second_norm(0)
    first_norm(1)
    feed(1)
    back_to_tokens(0)
    second_norm(1)
    back_to_tokens(1)


def backward_kernel(
    n_z, n_t, heads,
    grad, send_col, send_row, recv_col, recv_row, label_col, label_row,
    wa, wo, norm1, wu, wd, norm2,
    xp, grouped, ms, n1, inv1, hfull, act, gprime, n2, inv2,
    grad_next, g_attn, g_up, g_down, g_out, g_vec,
    db, dup, dsec, rs1_src, rs1_dst, mine1, dres, da, dmsend, dmrecv, dgc, dqsend, dproj,
    rs2_src, rs2_dst, mine2, din,
    a1_s, a1_r, r1_s, r1_r, a2_s, a2_r, m_s, m_r, q_s, q_r, r2_s, r2_r, a3_s, a3_r,
):
    rows = grad.shape[1]
    at = Place(n_z, n_t, rows)
    width = heads * HEAD_DIM
    scale = HEAD_DIM**-0.5
    a1_sems, r1_sems, a2_sems, m_sems, q_sems, r2_sems, a3_sems = (
        (a1_s, a1_r), (r1_s, r1_r), (a2_s, a2_r), (m_s, m_r), (q_s, q_r), (r2_s, r2_r), (a3_s, a3_r),
    )
    at.greet()
    g_vec[...] = jnp.zeros(g_vec.shape, f32)

    def add_vec(index, value):
        g_vec[index : index + 1, : value.shape[1]] += value

    def column_sum(value):
        return jnp.sum(value.astype(f32), axis=0, keepdims=True)

    def add_to(ref, m, value):
        if m == 0:
            ref[...] = value
        else:
            ref[...] += value

    def second_norm(m):
        here = at.own_rows()
        up = nn(pick_rows(send_col[m, here], rows), grad[m])
        normed = n2[m]
        down = norm_backward(up, normed, inv2[m][:, :1], norm2[0:1])
        dsec[m] = down
        low = down.astype(bf16)
        db[m, here] = low
        at.gather_start(m, db, a1_sems)
        add_vec(0, column_sum(up * normed))
        add_vec(1, column_sum(up))
        add_vec(2, column_sum(low))

    def feed(m):
        def part(k):
            at.gather_wait_from(m, k, db, a1_sems)
            here = rows_at(lax.rem(at.t + k, n_t), at.own)
            low = (nt(db[m, here], wd[...]) * gprime[m, here].astype(f32)).astype(bf16)
            dup[m, here] = low
            at.sum_put(m, k, nt(low, wu[...]), rs1_src, rs1_dst, r1_sems, mine1)

        loop(n_t, part)

    def feed_weights(m):
        add_to(g_down, m, tn(db[m], act[m]))
        add_to(g_up, m, tn(hfull[m], dup[m]))
        add_vec(6, column_sum(dup[m]))

    def first_norm(m):
        total = at.sum_take(m, rs1_src, rs1_dst, r1_sems, mine1)
        here = at.own_rows()
        up = dsec[m] + total
        normed = n1[m]
        down = norm_backward(up, normed, inv1[m][:, :1], norm1[0:1])
        dres[m] = down
        low = down.astype(bf16)
        da[m, here] = low
        at.gather_start(m, da, a2_sems)
        add_vec(3, column_sum(up * normed))
        add_vec(4, column_sum(up))
        add_vec(5, column_sum(low))

    def out_back(m):
        at.gather_wait(m, da, a2_sems)

        def chunk(kk):
            cc = at.z_chunk(kk)
            here = rows_at(cc, at.chunk)
            dmsend[m, here] = nt(da[m, here], wo[...]).astype(bf16)
            at.z_send_chunk(m, cc, dmsend, dmrecv, m_sems)

        loop(at.chunks, chunk)
        at.z_keep_own(m, dmsend, dmrecv)

    def out_weights(m):
        add_to(g_out, m, tn(da[m], ms[m]))

    def attend(m):
        at.z_wait(m, dmsend, dmrecv, m_sems)

        def cluster(c):
            here = rows_at(c, CLUSTER)
            dmix = nn(pick_rows(recv_col[m, here], rows), dmrecv[m]).astype(bf16)
            block = grouped[m, here]
            queries, keys, values = (block[:, i * width : (i + 1) * width] for i in range(3))
            keys_by_head = by_head(keys, heads)
            scores = nt(queries, keys_by_head) * scale
            same = label_col[m, here] == label_row[m, :, here]
            dprob = nt(dmix, by_head(values, heads))
            probs, dscores = [], []
            for h in range(heads):
                cut = slice(h * CLUSTER, (h + 1) * CLUSTER)
                prob = softmax_parts(scores[:, cut], same)[0]
                outer = prob * dprob[:, cut]
                dscore = outer - prob * jnp.sum(outer, axis=-1, keepdims=True)
                probs.append(prob.astype(bf16))
                dscores.append(dscore.astype(bf16))
            prob_all = jnp.concatenate(probs, axis=1)
            dscore_all = jnp.concatenate(dscores, axis=1)
            dgc[m, here, 0:width] = (nn(dscore_all, keys_by_head) * scale).astype(bf16)
            dkeys = fold_heads(tn(dscore_all, queries), heads)
            dgc[m, here, width : 2 * width] = (dkeys * scale).astype(bf16)
            dgc[m, here, 2 * width : 3 * width] = fold_heads(tn(prob_all, dmix), heads).astype(bf16)

        loop(rows // CLUSTER, cluster)

        def home(kk):
            cc = at.z_chunk(kk)
            here = rows_at(cc, at.chunk)
            one_hot = place_rows(recv_row[m], cc * at.chunk, at.chunk)
            dqsend[m, here] = nn(one_hot, dgc[m]).astype(bf16)
            at.z_send_chunk(m, cc, dqsend, dproj, q_sems)

        loop(at.chunks, home)
        at.z_keep_own(m, dqsend, dproj)

    def in_project(m):
        at.z_wait(m, dqsend, dproj, q_sems)

        def part(kk):
            k = lax.rem(kk + 1, n_t)
            here = rows_at(lax.rem(at.t + k, n_t), at.own)
            at.sum_put(m, k, nt(dproj[m, here], wa[...]), rs2_src, rs2_dst, r2_sems, mine2)

        loop(n_t, part)

    def in_weights(m):
        add_to(g_attn, m, tn(xp[m], dproj[m]))
        add_vec(7, column_sum(dproj[m]))

    def layer_input(m):
        total = at.sum_take(m, rs2_src, rs2_dst, r2_sems, mine2)
        here = at.own_rows()
        din[m, here] = (dres[m] + total).astype(bf16)
        at.gather_start(m, din, a3_sems)

    def back_to_tokens(m):
        at.gather_wait(m, din, a3_sems)

        def chunk(cc):
            one_hot = place_rows(send_row[m], cc * 128, 128)
            grad_next[m, rows_at(cc, 128)] = nn(one_hot, din[m]).astype(bf16)

        loop(rows // 128, chunk)
        at.gather_wait_sent(m, db, a1_sems)

    second_norm(0)
    second_norm(1)
    feed(0)
    feed(1)
    first_norm(0)
    feed_weights(0)
    out_back(0)
    first_norm(1)
    feed_weights(1)
    attend(0)
    out_weights(0)
    out_back(1)
    in_project(0)
    attend(1)
    in_weights(0)
    layer_input(0)
    out_weights(1)
    in_project(1)
    back_to_tokens(0)
    in_weights(1)
    layer_input(1)
    back_to_tokens(1)


def dma_pair(count):
    return [pltpu.SemaphoreType.DMA((2, count)), pltpu.SemaphoreType.DMA((2, count))]


def call(kernel, outs, scratch, args, name, collective_id):
    vmem = pl.BlockSpec(memory_space=pltpu.VMEM)
    return pl.pallas_call(
        kernel,
        out_shape=[jax.ShapeDtypeStruct(shape, dtype) for shape, dtype in outs],
        in_specs=[vmem] * len(args),
        out_specs=[vmem] * len(outs),
        scratch_shapes=scratch,
        compiler_params=pltpu.CompilerParams(
            collective_id=collective_id, has_side_effects=True, vmem_limit_bytes=VMEM_LIMIT
        ),
        name=name,
    )(*args)


def shards(
    inputs, out_grad, items, send_order, recv_order,
    attn_weight, qv_bias, out_weight, out_bias, norm_first,
    up_weight, up_bias, down_weight, down_bias, norm_second,
):
    micros, rows, width = inputs.shape
    n_z, n_t, n_s = lax.axis_size("dp"), lax.axis_size("tensor"), lax.axis_size("section")
    cols = attn_weight.shape[3]
    heads = cols // HEAD_DIM
    hidden = up_weight.shape[2]
    half = micros // n_s
    clusters = rows // CLUSTER
    own = rows // n_t
    core = lax.axis_index("section")
    z, t = lax.axis_index("dp"), lax.axis_index("tensor")

    def both(value):
        return lax.all_gather(value[0], "section")

    def mine(value, axis):
        return lax.dynamic_slice_in_dim(value, core * half, half, axis)

    wa = both(attn_weight).reshape(2, width, 3 * cols)
    wo, wu, wd = both(out_weight), both(up_weight), both(down_weight)
    small = jnp.concatenate(
        [
            qv_bias[0].reshape(-1), out_bias[0], norm_first[0].reshape(-1), up_bias[0],
            down_bias[0], norm_second[0].reshape(-1),
        ]
    )
    smalls = lax.all_gather(small, "section")
    index = jnp.stack([items[0], send_order[0, :, 0], recv_order[0, :, 0]])
    index = mine(lax.all_gather(index, "section"), 2)

    def vectors(layer):
        row = smalls[layer]
        cuts = [2 * cols, width, 2 * width, hidden, width, 2 * width]
        parts, start = [], 0
        for cut in cuts:
            parts.append(row[start : start + cut])
            start += cut
        ba = jnp.concatenate([parts[0][:cols], jnp.zeros((cols,), f32), parts[0][cols:]])
        return (
            ba[None], parts[1][None], parts[2].reshape(2, width), parts[3][None], parts[4][None],
            parts[5].reshape(2, width),
        )

    def orders(layer):
        out = []
        for value in (index[layer, 1], index[layer, 2], index[layer, 0]):
            out += [value[:, :, None], value[:, None, :]]
        return out

    def forward(layer, x):
        ba, bo, norm1, bu, bd, norm2 = vectors(layer)
        pair = (half, rows)
        outs = [
            ((*pair, width), bf16), ((*pair, 3 * cols), bf16), ((*pair, cols), bf16),
            ((half, own, width), f32), ((half, own, 128), f32), ((*pair, width), bf16),
            ((*pair, hidden), bf16), ((*pair, hidden), bf16),
            ((half, own, width), f32), ((half, own, 128), f32),
            ((half, max(8, clusters), 128), f32), ((*pair, width), bf16),
        ]
        sums = (half, n_t - 1, own, width)
        scratch = [
            pltpu.VMEM((*pair, 3 * cols), bf16), pltpu.VMEM((*pair, 3 * cols), bf16),
            pltpu.VMEM((*pair, cols), bf16), pltpu.VMEM((*pair, cols), bf16),
            pltpu.VMEM(sums, bf16), pltpu.VMEM(sums, bf16), pltpu.VMEM((half, own, width), f32),
            pltpu.VMEM((half, own, width), f32),
            pltpu.VMEM(sums, bf16), pltpu.VMEM(sums, bf16), pltpu.VMEM((half, own, width), f32),
            pltpu.VMEM((*pair, width), bf16),
            *dma_pair(n_z - 1), *dma_pair(n_z - 1),
            *dma_pair(n_t - 1), *dma_pair(n_t - 1), *dma_pair(n_t - 1), *dma_pair(n_t - 1),
        ]
        args = [
            x, *orders(layer), wa[layer], ba, wo[layer], bo, norm1, wu[layer], bu, wd[layer], bd,
            norm2,
        ]
        kernel = functools.partial(forward_kernel, n_z, n_t, heads)
        return call(kernel, outs, scratch, args, "layer_forward", 0)

    def backward(layer, grad, kept):
        _, _, norm1, _, _, norm2 = vectors(layer)
        pair = (half, rows)
        outs = [
            ((*pair, width), bf16), ((width, 3 * cols), f32), ((width, hidden), f32),
            ((width, hidden), f32), ((width, cols), f32), ((8, max(width, hidden, 3 * cols)), f32),
        ]
        sums = (half, n_t - 1, own, width)
        scratch = [
            pltpu.VMEM((*pair, width), bf16), pltpu.VMEM((*pair, hidden), bf16),
            pltpu.VMEM((half, own, width), f32),
            pltpu.VMEM(sums, bf16), pltpu.VMEM(sums, bf16), pltpu.VMEM((half, own, width), f32),
            pltpu.VMEM((half, own, width), f32), pltpu.VMEM((*pair, width), bf16),
            pltpu.VMEM((*pair, cols), bf16), pltpu.VMEM((*pair, cols), bf16),
            pltpu.VMEM((*pair, 3 * cols), bf16), pltpu.VMEM((*pair, 3 * cols), bf16),
            pltpu.VMEM((*pair, 3 * cols), bf16),
            pltpu.VMEM(sums, bf16), pltpu.VMEM(sums, bf16), pltpu.VMEM((half, own, width), f32),
            pltpu.VMEM((*pair, width), bf16),
            *dma_pair(n_t - 1), *dma_pair(n_t - 1), *dma_pair(n_t - 1),
            *dma_pair(n_z - 1), *dma_pair(n_z - 1), *dma_pair(n_t - 1), *dma_pair(n_t - 1),
        ]
        args = [
            grad, *orders(layer), wa[layer], wo[layer], norm1, wu[layer], wd[layer], norm2, *kept,
        ]
        kernel = functools.partial(backward_kernel, n_z, n_t, heads)
        return call(kernel, outs, scratch, args, "layer_backward", 1)

    *kept0, ent0, x1 = forward(0, mine(inputs, 0))
    *kept1, ent1, x2 = forward(1, x1)
    grad1, *sums1 = backward(1, mine(out_grad, 0), kept1)
    grad0, *sums0 = backward(0, grad1, kept0)

    swap = [(0, 1), (1, 0)]

    def to_owner(first, second):
        kept = jnp.where(core == 0, first, second)
        came = lax.ppermute(jnp.where(core == 0, second, first), "section", swap)
        return jnp.where(
            core == 0, jnp.concatenate([kept, came]), jnp.concatenate([came, kept])
        )

    activations = to_owner(x1, x2)
    input_grads = to_owner(grad0, grad1).astype(f32)

    def reduced(first, second):
        both_layers = jnp.stack([first, second]).astype(bf16)
        both_layers = both_layers.reshape(n_s * n_z, first.shape[0] // n_z, first.shape[1])
        return lax.psum_scatter(
            both_layers, ("section", "dp"), scatter_dimension=0, tiled=False
        ).astype(f32)

    attn_grad = reduced(sums0[0], sums1[0]).reshape(-1, 3, cols)
    up_grad = reduced(sums0[1], sums1[1])
    down_grad = reduced(sums0[2], sums1[2]).T
    out_grad_w = reduced(sums0[3], sums1[3]).T

    vec = jnp.stack([sums0[4], sums1[4]])
    by_rows = vec[:, :6, :width].reshape(n_s, -1)
    by_cols = jnp.concatenate([vec[:, 6, :hidden], vec[:, 7, : 3 * cols]], axis=1)
    spot = (jnp.arange(n_t) == t).astype(f32)
    by_cols = (spot[None, :, None] * by_cols[:, None, :]).reshape(n_s, -1)
    entropy = jnp.stack([ent0, ent1])[:, :, :clusters, :heads]
    spot_core = (jnp.arange(n_s) == core).astype(f32)
    spot_z = (jnp.arange(n_z) == z).astype(f32)
    entropy = (
        entropy[:, None, :, None, :, None, :]
        * spot_core[None, :, None, None, None, None, None]
        * spot_z[None, None, None, :, None, None, None]
        * spot[None, None, None, None, None, :, None]
    ).reshape(n_s, -1)
    sizes = [by_rows.shape[1], by_cols.shape[1], entropy.shape[1]]
    totals = lax.psum(
        jnp.concatenate([by_rows, by_cols, entropy], axis=1), ("section", "dp", "tensor")
    )
    totals = lax.dynamic_slice_in_dim(totals, core, 1, 0)[0]
    rows_part = totals[: sizes[0]].reshape(6, width)
    cols_part = totals[sizes[0] : sizes[0] + sizes[1]].reshape(n_t, -1)
    cols_part = lax.dynamic_slice_in_dim(cols_part, t, 1, 0)[0]
    entropy = totals[sizes[0] + sizes[1] :].reshape(micros, n_z, clusters, n_t, heads)
    entropy = lax.dynamic_slice_in_dim(entropy, z, 1, 1)[:, 0]
    entropy = lax.dynamic_slice_in_dim(entropy, t, 1, 2)[:, :, 0]
    qkv_sums = cols_part[hidden:].reshape(3, cols)

    item_numbers = jnp.arange(ITEMS, dtype=jnp.int32)
    grid = items[0].reshape(micros, clusters, CLUSTER)
    occupancy = jnp.sum((grid[..., None] == item_numbers).astype(f32), axis=2)
    results = (
        activations, input_grads, entropy, occupancy, attn_grad,
        jnp.stack([qkv_sums[0], qkv_sums[2]]), out_grad_w, rows_part[5], rows_part[3:5], up_grad,
        cols_part[:hidden], down_grad, rows_part[2], rows_part[0:2],
    )
    return tuple(value[None] for value in results)


def solution(mesh):
    return jax.shard_map(
        shards,
        mesh=mesh,
        in_specs=(
            P(None, "dp", None),
            P(None, "dp", None),
            P("section", None, "dp"),
            P("section", None, "dp", None),
            P("section", None, "dp", None),
            P("section", None, None, "tensor"),
            P("section", None, "tensor"),
            P("section", "tensor", None),
            P("section", None),
            P("section", None, None),
            P("section", None, "tensor"),
            P("section", "tensor"),
            P("section", "tensor", None),
            P("section", None),
            P("section", None, None),
        ),
        out_specs=(
            P("section", None, "dp", None),
            P("section", None, "dp", None),
            P("section", None, "dp", "tensor"),
            P("section", None, "dp", None),
            P("section", "dp", None, "tensor"),
            P("section", None, "tensor"),
            P("section", "tensor", "dp"),
            P("section", None),
            P("section", None, None),
            P("section", "dp", "tensor"),
            P("section", "tensor"),
            P("section", "tensor", "dp"),
            P("section", None),
            P("section", None, None),
        ),
        check_vma=False,
    )
```

```python
import functools

import jax
import jax.numpy as jnp
from jax import lax
from jax.experimental import pallas as pl
from jax.experimental.pallas import tpu as pltpu
from jax.sharding import PartitionSpec as P

HEAD_DIM = 64
CLUSTER = 128
ITEMS = 6
EPSILON = 1e-06
MESH = pl.DeviceIdType.MESH
VMEM_LIMIT = 60 * 1024 * 1024
bf16 = jnp.bfloat16
f32 = jnp.float32


def nn(a, b):
    return lax.dot_general(a, b, (((1,), (0,)), ((), ())), preferred_element_type=f32)


def nt(a, b):
    return lax.dot_general(a, b, (((1,), (1,)), ((), ())), preferred_element_type=f32)


def tn(a, b):
    return lax.dot_general(a, b, (((0,), (0,)), ((), ())), preferred_element_type=f32)


def loop(count, body):
    def step(index, carry):
        body(index)
        return carry

    lax.fori_loop(0, count, step, 0)


def rows_at(index, size):
    return pl.ds(pl.multiple_of(index * size, size), size)


class Bag:
    def __init__(self, names, values):
        self.__dict__.update(zip(names, values, strict=True))


def place_rows(row, first, count):
    numbers = lax.broadcasted_iota(jnp.int32, (count, row.shape[1]), 0) + first
    return (numbers == row).astype(bf16)


def by_head(block, heads):
    lane = lax.broadcasted_iota(jnp.int32, block.shape, 1) // HEAD_DIM
    return jnp.concatenate([jnp.where(lane == h, block, jnp.zeros_like(block)) for h in range(heads)])


def fold_heads(stacked, heads):
    count = stacked.shape[0] // heads
    lane = lax.broadcasted_iota(jnp.int32, (count, stacked.shape[1]), 1) // HEAD_DIM
    total = jnp.where(lane == 0, stacked[:count], 0.0)
    for h in range(1, heads):
        total = jnp.where(lane == h, stacked[h * count : (h + 1) * count], total)
    return total


def softmax_parts(scores, same):
    masked = jnp.where(same, scores, -1e30)
    centred = masked - jnp.max(masked, axis=-1, keepdims=True)
    grown = jnp.exp(centred)
    total = jnp.sum(grown, axis=-1, keepdims=True)
    return grown / total, centred, total


def same_item(row):
    wide = jnp.broadcast_to(row.astype(f32), (row.shape[1], row.shape[1]))
    return wide == wide.T


def normalise(values):
    centre = jnp.mean(values, axis=-1, keepdims=True)
    spread = values - centre
    second = jnp.mean(spread * spread, axis=-1, keepdims=True)
    inverse = lax.rsqrt(second + EPSILON)
    return spread * inverse, inverse


def norm_backward(grad, normed, inverse, gain):
    scaled = grad * gain
    first = jnp.mean(scaled, axis=-1, keepdims=True)
    second = jnp.mean(scaled * normed, axis=-1, keepdims=True)
    return inverse * (scaled - first - normed * second)


def column_sum(value):
    return jnp.sum(value.astype(f32), axis=0, keepdims=True)


def remote(src, dst, sems, device):
    return pltpu.make_async_remote_copy(
        src_ref=src, dst_ref=dst, send_sem=sems[0], recv_sem=sems[1],
        device_id=device, device_id_type=MESH,
    )


def layers_kernel(n_z, n_t, rows, width, cols, names, *refs):
    r = Bag(names, refs)
    heads, half_width = cols // HEAD_DIM, width // 2
    scale = HEAD_DIM**-0.5
    core, z, t = lax.axis_index("section"), lax.axis_index("dp"), lax.axis_index("tensor")
    other = {"section": 1 - core}
    step_x, step_y = 1 - 2 * lax.rem(t, 2), 2 - 4 * (t // 2)
    t_x, t_y = t + step_x, t + step_y
    t_far = t + step_x + step_y
    piece, own = rows // n_z, rows // n_t
    chunk_rows = max(piece, 128)
    chunks, per_chunk = rows // chunk_rows, chunk_rows // piece
    mine = rows_at(t, own)
    weights = ("wa", "wo", "wu", "wd")

    def load(i):
        if i < 2:
            return pltpu.make_async_copy(r.x_in.at[core * 2 + i], r.x.at[i], r.load_sem.at[i])
        if i < 4:
            return pltpu.make_async_copy(r.g_in.at[core * 2 + i - 2], r.g.at[i - 2], r.load_sem.at[i])
        name = weights[i - 4]
        return pltpu.make_async_copy(
            getattr(r, name + "_in"), getattr(r, name).at[core], r.load_sem.at[i]
        )

    def swap(i):
        sems = (r.swap_s.at[i], r.swap_r.at[i])
        if i == 4:
            return remote(r.idx_in, r.idx.at[core], sems, other)
        if i == 5:
            return remote(r.par_in, r.par.at[core], sems, other)
        name = weights[i]
        return remote(getattr(r, name + "_in"), getattr(r, name).at[core], sems, other)

    def start():
        for i in (0, 4, 1, 5, 6, 7, 2, 3):
            load(i).start()
        r.idx[core] = r.idx_in[...]
        r.par[core] = r.par_in[...]
        r.vec[...] = jnp.zeros(r.vec.shape, f32)
        barrier = pltpu.get_barrier_semaphore()
        pl.semaphore_signal(barrier, inc=1, device_id=other, device_id_type=MESH)

        def greet_z(k):
            peer = lax.rem(z + 1 + k, n_z)
            pl.semaphore_signal(barrier, inc=1, device_id={"dp": peer}, device_id_type=MESH)

        def greet_t(k):
            peer = lax.rem(t + 1 + k, n_t)
            pl.semaphore_signal(barrier, inc=1, device_id={"tensor": peer}, device_id_type=MESH)

        loop(n_z - 1, greet_z)
        loop(n_t - 1, greet_t)
        pl.semaphore_wait(barrier, n_z + n_t - 1)
        for i in (4, 5, 0, 1, 2, 3):
            swap(i).start()
        swap(4).wait()
        swap(5).wait()

    def need_weight(layer, i):
        @pl.when(core == layer)
        def _():
            load(4 + i).wait()

        @pl.when(core != layer)
        def _():
            swap(i).wait_recv()

    def index_cut(kind, layer, m, first, count):
        cuts = [
            r.idx[layer, kind * 4 + core * 2 + m, first // 128 + i] for i in range(count // 128)
        ]
        return cuts[0] if len(cuts) == 1 else jnp.concatenate(cuts, axis=1)

    def index_row(kind, layer, m):
        return index_cut(kind, layer, m, 0, rows)

    def par(layer, i, count=None):
        return r.par[layer, i : i + 1, : count or width]

    def z_copy(kind, m, k, src, dst):
        peer = lax.rem(z + k, n_z)
        return remote(
            src.at[rows_at(peer, piece)], dst.at[rows_at(z, piece)],
            (r.z_s.at[kind, m, k - 1], r.z_r.at[kind, m, k - 1]), {"dp": peer},
        )

    def z_chunk(kk):
        return lax.rem(z // per_chunk + 1 + kk, chunks)

    def z_send(kind, m, cc, src, dst):
        def one(j):
            peer = cc * per_chunk + j
            k = lax.rem(peer - z + n_z, n_z)

            @pl.when(k > 0)
            def _():
                z_copy(kind, m, k, src, dst).start()

        loop(per_chunk, one)

    def z_wait(kind, m, src, dst):
        loop(n_z - 1, lambda k: z_copy(kind, m, k + 1, src, dst).wait())

    def keep_piece(src, dst, m):
        here = rows_at(z, piece)
        dst[m, here] = src[m, here]

    left, right = slice(0, half_width), slice(half_width, width)

    def sum_copy(m, j):
        peer = t_x if j in (0, 1, 5) else t_y
        return remote(
            r.sum_src.at[m, j], r.sum_dst.at[m, j], (r.sum_s.at[m, j], r.sum_r.at[m, j]),
            {"tensor": peer},
        )

    def sum_put(m, role, part):
        @pl.when(role == 0)
        def _():
            r.sum_own[m] = part

        @pl.when(role == 1)
        def _():
            r.sum_src[m, 1] = part[:, left].astype(bf16)
            r.sum_keep[m, 1] = part[:, right]
            sum_copy(m, 1).start()

        @pl.when(role == 2)
        def _():
            r.sum_src[m, 3] = part[:, right].astype(bf16)
            r.sum_keep[m, 0] = part[:, left]
            sum_copy(m, 3).start()

        @pl.when(role == 3)
        def _():
            r.sum_src[m, 0] = part[:, left].astype(bf16)
            sum_copy(m, 0).start()
            r.sum_src[m, 2] = part[:, right].astype(bf16)
            sum_copy(m, 2).start()

    def sum_mid(m):
        sum_copy(m, 0).wait_recv()
        r.sum_src[m, 4] = (r.sum_keep[m, 0] + r.sum_dst[m, 0].astype(f32)).astype(bf16)
        sum_copy(m, 4).start()
        sum_copy(m, 2).wait_recv()
        r.sum_src[m, 5] = (r.sum_keep[m, 1] + r.sum_dst[m, 2].astype(f32)).astype(bf16)
        sum_copy(m, 5).start()

    def sum_take(m):
        for j in (1, 3, 4, 5):
            sum_copy(m, j).wait_recv()
        for j in range(6):
            sum_copy(m, j).wait_send()
        added = jnp.concatenate(
            [
                r.sum_dst[m, 1].astype(f32) + r.sum_dst[m, 4].astype(f32),
                r.sum_dst[m, 3].astype(f32) + r.sum_dst[m, 5].astype(f32),
            ],
            axis=1,
        )
        return r.sum_own[m] + added

    def role_rows(role):
        return rows_at(t + lax.rem(role, 2) * step_x + (role // 2) * step_y, own)

    def gather_copy(kind, m, j, buf):
        if j < 2:
            here = mine
        elif j == 2:
            here = pl.ds(pl.multiple_of(t_x * own, own), own // 2)
        else:
            here = pl.ds(pl.multiple_of(t_y * own + own // 2, own // 2), own // 2)
        return remote(
            buf.at[here], buf.at[here], (r.gather_s.at[kind, m, j], r.gather_r.at[kind, m, j]),
            {"tensor": t_x if j in (0, 3) else t_y},
        )

    def gather_start(kind, m, buf):
        gather_copy(kind, m, 0, buf).start()
        gather_copy(kind, m, 1, buf).start()

    def gather_on(kind, m, buf):
        gather_copy(kind, m, 0, buf).wait_recv()
        gather_copy(kind, m, 2, buf).start()
        gather_copy(kind, m, 1, buf).wait_recv()
        gather_copy(kind, m, 3, buf).start()

    def gather_far(kind, m, buf):
        gather_copy(kind, m, 2, buf).wait_recv()
        gather_copy(kind, m, 3, buf).wait_recv()

    def gather_sent(kind, m, buf):
        for j in range(4):
            gather_copy(kind, m, j, buf).wait_send()

    def gather_step(kind, m, role, buf):
        @pl.when(role == 1)
        def _():
            gather_on(kind, m, buf)

        @pl.when(role == 3)
        def _():
            gather_far(kind, m, buf)

    def out_local(kind, m, src, out):
        return pltpu.make_async_copy(src, out.at[core * 2 + m], r.out_l.at[kind, m])

    def out_away(kind, m, src, out):
        return remote(src, out.at[core * 2 + m], (r.out_s.at[kind, m], r.out_r.at[kind, m]), other)

    def out_start(kind, layer, m, src, out):
        @pl.when(core == layer)
        def _():
            out_local(kind, m, src, out).start()

        @pl.when(core != layer)
        def _():
            out_away(kind, m, src, out).start()

    def out_wait(kind, layer, m, src, out):
        @pl.when(core == layer)
        def _():
            out_local(kind, m, src, out).wait()

        @pl.when(core != layer)
        def _():
            out_away(kind, m, src, out).wait_send()

    def project(l, m):
        if m == 0:
            need_weight(l, 0)
        if l == 0:
            load(m).wait()

        def chunk(kk):
            cc = z_chunk(kk)
            here = rows_at(cc, chunk_rows)
            numbers = lax.broadcasted_iota(jnp.int32, (rows, chunk_rows), 0)
            pick = (numbers == index_cut(1, l, m, cc * chunk_rows, chunk_rows)).astype(bf16)
            moved = tn(pick, r.x[m]).astype(bf16)
            r.xp[l, m, here] = moved
            r.zs[m, here] = (nn(moved, r.wa[l]) + par(l, 0, 3 * cols)).astype(bf16)
            z_send(0, m, cc, r.zs.at[m], r.zr.at[m])

        loop(chunks, chunk)
        keep_piece(r.zs, r.zr, m)

    def attend(l, m):
        z_wait(0, m, r.zs.at[m], r.zr.at[m])
        lane = lax.broadcasted_iota(jnp.int32, (1, 128), 1)

        def cluster(c):
            here = rows_at(c, CLUSTER)
            numbers = lax.broadcasted_iota(jnp.int32, (rows, CLUSTER), 0)
            pick = (numbers == index_cut(2, l, m, c * CLUSTER, CLUSTER)).astype(bf16)
            block = tn(pick, r.zr[m]).astype(bf16)
            r.grouped[l, m, here] = block
            queries, keys, values = (block[:, i * cols : (i + 1) * cols] for i in range(3))
            scores = nt(queries, by_head(keys, heads)) * scale
            same = same_item(index_cut(0, l, m, c * CLUSTER, CLUSTER))
            probs = []
            log_row = jnp.zeros((1, 128), f32)
            for h in range(heads):
                cut = slice(h * CLUSTER, (h + 1) * CLUSTER)
                prob, centred, total = softmax_parts(scores[:, cut], same)
                inner = jnp.sum(jnp.where(same, prob * centred, 0.0), axis=-1, keepdims=True)
                entropy = jnp.mean(jnp.log(total) - inner, axis=0, keepdims=True)
                log_row = jnp.where(lane == h, entropy, log_row)
                probs.append(prob.astype(bf16))
            r.entropy[l, m, pl.ds(c, 1)] = log_row
            mixed = nn(jnp.concatenate(probs, axis=1), by_head(values, heads))
            r.mixc[m, here] = mixed.astype(bf16)

        loop(rows // CLUSTER, cluster)

        def home(kk):
            cc = z_chunk(kk)
            here = rows_at(cc, chunk_rows)
            one_hot = place_rows(index_row(2, l, m), cc * chunk_rows, chunk_rows)
            r.ms_src[m, here] = nn(one_hot, r.mixc[m]).astype(bf16)
            z_send(1, m, cc, r.ms_src.at[m], r.ms.at[l, m])

        loop(chunks, home)
        here = rows_at(z, piece)
        r.ms[l, m, here] = r.ms_src[m, here]

    def out_project(l, m):
        if m == 0:
            need_weight(l, 1)
        z_wait(1, m, r.ms_src.at[m], r.ms.at[l, m])

        def part(kk):
            role = 3 - kk
            sum_put(m, role, nn(r.ms[l, m, role_rows(role)], r.wo[l]))

        loop(n_t, part)

    def middle(l, m):
        sum_mid(m)

    def first_norm(l, m):
        total = sum_take(m) + par(l, 1)
        normed, inverse = normalise(r.xp[l, m, mine].astype(f32) + total)
        hidden = normed * par(l, 2) + par(l, 3)
        r.n1[l, m] = normed
        r.inv1[l, m] = jnp.broadcast_to(inverse, (own, 128))
        r.hid[m] = hidden
        r.hfull[l, m, mine] = hidden.astype(bf16)
        gather_start(0, m, r.hfull.at[l, m])

    def feed(l, m):
        if m == 0:
            need_weight(l, 2)
            need_weight(l, 3)

        def part(role):
            gather_step(0, m, role, r.hfull.at[l, m])
            here = role_rows(role)
            up = nn(r.hfull[l, m, here], r.wu[l]) + par(l, 4)
            square = up * up
            tanh = jnp.tanh(0.7978845608028654 * up * (1.0 + 0.044715 * square))
            half = 0.5 * (1.0 + tanh)
            slope = 0.7978845608028654 * (1.0 + 3 * 0.044715 * square)
            r.gp[l, m, here] = (half + 0.5 * up * (1.0 - tanh * tanh) * slope).astype(bf16)
            active = (up * half).astype(bf16)
            r.act[l, m, here] = active
            sum_put(m, role, nn(active, r.wd[l]))

        loop(n_t, part)

    def second_norm(l, m):
        gather_sent(0, m, r.hfull.at[l, m])
        total = sum_take(m) + par(l, 5)
        normed, inverse = normalise(r.hid[m] + total)
        r.n2[l, m] = normed
        r.inv2[l, m] = jnp.broadcast_to(inverse, (own, 128))
        r.ag[m, mine] = (normed * par(l, 6) + par(l, 7)).astype(bf16)
        gather_start(1, m, r.ag.at[m])

    def out_on(l, m):
        gather_on(1, m, r.ag.at[m])

    def to_tokens(l, m, dst, buf):
        def chunk(cc):
            one_hot = place_rows(index_row(1, l, m), cc * 128, 128)
            dst[m, rows_at(cc, 128)] = nn(one_hot, buf[m]).astype(bf16)

        loop(rows // 128, chunk)

    def out_tokens(l, m):
        gather_far(1, m, r.ag.at[m])
        gather_sent(1, m, r.ag.at[m])
        if l == 1:
            out_wait(0, 0, m, r.x.at[m], r.acts)
        to_tokens(l, m, r.x, r.ag)
        out_start(0, l, m, r.x.at[m], r.acts)

    def add_vec(l, index, value):
        r.vec[l, index : index + 1, : value.shape[1]] += value

    def b_second_norm(l, m):
        if l == 1:
            load(2 + m).wait()
        numbers = lax.broadcasted_iota(jnp.int32, (rows, own), 0)
        pick = (numbers == index_cut(1, l, m, t * own, own)).astype(bf16)
        up = tn(pick, r.g[m])
        normed = r.n2[l, m]
        down = norm_backward(up, normed, r.inv2[l, m][:, :1], par(l, 6))
        r.hid[m] = down
        low = down.astype(bf16)
        r.db[m, mine] = low
        gather_start(2, m, r.db.at[m])
        add_vec(l, 0, column_sum(up * normed))
        add_vec(l, 1, column_sum(up))
        add_vec(l, 2, column_sum(low))

    def b_feed(l, m):
        def part(role):
            gather_step(2, m, role, r.db.at[m])
            here = role_rows(role)
            low = (nt(r.db[m, here], r.wd[l]) * r.gp[l, m, here].astype(f32)).astype(bf16)
            r.gp[l, m, here] = low
            sum_put(m, role, nt(low, r.wu[l]))

        loop(n_t, part)

    def grad_slabs(ref, value, lanes):
        ref[:, :, lanes] = value.reshape(n_z, width // n_z, value.shape[1]).astype(bf16)

    def feed_weights(l, m):
        for i in range(2):
            gather_sent(2, i, r.db.at[i])
            add_vec(l, 6, column_sum(r.gp[l, i]))
        up = tn(r.hfull[l, 0], r.gp[l, 0]) + tn(r.hfull[l, 1], r.gp[l, 1])
        grad_slabs(r.gs_feed, up, slice(0, width))
        down = tn(r.db[0], r.act[l, 0]) + tn(r.db[1], r.act[l, 1])
        grad_slabs(r.gs_feed, down, slice(width, 2 * width))
        grads_send(0, l, r.gs_feed, r.gr_feed)

    def b_first_norm(l, m):
        up = r.hid[m] + sum_take(m)
        normed = r.n1[l, m]
        down = norm_backward(up, normed, r.inv1[l, m][:, :1], par(l, 2))
        r.dres[m] = down
        low = down.astype(bf16)
        r.da[m, mine] = low
        gather_start(3, m, r.da.at[m])
        add_vec(l, 3, column_sum(up * normed))
        add_vec(l, 4, column_sum(up))
        add_vec(l, 5, column_sum(low))

    def b_on(l, m):
        gather_on(3, m, r.da.at[m])

    def out_back(l, m):
        gather_far(3, m, r.da.at[m])
        gather_sent(3, m, r.da.at[m])

        def chunk(kk):
            cc = z_chunk(kk)
            here = rows_at(cc, chunk_rows)
            r.ms_src[m, here] = nt(r.da[m, here], r.wo[l]).astype(bf16)
            z_send(2, m, cc, r.ms_src.at[m], r.dmr.at[m])

        loop(chunks, chunk)
        keep_piece(r.ms_src, r.dmr, m)

    def out_weights(l, m):
        value = tn(r.da[0], r.ms[l, 0]) + tn(r.da[1], r.ms[l, 1])
        grad_slabs(r.gs_attn, value, slice(3 * cols, 4 * cols))

    def b_attend(l, m):
        z_wait(2, m, r.ms_src.at[m], r.dmr.at[m])

        def cluster(c):
            here = rows_at(c, CLUSTER)
            numbers = lax.broadcasted_iota(jnp.int32, (rows, CLUSTER), 0)
            pick = (numbers == index_cut(2, l, m, c * CLUSTER, CLUSTER)).astype(bf16)
            dmix = tn(pick, r.dmr[m]).astype(bf16)
            block = r.grouped[l, m, here]
            queries, keys, values = (block[:, i * cols : (i + 1) * cols] for i in range(3))
            keys_by_head = by_head(keys, heads)
            scores = nt(queries, keys_by_head) * scale
            same = same_item(index_cut(0, l, m, c * CLUSTER, CLUSTER))
            dprob = nt(dmix, by_head(values, heads))
            probs, dscores = [], []
            for h in range(heads):
                cut = slice(h * CLUSTER, (h + 1) * CLUSTER)
                prob = softmax_parts(scores[:, cut], same)[0]
                outer = prob * dprob[:, cut]
                dscore = outer - prob * jnp.sum(outer, axis=-1, keepdims=True)
                probs.append(prob.astype(bf16))
                dscores.append(dscore.astype(bf16))
            prob_all = jnp.concatenate(probs, axis=1)
            dscore_all = jnp.concatenate(dscores, axis=1)
            dqueries = nn(dscore_all, keys_by_head) * scale
            dkeys = fold_heads(tn(dscore_all, queries), heads) * scale
            dvalues = fold_heads(tn(prob_all, dmix), heads)
            r.grouped[l, m, here] = jnp.concatenate([dqueries, dkeys, dvalues], axis=1).astype(bf16)

        loop(rows // CLUSTER, cluster)

        def home(kk):
            cc = z_chunk(kk)
            here = rows_at(cc, chunk_rows)
            one_hot = place_rows(index_row(2, l, m), cc * chunk_rows, chunk_rows)
            r.zs[m, here] = nn(one_hot, r.grouped[l, m]).astype(bf16)
            z_send(3, m, cc, r.zs.at[m], r.zr.at[m])

        loop(chunks, home)
        keep_piece(r.zs, r.zr, m)

    def in_project(l, m):
        z_wait(3, m, r.zs.at[m], r.zr.at[m])

        def part(kk):
            role = 3 - kk
            sum_put(m, role, nt(r.zr[m, role_rows(role)], r.wa[l]))

        loop(n_t, part)

    def in_weights(l, m):
        for i in range(2):
            add_vec(l, 7, column_sum(r.zr[i]))
        value = tn(r.xp[l, 0], r.zr[0]) + tn(r.xp[l, 1], r.zr[1])
        grad_slabs(r.gs_attn, value, slice(0, 3 * cols))
        grads_send(1, l, r.gs_attn, r.gr_attn)

    def layer_input(l, m):
        r.ag[m, mine] = (r.dres[m] + sum_take(m)).astype(bf16)
        gather_start(4, m, r.ag.at[m])

    def b_out_on(l, m):
        gather_on(4, m, r.ag.at[m])

    def b_tokens(l, m):
        gather_far(4, m, r.ag.at[m])
        gather_sent(4, m, r.ag.at[m])
        if l == 0:
            out_wait(1, 1, m, r.g.at[m], r.grads)
        to_tokens(l, m, r.g, r.ag)
        out_start(1, l, m, r.g.at[m], r.grads)

    def grad_core_copy(kind, k, src, dst):
        return remote(src.at[k], dst.at[k], (r.gc_s.at[kind, k], r.gc_r.at[kind, k]), other)

    def grad_z_copy(kind, k, src, dst):
        peer = lax.rem(z + k, n_z)
        return remote(
            src.at[peer], dst.at[k - 1], (r.gz_s.at[kind, k - 1], r.gz_r.at[kind, k - 1]),
            {"dp": peer},
        )

    def grads_send(kind, l, src, dst):
        @pl.when(core != l)
        def _():
            loop(n_z, lambda k: grad_core_copy(kind, lax.rem(z + 1 + k, n_z), src, dst).start())

    def grads_mid(kind, l, src, came, dst):
        @pl.when(core == l)
        def _():
            def one(kk):
                k = lax.rem(kk + 1, n_z)
                peer = lax.rem(z + k, n_z)
                grad_core_copy(kind, peer, src, came).wait_recv()
                src[peer] = (src[peer].astype(f32) + came[peer].astype(f32)).astype(bf16)

                @pl.when(k > 0)
                def _():
                    grad_z_copy(kind, k, src, dst).start()

            loop(n_z, one)

    def grads_end(kind, l, src, came, dst, out):
        @pl.when(core == l)
        def _():
            out[...] = src[z].astype(f32)

            def one(k):
                grad_z_copy(kind, k + 1, src, dst).wait()
                out[...] += dst[k].astype(f32)

            loop(n_z - 1, one)

        @pl.when(core != l)
        def _():
            loop(n_z, lambda k: grad_core_copy(kind, k, src, came).wait_send())

    def feed_mid(l, m):
        grads_mid(0, l, r.gs_feed, r.gr_feed, r.gz_feed)

    def feed_end(l, m):
        grads_end(0, l, r.gs_feed, r.gr_feed, r.gz_feed, r.g_feed)

    def attn_mid(l, m):
        grads_mid(1, l, r.gs_attn, r.gr_attn, r.gz_attn)

    def attn_end(l, m):
        grads_end(1, l, r.gs_attn, r.gr_attn, r.gz_attn, r.g_attn)

    def vec_copy(l):
        return remote(r.vec.at[l], r.vec_came, (r.vc_s.at[0], r.vc_r.at[0]), other)

    def vec_t_copy(k):
        return remote(
            r.vec_t.at[t], r.vec_t.at[t], (r.vt_s.at[k - 1], r.vt_r.at[k - 1]),
            {"tensor": lax.rem(t + k, n_t)},
        )

    def vec_z_copy(k):
        return remote(
            r.vec_z.at[z], r.vec_z.at[z], (r.vz_s.at[k - 1], r.vz_r.at[k - 1]),
            {"dp": lax.rem(z + k, n_z)},
        )

    def entropy_copy(l, m):
        return remote(
            r.entropy.at[l, m], r.ent.at[core * 2 + m], (r.en_s.at[m], r.en_r.at[m]), other
        )

    def vec_start(l, m):
        @pl.when(core != l)
        def _():
            vec_copy(l).start()
            for i in range(2):
                entropy_copy(l, i).start()

    def vec_sum_t(l, m):
        @pl.when(core == l)
        def _():
            for i in range(2):
                r.ent[core * 2 + i] = r.entropy[l, i]
            vec_copy(l).wait_recv()
            r.vec_t[t] = r.vec[l] + r.vec_came[...]
            for k in range(1, n_t):
                vec_t_copy(k).start()

    def vec_sum_z(l, m):
        @pl.when(core == l)
        def _():
            for k in range(1, n_t):
                vec_t_copy(k).wait()
            total = r.vec_t[0]
            for k in range(1, n_t):
                total = total + r.vec_t[k]
            lane_rows = lax.broadcasted_iota(jnp.int32, total.shape, 0)
            r.vec_z[z] = jnp.where(lane_rows < 6, total, r.vec_t[t])
            loop(n_z - 1, lambda k: vec_z_copy(k + 1).start())

    def vec_end(l, m):
        @pl.when(core == l)
        def _():
            loop(n_z - 1, lambda k: vec_z_copy(k + 1).wait())
            r.vec_out[...] = r.vec_z[0]

            def one(k):
                r.vec_out[...] += r.vec_z[k + 1]

            loop(n_z - 1, one)

        @pl.when(core != l)
        def _():
            vec_copy(l).wait_send()
            for i in range(2):
                entropy_copy(l, i).wait_send()

    def finish():
        for m in range(2):
            out_wait(0, 1, m, r.x.at[m], r.acts)
            out_wait(1, 0, m, r.g.at[m], r.grads)
            for kind, out, src in ((0, r.acts, r.x), (1, r.grads, r.g)):
                out_away(kind, m, src.at[m], out).wait_recv()
            entropy_copy(0, m).wait_recv()
        for i in range(4):
            swap(i).wait_send()

    schedule = (
        (project, 0, 0), (attend, 0, 0), (project, 0, 1), (out_project, 0, 0), (middle, 0, 0),
        (first_norm, 0, 0), (attend, 0, 1), (feed, 0, 0), (middle, 0, 0), (out_project, 0, 1),
        (second_norm, 0, 0), (middle, 0, 1), (out_on, 0, 0), (first_norm, 0, 1), (out_tokens, 0, 0),
        (project, 1, 0), (feed, 0, 1), (middle, 0, 1), (attend, 1, 0), (second_norm, 0, 1), (out_on, 0, 1),
        (out_project, 1, 0), (out_tokens, 0, 1), (project, 1, 1), (middle, 1, 0), (first_norm, 1, 0),
        (attend, 1, 1), (feed, 1, 0), (middle, 1, 0), (out_project, 1, 1), (second_norm, 1, 0),
        (middle, 1, 1), (b_second_norm, 1, 0), (out_on, 1, 0), (first_norm, 1, 1), (out_tokens, 1, 0),
        (b_feed, 1, 0), (feed, 1, 1), (middle, 1, 0), (middle, 1, 1), (b_first_norm, 1, 0),
        (second_norm, 1, 1), (b_on, 1, 0), (b_second_norm, 1, 1), (out_on, 1, 1), (out_back, 1, 0),
        (out_tokens, 1, 1), (b_feed, 1, 1), (middle, 1, 1), (b_attend, 1, 0), (b_first_norm, 1, 1),
        (feed_weights, 1, 1), (b_on, 1, 1), (in_project, 1, 0), (feed_mid, 1, 0), (out_back, 1, 1),
        (middle, 1, 0), (layer_input, 1, 0), (out_weights, 1, 1), (b_out_on, 1, 0), (b_attend, 1, 1),
        (b_tokens, 1, 0), (b_second_norm, 0, 0), (in_project, 1, 1), (b_feed, 0, 0), (middle, 1, 1),
        (middle, 0, 0), (in_weights, 1, 1), (vec_start, 1, 0), (layer_input, 1, 1), (b_first_norm, 0, 0),
        (b_out_on, 1, 1), (b_on, 0, 0), (b_tokens, 1, 1), (out_back, 0, 0), (b_second_norm, 0, 1),
        (attn_mid, 1, 0), (vec_sum_t, 1, 0), (b_feed, 0, 1), (middle, 0, 1), (b_attend, 0, 0),
        (feed_end, 1, 0), (b_first_norm, 0, 1), (vec_sum_z, 1, 0), (feed_weights, 0, 1), (b_on, 0, 1),
        (in_project, 0, 0), (out_back, 0, 1), (middle, 0, 0), (feed_mid, 0, 0), (layer_input, 0, 0),
        (vec_end, 1, 0), (attn_end, 1, 0), (out_weights, 0, 1), (b_attend, 0, 1), (b_out_on, 0, 0),
        (b_tokens, 0, 0), (in_project, 0, 1), (in_weights, 0, 1), (attn_mid, 0, 0), (middle, 0, 1),
        (vec_start, 0, 0), (layer_input, 0, 1), (vec_sum_t, 0, 0), (b_out_on, 0, 1), (vec_sum_z, 0, 0),
        (b_tokens, 0, 1), (feed_end, 0, 0), (vec_end, 0, 0), (attn_end, 0, 0),
    )
    start()
    for step, layer, micro in schedule:
        step(layer, micro)
    finish()


def run_layers(n_z, x, g, idx, par, wa, wo, wu, wd):
    micros, rows, width = x.shape
    cols, hidden = wo.shape[0], wu.shape[1]
    n_t = lax.axis_size("tensor")
    own, slab = rows // n_t, width // n_z
    pair = (2, rows)
    both = (2, 2, rows)
    anywhere, vmem = pl.BlockSpec(memory_space=pl.ANY), pl.BlockSpec(memory_space=pltpu.VMEM)
    ins = dict(
        x_in=anywhere, g_in=anywhere, idx_in=vmem, par_in=vmem, wa_in=anywhere, wo_in=anywhere,
        wu_in=anywhere, wd_in=anywhere,
    )
    outs = dict(
        acts=(anywhere, x.shape, bf16), grads=(anywhere, x.shape, bf16),
        g_feed=(vmem, (slab, 2 * width), f32), g_attn=(vmem, (slab, width), f32),
        vec_out=(vmem, (8, width), f32), ent=(vmem, (micros, max(8, rows // CLUSTER), 128), f32),
    )
    sem = pltpu.SemaphoreType.DMA
    scratch = dict(
        x=((*pair, width), bf16), g=((*pair, width), bf16),
        wa=((2, width, 3 * cols), bf16), wo=((2, cols, width), bf16),
        wu=((2, width, hidden), bf16), wd=((2, hidden, width), bf16),
        idx=((2, *idx.shape), jnp.int32), par=((2, *par.shape), f32),
        xp=((*both, width), bf16), grouped=((*both, 3 * cols), bf16), ms=((*both, cols), bf16),
        n1=((2, 2, own, width), f32), inv1=((2, 2, own, 128), f32), hfull=((*both, width), bf16),
        act=((*both, hidden), bf16), gp=((*both, hidden), bf16),
        n2=((2, 2, own, width), f32), inv2=((2, 2, own, 128), f32),
        entropy=((2, 2, max(8, rows // CLUSTER), 128), f32),
        zs=((*pair, 3 * cols), bf16), zr=((*pair, 3 * cols), bf16), mixc=((*pair, cols), bf16),
        ms_src=((*pair, cols), bf16), dmr=((*pair, cols), bf16),
        sum_src=((2, 6, own, width // 2), bf16), sum_dst=((2, 6, own, width // 2), bf16),
        sum_keep=((2, 2, own, width // 2), f32), sum_own=((2, own, width), f32),
        hid=((2, own, width), f32), dres=((2, own, width), f32),
        ag=((*pair, width), bf16), db=((*pair, width), bf16), da=((*pair, width), bf16),
        gs_feed=((n_z, slab, 2 * width), bf16), gr_feed=((n_z, slab, 2 * width), bf16),
        gz_feed=((n_z - 1, slab, 2 * width), bf16),
        gs_attn=((n_z, slab, width), bf16), gr_attn=((n_z, slab, width), bf16),
        gz_attn=((n_z - 1, slab, width), bf16),
        vec=((2, 8, width), f32), vec_came=((8, width), f32), vec_t=((n_t, 8, width), f32),
        vec_z=((n_z, 8, width), f32),
    )
    sems = dict(load_sem=(8,))
    for name, shape in dict(
        swap=(6,), z=(4, 2, n_z - 1), sum=(2, 6), gather=(5, 2, 4), out=(2, 2), gc=(2, n_z),
        gz=(2, n_z - 1), vc=(1,), vt=(n_t - 1,), vz=(n_z - 1,), en=(2,),
    ).items():
        sems[name + "_s"] = shape
        sems[name + "_r"] = shape
    sems["out_l"] = (2, 2)
    names = [*ins, *outs, *scratch, *sems]
    return pl.pallas_call(
        functools.partial(layers_kernel, n_z, n_t, rows, width, cols, names),
        out_shape=[jax.ShapeDtypeStruct(shape, dtype) for _, shape, dtype in outs.values()],
        in_specs=list(ins.values()),
        out_specs=[spec for spec, _, _ in outs.values()],
        scratch_shapes=[
            *(pltpu.VMEM(shape, dtype) for shape, dtype in scratch.values()),
            *(sem(shape) for shape in sems.values()),
        ],
        compiler_params=pltpu.CompilerParams(
            collective_id=0, has_side_effects=True, vmem_limit_bytes=VMEM_LIMIT
        ),
        name="layers",
    )(x, g, idx, par, wa, wo, wu, wd)


def shards(
    inputs, out_grad, items, send_order, recv_order,
    attn_weight, qv_bias, out_weight, out_bias, norm_first,
    up_weight, up_bias, down_weight, down_bias, norm_second,
):
    micros, rows, width = inputs.shape
    n_z = lax.axis_size("dp")
    cols = attn_weight.shape[3]
    heads = cols // HEAD_DIM
    clusters = rows // CLUSTER

    idx = jnp.concatenate(
        [items[0], send_order[0, :, 0], recv_order[0, :, 0], jnp.zeros((4, rows), jnp.int32)]
    ).reshape(16, rows // 128, 1, 128)
    ba = jnp.concatenate(
        [qv_bias[0, 0], jnp.zeros((cols,), f32), qv_bias[0, 1], jnp.zeros((width - 3 * cols,), f32)]
    )
    par = jnp.concatenate(
        [ba[None], out_bias, norm_first[0], up_bias, down_bias, norm_second[0]]
    )
    acts, grads, g_feed, g_attn, vec, ent = run_layers(
        n_z, inputs, out_grad, idx, par, attn_weight[0].reshape(width, 3 * cols), out_weight[0],
        up_weight[0], down_weight[0],
    )
    item_numbers = jnp.arange(ITEMS, dtype=jnp.int32)
    grid = items[0].reshape(micros, clusters, CLUSTER)
    occupancy = jnp.sum((grid[..., None] == item_numbers).astype(f32), axis=2)
    results = (
        acts, grads.astype(f32), ent[:, :clusters, :heads], occupancy,
        g_attn[:, : 3 * cols].reshape(-1, 3, cols),
        jnp.stack([vec[7, :cols], vec[7, 2 * cols : 3 * cols]]), g_attn[:, 3 * cols :].T,
        vec[5], vec[3:5], g_feed[:, :width], vec[6], g_feed[:, width:].T, vec[2], vec[0:2],
    )
    return tuple(value[None] for value in results)


def solution(mesh):
    return jax.shard_map(
        shards,
        mesh=mesh,
        in_specs=(
            P(None, "dp", None),
            P(None, "dp", None),
            P("section", None, "dp"),
            P("section", None, "dp", None),
            P("section", None, "dp", None),
            P("section", None, None, "tensor"),
            P("section", None, "tensor"),
            P("section", "tensor", None),
            P("section", None),
            P("section", None, None),
            P("section", None, "tensor"),
            P("section", "tensor"),
            P("section", "tensor", None),
            P("section", None),
            P("section", None, None),
        ),
        out_specs=(
            P("section", None, "dp", None),
            P("section", None, "dp", None),
            P("section", None, "dp", "tensor"),
            P("section", None, "dp", None),
            P("section", "dp", None, "tensor"),
            P("section", None, "tensor"),
            P("section", "tensor", "dp"),
            P("section", None),
            P("section", None, None),
            P("section", "dp", "tensor"),
            P("section", "tensor"),
            P("section", "tensor", "dp"),
            P("section", None),
            P("section", None, None),
        ),
        check_vma=False,
    )
```

```python
import functools

import jax
import jax.numpy as jnp
from jax import lax
from jax.experimental import pallas as pl
from jax.experimental.pallas import tpu as pltpu
from jax.sharding import PartitionSpec as P

HEAD_DIM = 64
CLUSTER = 128
ITEMS = 6
EPSILON = 1e-06
MESH = pl.DeviceIdType.MESH
VMEM_LIMIT = 61 * 1024 * 1024
bf16 = jnp.bfloat16
f32 = jnp.float32


def nn(a, b):
    return lax.dot_general(a, b, (((1,), (0,)), ((), ())), preferred_element_type=f32)


def nt(a, b):
    return lax.dot_general(a, b, (((1,), (1,)), ((), ())), preferred_element_type=f32)


def tn(a, b):
    return lax.dot_general(a, b, (((0,), (0,)), ((), ())), preferred_element_type=f32)


def loop(count, body):
    def step(index, carry):
        body(index)
        return carry

    lax.fori_loop(0, count, step, 0)


def rows_at(index, size):
    return pl.ds(pl.multiple_of(index * size, size), size)


class Bag:
    def __init__(self, names, values):
        self.__dict__.update(zip(names, values, strict=True))


def place_rows(row, first, count):
    numbers = lax.broadcasted_iota(jnp.int32, (count, row.shape[1]), 0) + first
    return (numbers == row).astype(bf16)


def by_head(block, heads):
    lane = lax.broadcasted_iota(jnp.int32, block.shape, 1) // HEAD_DIM
    return jnp.concatenate([jnp.where(lane == h, block, jnp.zeros_like(block)) for h in range(heads)])


def fold_heads(stacked, heads):
    count = stacked.shape[0] // heads
    lane = lax.broadcasted_iota(jnp.int32, (count, stacked.shape[1]), 1) // HEAD_DIM
    total = jnp.where(lane == 0, stacked[:count], 0.0)
    for h in range(1, heads):
        total = jnp.where(lane == h, stacked[h * count : (h + 1) * count], total)
    return total


def softmax_parts(scores, same):
    masked = jnp.where(same, scores, -1e30)
    centred = masked - jnp.max(masked, axis=-1, keepdims=True)
    grown = jnp.exp(centred)
    total = jnp.sum(grown, axis=-1, keepdims=True)
    return grown / total, centred, total


def same_item(row):
    wide = jnp.broadcast_to(row.astype(f32), (row.shape[1], row.shape[1]))
    return wide == wide.T


def normalise(values):
    centre = jnp.mean(values, axis=-1, keepdims=True)
    spread = values - centre
    second = jnp.mean(spread * spread, axis=-1, keepdims=True)
    inverse = lax.rsqrt(second + EPSILON)
    return spread * inverse, inverse


def norm_backward(grad, normed, inverse, gain):
    scaled = grad * gain
    first = jnp.mean(scaled, axis=-1, keepdims=True)
    second = jnp.mean(scaled * normed, axis=-1, keepdims=True)
    return inverse * (scaled - first - normed * second)


def column_sum(value):
    return jnp.sum(value.astype(f32), axis=0, keepdims=True)


def remote(src, dst, sems, device):
    return pltpu.make_async_remote_copy(
        src_ref=src, dst_ref=dst, send_sem=sems[0], recv_sem=sems[1],
        device_id=device, device_id_type=MESH,
    )


def layers_kernel(n_z, n_t, rows, width, cols, names, *refs):
    r = Bag(names, refs)
    heads, half_width = cols // HEAD_DIM, width // 2
    scale = HEAD_DIM**-0.5
    core, z, t = lax.axis_index("section"), lax.axis_index("dp"), lax.axis_index("tensor")
    other = {"section": 1 - core}
    step_x, step_y = 1 - 2 * lax.rem(t, 2), 2 - 4 * (t // 2)
    t_x, t_y = t + step_x, t + step_y
    t_far = t + step_x + step_y
    piece, own = rows // n_z, rows // n_t
    chunk_rows = max(piece, 128)
    chunks, per_chunk = rows // chunk_rows, chunk_rows // piece
    mine = rows_at(t, own)
    weights = ("wa", "wo", "wu", "wd")

    def load(i):
        if i < 2:
            return pltpu.make_async_copy(r.x_in.at[core * 2 + i], r.x.at[i], r.load_sem.at[i])
        if i < 4:
            return pltpu.make_async_copy(r.g_in.at[core * 2 + i - 2], r.g.at[i - 2], r.load_sem.at[i])
        if i == 5:
            return pltpu.make_async_copy(r.wo_in, r.wo.at[core, t], r.load_sem.at[i])
        name = weights[i - 4]
        return pltpu.make_async_copy(
            getattr(r, name + "_in"), getattr(r, name).at[core], r.load_sem.at[i]
        )

    def swap(i):
        sems = (r.swap_s.at[i], r.swap_r.at[i])
        if i == 4:
            return remote(r.idx.at[core], r.idx.at[core], sems, other)
        if i == 5:
            return remote(r.par.at[core], r.par.at[core], sems, other)
        if i == 1:
            return remote(r.wo_in, r.wo.at[core, t], sems, other)
        name = weights[i]
        return remote(getattr(r, name + "_in"), getattr(r, name).at[core], sems, other)

    def start():
        for i in (0, 4, 1, 5, 6, 7, 2, 3):
            load(i).start()
        for kind, index in enumerate((r.items_in, r.send_in, r.recv_in)):
            for i in range(4):
                for c in range(rows // 128):
                    cut = slice(c * 128, (c + 1) * 128)
                    row = index[i : i + 1, cut] if kind == 0 else index[i, :, cut]
                    r.idx[core, kind * 4 + i, c] = row
        r.par[core, 0:1, :] = jnp.zeros((1, width), f32)
        r.par[core, 0:1, :cols] = r.qv_in[0:1]
        r.par[core, 0:1, 2 * cols : 3 * cols] = r.qv_in[1:2]
        for first, value in ((1, r.bo_in), (2, r.norm1_in), (4, r.bu_in), (5, r.bd_in), (6, r.norm2_in)):
            r.par[core, first : first + value.shape[0], :] = value[...]
        r.vec[...] = jnp.zeros(r.vec.shape, f32)
        barrier = pltpu.get_barrier_semaphore()
        pl.semaphore_signal(barrier, inc=1, device_id=other, device_id_type=MESH)

        def greet_z(k):
            peer = lax.rem(z + 1 + k, n_z)
            pl.semaphore_signal(barrier, inc=1, device_id={"dp": peer}, device_id_type=MESH)

        def greet_t(k):
            peer = lax.rem(t + 1 + k, n_t)
            pl.semaphore_signal(barrier, inc=1, device_id={"tensor": peer}, device_id_type=MESH)

        loop(n_z - 1, greet_z)
        loop(n_t - 1, greet_t)
        pl.semaphore_wait(barrier, n_z + n_t - 1)
        for i in (4, 5, 0, 1):
            swap(i).start()
        for k in range(1, n_t):
            wo_copy(k).start()
        for i in (2, 3):
            swap(i).start()
        swap(4).wait()
        swap(5).wait()

    def wo_copy(k):
        return remote(
            r.wo_in, r.wo.at[core, t], (r.wt_s.at[k - 1], r.wt_r.at[k - 1]),
            {"tensor": lax.rem(t + k, n_t)},
        )

    def wo_on_copy(k):
        slab = r.wo.at[core, lax.rem(t - k + n_t, n_t)]
        return remote(slab, slab, (r.wc_s.at[k - 1], r.wc_r.at[k - 1]), other)

    def out_weight_on(l, m):
        load(5).wait()
        for k in range(1, n_t):
            wo_copy(k).wait_recv()
            wo_on_copy(k).start()

    asked = set()

    def need_weight(layer, i):
        if (layer, i) in asked:
            return
        asked.add((layer, i))

        if i != 1:

            @pl.when(core == layer)
            def _():
                load(4 + i).wait()

        @pl.when(core != layer)
        def _():
            swap(i).wait_recv()
            if i == 1:
                for k in range(1, n_t):
                    wo_on_copy(k).wait_recv()

    def index_cut(kind, layer, m, first, count):
        cuts = [
            r.idx[layer, kind * 4 + core * 2 + m, first // 128 + i] for i in range(count // 128)
        ]
        return cuts[0] if len(cuts) == 1 else jnp.concatenate(cuts, axis=1)

    def index_row(kind, layer, m):
        return index_cut(kind, layer, m, 0, rows)

    def par(layer, i, count=None):
        return r.par[layer, i : i + 1, : count or width]

    def z_copy(kind, m, k, src, dst):
        peer = lax.rem(z + k, n_z)
        return remote(
            src.at[rows_at(peer, piece)], dst.at[rows_at(z, piece)],
            (r.z_s.at[kind, m, k - 1], r.z_r.at[kind, m, k - 1]), {"dp": peer},
        )

    def z_chunk(kk):
        return lax.rem(z // per_chunk + 1 + kk, chunks)

    def z_send(kind, m, cc, src, dst):
        def one(j):
            peer = cc * per_chunk + j
            k = lax.rem(peer - z + n_z, n_z)

            @pl.when(k > 0)
            def _():
                z_copy(kind, m, k, src, dst).start()

        loop(per_chunk, one)

    def z_wait(kind, m, src, dst):
        loop(n_z - 1, lambda k: z_copy(kind, m, k + 1, src, dst).wait())

    def keep_piece(src, dst, m):
        here = rows_at(z, piece)
        dst[m, here] = src[m, here]

    left, right = slice(0, half_width), slice(half_width, width)

    def sum_copy(m, j):
        peer = t_x if j in (0, 1, 5) else t_y
        return remote(
            r.sum_src.at[m, j], r.sum_dst.at[m, j], (r.sum_s.at[m, j], r.sum_r.at[m, j]),
            {"tensor": peer},
        )

    def sum_put(m, role, part):
        @pl.when(role == 0)
        def _():
            r.sum_own[m] = part

        @pl.when(role == 1)
        def _():
            r.sum_src[m, 1] = part[:, left].astype(bf16)
            r.sum_keep[m, 1] = part[:, right].astype(bf16)
            sum_copy(m, 1).start()

        @pl.when(role == 2)
        def _():
            r.sum_src[m, 3] = part[:, right].astype(bf16)
            r.sum_keep[m, 0] = part[:, left].astype(bf16)
            sum_copy(m, 3).start()

        @pl.when(role == 3)
        def _():
            r.sum_src[m, 0] = part[:, left].astype(bf16)
            sum_copy(m, 0).start()
            r.sum_src[m, 2] = part[:, right].astype(bf16)
            sum_copy(m, 2).start()

    def sum_mid(m):
        sum_copy(m, 0).wait_recv()
        r.sum_src[m, 4] = (r.sum_keep[m, 0].astype(f32) + r.sum_dst[m, 0].astype(f32)).astype(bf16)
        sum_copy(m, 4).start()
        sum_copy(m, 2).wait_recv()
        r.sum_src[m, 5] = (r.sum_keep[m, 1].astype(f32) + r.sum_dst[m, 2].astype(f32)).astype(bf16)
        sum_copy(m, 5).start()

    def sum_take(m):
        for j in (1, 3, 4, 5):
            sum_copy(m, j).wait_recv()
        for j in range(6):
            sum_copy(m, j).wait_send()
        added = jnp.concatenate(
            [
                r.sum_dst[m, 1].astype(f32) + r.sum_dst[m, 4].astype(f32),
                r.sum_dst[m, 3].astype(f32) + r.sum_dst[m, 5].astype(f32),
            ],
            axis=1,
        )
        return r.sum_own[m] + added

    def role_rows(role):
        return rows_at(t + lax.rem(role, 2) * step_x + (role // 2) * step_y, own)

    def gather_copy(kind, m, j, buf):
        first = (t, t, t, t, t_x, t_y)[j] * own
        low = j in (1, 2, 5)
        here = pl.ds(pl.multiple_of(first + (own // 2 if low else 0), own // 2), own // 2)
        return remote(
            buf.at[here], buf.at[here], (r.gather_s.at[kind, m, j], r.gather_r.at[kind, m, j]),
            {"tensor": t_x if j in (0, 1, 5) else t_y},
        )

    def gather_start(kind, m, buf):
        for j in (0, 2, 1, 3):
            gather_copy(kind, m, j, buf).start()

    def gather_on(kind, m, buf):
        gather_copy(kind, m, 0, buf).wait_recv()
        gather_copy(kind, m, 4, buf).start()
        gather_copy(kind, m, 2, buf).wait_recv()
        gather_copy(kind, m, 5, buf).start()

    def gather_near(kind, m, buf, j):
        gather_copy(kind, m, j, buf).wait_recv()

    def gather_far(kind, m, buf):
        gather_copy(kind, m, 4, buf).wait_recv()
        gather_copy(kind, m, 5, buf).wait_recv()

    def gather_rest(kind, m, buf):
        for j in (1, 3, 4, 5):
            gather_copy(kind, m, j, buf).wait_recv()
        gather_sent(kind, m, buf)

    def gather_sent(kind, m, buf):
        for j in range(6):
            gather_copy(kind, m, j, buf).wait_send()

    def gather_step(kind, m, role, buf):
        @pl.when(role == 1)
        def _():
            gather_on(kind, m, buf)
            gather_near(kind, m, buf, 1)

        @pl.when(role == 2)
        def _():
            gather_near(kind, m, buf, 3)

        @pl.when(role == 3)
        def _():
            gather_far(kind, m, buf)

    def out_local(kind, m, src, out):
        return pltpu.make_async_copy(src, out.at[core * 2 + m], r.out_l.at[kind, m])

    def out_away(kind, m, src, out):
        return remote(src, out.at[core * 2 + m], (r.out_s.at[kind, m], r.out_r.at[kind, m]), other)

    def out_start(kind, layer, m, src, out):
        @pl.when(core == layer)
        def _():
            out_local(kind, m, src, out).start()

        @pl.when(core != layer)
        def _():
            out_away(kind, m, src, out).start()

    def out_wait(kind, layer, m, src, out):
        @pl.when(core == layer)
        def _():
            out_local(kind, m, src, out).wait()

        @pl.when(core != layer)
        def _():
            out_away(kind, m, src, out).wait_send()

    def project(l, m):
        need_weight(l, 0)
        if l == 0:
            load(m).wait()

        def chunk(kk):
            cc = z_chunk(kk)
            here = rows_at(cc, chunk_rows)
            numbers = lax.broadcasted_iota(jnp.int32, (rows, chunk_rows), 0)
            pick = (numbers == index_cut(1, l, m, cc * chunk_rows, chunk_rows)).astype(bf16)
            moved = tn(pick, r.x[m]).astype(bf16)
            r.xp[l, m, here] = moved
            r.zs[m, here] = (nt(moved, r.wa[l]) + par(l, 0, 3 * cols)).astype(bf16)
            z_send(0, m, cc, r.zs.at[m], r.zr.at[m])

        loop(chunks, chunk)
        keep_piece(r.zs, r.zr, m)

    def attend(l, m):
        z_wait(0, m, r.zs.at[m], r.zr.at[m])
        lane = lax.broadcasted_iota(jnp.int32, (1, 128), 1)

        def cluster(c):
            here = rows_at(c, CLUSTER)
            numbers = lax.broadcasted_iota(jnp.int32, (rows, CLUSTER), 0)
            pick = (numbers == index_cut(2, l, m, c * CLUSTER, CLUSTER)).astype(bf16)
            block = tn(pick, r.zr[m]).astype(bf16)
            r.grouped[l, m, here] = block
            queries, keys, values = (block[:, i * cols : (i + 1) * cols] for i in range(3))
            scores = nt(queries, by_head(keys, heads)) * scale
            same = same_item(index_cut(0, l, m, c * CLUSTER, CLUSTER))
            probs = []
            log_row = jnp.zeros((1, 128), f32)
            for h in range(heads):
                cut = slice(h * CLUSTER, (h + 1) * CLUSTER)
                prob, centred, total = softmax_parts(scores[:, cut], same)
                inner = jnp.sum(jnp.where(same, prob * centred, 0.0), axis=-1, keepdims=True)
                entropy = jnp.mean(jnp.log(total) - inner, axis=0, keepdims=True)
                log_row = jnp.where(lane == h, entropy, log_row)
                probs.append(prob.astype(bf16))
            r.entropy[l, m, pl.ds(c, 1)] = log_row
            mixed = nn(jnp.concatenate(probs, axis=1), by_head(values, heads))
            r.dmt[m, here] = mixed.astype(bf16)

        loop(rows // CLUSTER, cluster)

        def home(kk):
            cc = z_chunk(kk)
            here = rows_at(cc, chunk_rows)
            one_hot = place_rows(index_row(2, l, m), cc * chunk_rows, chunk_rows)
            r.dmr[m, here] = nn(one_hot, r.dmt[m]).astype(bf16)
            z_send(1, m, cc, r.dmr.at[m], r.ms.at[m])

        loop(chunks, home)
        keep_piece(r.dmr, r.ms, m)

    def heads_copy(l, m, k):
        peer = lax.rem(t + k, n_t)
        return remote(
            r.ms.at[m, rows_at(peer, own)], r.mt.at[l, m, t],
            (r.ta_s.at[m, k - 1], r.ta_r.at[m, k - 1]), {"tensor": peer},
        )

    def out_project(l, m):
        z_wait(1, m, r.dmr.at[m], r.ms.at[m])
        for k in (2, 1, 3):
            heads_copy(l, m, k).start()
        r.mt[l, m, t] = r.ms[m, mine]

    def middle(l, m):
        sum_mid(m)

    def first_norm(l, m):
        need_weight(l, 1)
        for k in range(1, n_t):
            heads_copy(l, m, k).wait()
        total = r.xp[l, m, mine].astype(f32) + par(l, 1)
        for s in range(n_t):
            total = total + nn(r.mt[l, m, s], r.wo[l, s])
        normed, inverse = normalise(total)
        hidden = normed * par(l, 2) + par(l, 3)
        r.n1[l, m] = normed.astype(bf16)
        r.inv1[l, m] = jnp.broadcast_to(inverse, (own, 128))
        r.hid[m] = hidden
        r.hfull[l, m, mine] = hidden.astype(bf16)
        gather_start(0, m, r.hfull.at[l, m])

    def feed(l, m):
        need_weight(l, 2)
        need_weight(l, 3)

        def part(role):
            gather_step(0, m, role, r.hfull.at[l, m])
            here = role_rows(role)
            up = nn(r.hfull[l, m, here], r.wu[l]) + par(l, 4)
            square = up * up
            tanh = jnp.tanh(0.7978845608028654 * up * (1.0 + 0.044715 * square))
            half = 0.5 * (1.0 + tanh)
            slope = 0.7978845608028654 * (1.0 + 3 * 0.044715 * square)
            r.gp[l, m, here] = (half + 0.5 * up * (1.0 - tanh * tanh) * slope).astype(bf16)
            active = (up * half).astype(bf16)
            r.act[l, m, here] = active
            sum_put(m, role, nn(active, r.wd[l]))

        loop(n_t, part)

    def second_norm(l, m):
        gather_sent(0, m, r.hfull.at[l, m])
        total = sum_take(m) + par(l, 5)
        normed, inverse = normalise(r.hid[m] + total)
        r.n2[l, m] = normed.astype(bf16)
        r.inv2[l, m] = jnp.broadcast_to(inverse, (own, 128))
        r.ag[m, mine] = (normed * par(l, 6) + par(l, 7)).astype(bf16)
        gather_start(1, m, r.ag.at[m])

    def out_on(l, m):
        gather_on(1, m, r.ag.at[m])

    def to_tokens(l, m, dst, buf):
        def chunk(cc):
            one_hot = place_rows(index_row(1, l, m), cc * 128, 128)
            dst[m, rows_at(cc, 128)] = nn(one_hot, buf[m]).astype(bf16)

        loop(rows // 128, chunk)

    def out_tokens(l, m):
        gather_rest(1, m, r.ag.at[m])
        if l == 1:
            out_wait(0, 0, m, r.x.at[m], r.acts)
        to_tokens(l, m, r.x, r.ag)
        out_start(0, l, m, r.x.at[m], r.acts)

    def add_vec(l, index, value):
        r.vec[l, index : index + 1, : value.shape[1]] += value

    def b_second_norm(l, m):
        if l == 1:
            load(2 + m).wait()
        numbers = lax.broadcasted_iota(jnp.int32, (rows, own), 0)
        pick = (numbers == index_cut(1, l, m, t * own, own)).astype(bf16)
        up = tn(pick, r.g[m])
        normed = r.n2[l, m].astype(f32)
        down = norm_backward(up, normed, r.inv2[l, m][:, :1], par(l, 6))
        r.hid[m] = down
        low = down.astype(bf16)
        r.db[m, mine] = low
        gather_start(2, m, r.db.at[m])
        add_vec(l, 0, column_sum(up * normed))
        add_vec(l, 1, column_sum(up))
        add_vec(l, 2, column_sum(low))

    def b_feed(l, m):
        def part(role):
            gather_step(2, m, role, r.db.at[m])
            here = role_rows(role)
            low = (nt(r.db[m, here], r.wd[l]) * r.gp[l, m, here].astype(f32)).astype(bf16)
            r.gp[l, m, here] = low
            sum_put(m, role, nt(low, r.wu[l]))

        loop(n_t, part)

    def grad_slabs(ref, value, lanes):
        ref[:, :, lanes] = value.reshape(n_z, width // n_z, value.shape[1]).astype(bf16)

    def feed_weights(l, m):
        for i in range(2):
            gather_sent(2, i, r.db.at[i])
            add_vec(l, 6, column_sum(r.gp[l, i]))

        def block(c):
            cut = rows_at(c, 256)
            up = tn(r.hfull[l, 0], r.gp[l, 0, :, cut]) + tn(r.hfull[l, 1], r.gp[l, 1, :, cut])
            grad_slabs(r.gs_feed, up, cut)
            down = tn(r.db[0], r.act[l, 0, :, cut]) + tn(r.db[1], r.act[l, 1, :, cut])
            grad_slabs(r.gs_feed, down, pl.ds(pl.multiple_of(width + c * 256, 256), 256))

        loop(width // 256, block)
        grads_send(0, l, r.gs_feed, r.gr_feed)

    def b_first_norm(l, m):
        up = r.hid[m] + sum_take(m)
        normed = r.n1[l, m].astype(f32)
        down = norm_backward(up, normed, r.inv1[l, m][:, :1], par(l, 2))
        r.dres[m] = down
        low = down.astype(bf16)
        r.da[m] = low

        def part(kk):
            k = lax.rem(kk + 1, n_t)
            peer = lax.rem(t + k, n_t)
            block = nt(low, r.wo[l, peer]).astype(bf16)

            @pl.when(k > 0)
            def _():
                r.ms[m, rows_at(peer, own)] = block
                rows_copy(m, k).start()

            @pl.when(k == 0)
            def _():
                r.dmt[m, mine] = block

        loop(n_t, part)
        add_vec(l, 3, column_sum(up * normed))
        add_vec(l, 4, column_sum(up))
        add_vec(l, 5, column_sum(low))

    def rows_copy(m, k):
        peer = lax.rem(t + k, n_t)
        return remote(
            r.ms.at[m, rows_at(peer, own)], r.dmt.at[m, mine], (r.tb_s.at[m, k - 1], r.tb_r.at[m, k - 1]),
            {"tensor": peer},
        )

    def out_back(l, m):
        for k in range(1, n_t):
            rows_copy(m, k).wait()
        loop(chunks, lambda kk: z_send(2, m, z_chunk(kk), r.dmt.at[m], r.dmr.at[m]))
        keep_piece(r.dmt, r.dmr, m)

    def out_weights(l, m):
        for s in range(n_t):
            value = tn(r.da[0], r.mt[l, 0, s]) + tn(r.da[1], r.mt[l, 1, s])
            r.gs_out[s] = value.reshape(n_z, width // n_z, cols).astype(bf16)

        @pl.when(core != l)
        def _():
            for k in range(n_t):
                out_core_copy(lax.rem(t + 1 + k, n_t)).start()

    def b_attend(l, m):
        z_wait(2, m, r.dmt.at[m], r.dmr.at[m])

        def cluster(c):
            here = rows_at(c, CLUSTER)
            numbers = lax.broadcasted_iota(jnp.int32, (rows, CLUSTER), 0)
            pick = (numbers == index_cut(2, l, m, c * CLUSTER, CLUSTER)).astype(bf16)
            dmix = tn(pick, r.dmr[m]).astype(bf16)
            block = r.grouped[l, m, here]
            queries, keys, values = (block[:, i * cols : (i + 1) * cols] for i in range(3))
            keys_by_head = by_head(keys, heads)
            scores = nt(queries, keys_by_head) * scale
            same = same_item(index_cut(0, l, m, c * CLUSTER, CLUSTER))
            dprob = nt(dmix, by_head(values, heads))
            probs, dscores = [], []
            for h in range(heads):
                cut = slice(h * CLUSTER, (h + 1) * CLUSTER)
                prob = softmax_parts(scores[:, cut], same)[0]
                outer = prob * dprob[:, cut]
                dscore = outer - prob * jnp.sum(outer, axis=-1, keepdims=True)
                probs.append(prob.astype(bf16))
                dscores.append(dscore.astype(bf16))
            prob_all = jnp.concatenate(probs, axis=1)
            dscore_all = jnp.concatenate(dscores, axis=1)
            dqueries = nn(dscore_all, keys_by_head) * scale
            dkeys = fold_heads(tn(dscore_all, queries), heads) * scale
            dvalues = fold_heads(tn(prob_all, dmix), heads)
            r.grouped[l, m, here] = jnp.concatenate([dqueries, dkeys, dvalues], axis=1).astype(bf16)

        loop(rows // CLUSTER, cluster)

        def home(kk):
            cc = z_chunk(kk)
            here = rows_at(cc, chunk_rows)
            one_hot = place_rows(index_row(2, l, m), cc * chunk_rows, chunk_rows)
            r.zs[m, here] = nn(one_hot, r.grouped[l, m]).astype(bf16)
            z_send(3, m, cc, r.zs.at[m], r.zr.at[m])

        loop(chunks, home)
        keep_piece(r.zs, r.zr, m)

    def in_project(l, m):
        z_wait(3, m, r.zs.at[m], r.zr.at[m])

        def part(kk):
            role = 3 - kk
            sum_put(m, role, nn(r.zr[m, role_rows(role)], r.wa[l]))

        loop(n_t, part)

    def in_weights(l, m):
        for i in range(2):
            add_vec(l, 7, column_sum(r.zr[i]))
        for first in range(0, 3 * cols, 256):
            cut = slice(first, min(first + 256, 3 * cols))
            value = tn(r.xp[l, 0], r.zr[0, :, cut]) + tn(r.xp[l, 1], r.zr[1, :, cut])
            grad_slabs(r.gs_attn, value, cut)
        grads_send(1, l, r.gs_attn, r.gr_attn)

    def layer_input(l, m):
        r.ag[m, mine] = (r.dres[m] + sum_take(m)).astype(bf16)
        gather_start(4, m, r.ag.at[m])

    def b_out_on(l, m):
        gather_on(4, m, r.ag.at[m])

    def b_tokens(l, m):
        gather_rest(4, m, r.ag.at[m])
        if l == 0:
            out_wait(1, 1, m, r.g.at[m], r.grads)
        to_tokens(l, m, r.g, r.ag)
        out_start(1, l, m, r.g.at[m], r.grads)

    def grad_core_copy(kind, k, src, dst):
        return remote(src.at[k], dst.at[k], (r.gc_s.at[kind, k], r.gc_r.at[kind, k]), other)

    def grad_z_copy(kind, k, src, dst, lanes=slice(None)):
        peer = lax.rem(z + k, n_z)
        return remote(
            src.at[peer, :, lanes], dst.at[k - 1, :, lanes], (r.gz_s.at[kind, k - 1], r.gz_r.at[kind, k - 1]),
            {"dp": peer},
        )

    def grads_send(kind, l, src, dst):
        @pl.when(core != l)
        def _():
            loop(n_z, lambda k: grad_core_copy(kind, lax.rem(z + 1 + k, n_z), src, dst).start())

    def grads_add(kind, src, came, k, wait, lanes):
        peer = lax.rem(z + k, n_z)
        if wait:
            grad_core_copy(kind, peer, src, came).wait_recv()
        total = src[peer, :, lanes].astype(f32) + came[peer, :, lanes].astype(f32)
        src[peer, :, lanes] = total.astype(bf16)

    def grads_part(kind, sem, l, src, came, dst, part, wait, lanes):
        @pl.when(core == l)
        def _():
            first, last = part * (n_z - 1) // 3, (part + 1) * (n_z - 1) // 3

            def one(i):
                grads_add(kind, src, came, first + 1 + i, wait, lanes)
                grad_z_copy(sem, first + 1 + i, src, dst, lanes).start()

            loop(last - first, one)

    def grads_end(kind, sems, l, src, came, dst, outs):
        @pl.when(core == l)
        def _():
            lanes = src.shape[2] // len(sems)
            for i in range(len(sems)):
                grads_add(kind, src, came, 0, i == 0, slice(i * lanes, (i + 1) * lanes))
            cuts, first = [], 0
            for out in outs:
                cuts.append(slice(first, first + out.shape[-1]))
                first += out.shape[-1]
            for out, cut in zip(outs, cuts):
                out[...] = src[z, :, cut].astype(f32)

            def one(k):
                for i, sem in enumerate(sems):
                    grad_z_copy(sem, k + 1, src, dst, slice(i * lanes, (i + 1) * lanes)).wait()
                for out, cut in zip(outs, cuts):
                    out[...] += dst[k, :, cut].astype(f32)

            loop(n_z - 1, one)

        @pl.when(core != l)
        def _():
            loop(n_z, lambda k: grad_core_copy(kind, k, src, came).wait_send())

    def feed_part(i):
        lanes = slice(0, width) if i % 2 == 0 else slice(width, 2 * width)
        return lambda l, m: grads_part(
            0, i % 2, l, r.gs_feed, r.gr_feed, r.gz_feed, i // 2, i % 2 == 0, lanes
        )

    def attn_part(i):
        return lambda l, m: grads_part(
            1, 2, l, r.gs_attn, r.gr_attn, r.gz_attn, i, True, slice(None)
        )

    feed_0, feed_1, feed_2, feed_3, feed_4, feed_5 = (feed_part(i) for i in range(6))
    attn_0, attn_1, attn_2 = (attn_part(i) for i in range(3))

    def feed_end(l, m):
        grads_end(0, (0, 1), l, r.gs_feed, r.gr_feed, r.gz_feed, (r.g_up, r.g_down))

    def attn_end(l, m):
        grads_end(1, (2,), l, r.gs_attn, r.gr_attn, r.gz_attn, tuple(r.g_attn.at[i] for i in range(3)))

    def out_core_copy(s):
        return remote(r.gs_out.at[s], r.gr_out.at[s], (r.oc_s.at[s], r.oc_r.at[s]), other)

    def out_t_copy(k):
        peer = lax.rem(t + k, n_t)
        return remote(
            r.gs_out.at[peer], r.gt_out.at[k - 1], (r.ot_s.at[k - 1], r.ot_r.at[k - 1]),
            {"tensor": peer},
        )

    def out_z_copy(k):
        peer = lax.rem(z + k, n_z)
        return remote(
            r.gs_out.at[t, peer], r.gz_out.at[k - 1], (r.gz_s.at[3, k - 1], r.gz_r.at[3, k - 1]),
            {"dp": peer},
        )

    def out_sum_t(l, m):
        @pl.when(core == l)
        def _():
            for kk in range(n_t):
                k = (kk + 1) % n_t
                s = lax.rem(t + k, n_t)
                out_core_copy(s).wait_recv()
                r.gs_out[s] = (r.gs_out[s].astype(f32) + r.gr_out[s].astype(f32)).astype(bf16)
                if k > 0:
                    out_t_copy(k).start()

    def out_sum_z(l, m):
        @pl.when(core == l)
        def _():
            for k in range(1, n_t):
                out_t_copy(k).wait()
            total = r.gs_out[t].astype(f32)
            for k in range(1, n_t):
                total = total + r.gt_out[k - 1].astype(f32)
            r.gs_out[t] = total.astype(bf16)
            loop(n_z - 1, lambda k: out_z_copy(k + 1).start())

        @pl.when(core != l)
        def _():
            for s in range(n_t):
                out_core_copy(s).wait_send()

    def out_end(l, m):
        @pl.when(core == l)
        def _():
            r.g_out[...] = r.gs_out[t, z].astype(f32)

            def one(k):
                out_z_copy(k + 1).wait()
                r.g_out[...] += r.gz_out[k].astype(f32)

            loop(n_z - 1, one)

    def vec_copy(l):
        return remote(r.vec.at[l], r.vec_came, (r.vc_s.at[0], r.vc_r.at[0]), other)

    def vec_t_copy(k):
        return remote(
            r.vec_t.at[t], r.vec_t.at[t], (r.vt_s.at[k - 1], r.vt_r.at[k - 1]),
            {"tensor": lax.rem(t + k, n_t)},
        )

    def vec_z_copy(k):
        return remote(
            r.vec_z.at[z], r.vec_z.at[z], (r.vz_s.at[k - 1], r.vz_r.at[k - 1]),
            {"dp": lax.rem(z + k, n_z)},
        )

    def entropy_copy(l, m):
        return remote(
            r.entropy.at[l, m], r.ent.at[core * 2 + m], (r.en_s.at[m], r.en_r.at[m]), other
        )

    def vec_start(l, m):
        @pl.when(core != l)
        def _():
            vec_copy(l).start()
            for i in range(2):
                entropy_copy(l, i).start()

    def vec_sum_t(l, m):
        @pl.when(core == l)
        def _():
            for i in range(2):
                r.ent[core * 2 + i] = r.entropy[l, i]
            vec_copy(l).wait_recv()
            r.vec_t[t] = r.vec[l] + r.vec_came[...]
            for k in range(1, n_t):
                vec_t_copy(k).start()

    def vec_sum_z(l, m):
        @pl.when(core == l)
        def _():
            for k in range(1, n_t):
                vec_t_copy(k).wait()
            total = r.vec_t[0]
            for k in range(1, n_t):
                total = total + r.vec_t[k]
            lane_rows = lax.broadcasted_iota(jnp.int32, total.shape, 0)
            r.vec_z[z] = jnp.where(lane_rows < 6, total, r.vec_t[t])
            loop(n_z - 1, lambda k: vec_z_copy(k + 1).start())

    def vec_end(l, m):
        @pl.when(core == l)
        def _():
            loop(n_z - 1, lambda k: vec_z_copy(k + 1).wait())
            r.vec_out[...] = r.vec_z[0]

            def one(k):
                r.vec_out[...] += r.vec_z[k + 1]

            loop(n_z - 1, one)

        @pl.when(core != l)
        def _():
            vec_copy(l).wait_send()
            for i in range(2):
                entropy_copy(l, i).wait_send()

    def finish():
        for m in range(2):
            out_wait(0, 1, m, r.x.at[m], r.acts)
            out_wait(1, 0, m, r.g.at[m], r.grads)
            for kind, out, src in ((0, r.acts, r.x), (1, r.grads, r.g)):
                out_away(kind, m, src.at[m], out).wait_recv()
            entropy_copy(0, m).wait_recv()
        for i in range(4):
            swap(i).wait_send()
        for k in range(1, n_t):
            wo_copy(k).wait_send()
            wo_on_copy(k).wait_send()

    schedule = (
        (project, 0, 1), (attend, 0, 1), (project, 0, 0), (out_weight_on, 0, 0), (out_project, 0, 1),
        (first_norm, 0, 1), (feed, 0, 1), (attend, 0, 0), (middle, 0, 1), (second_norm, 0, 1),
        (out_project, 0, 0), (out_on, 0, 1), (first_norm, 0, 0), (out_tokens, 0, 1), (project, 1, 1),
        (feed, 0, 0), (middle, 0, 0), (attend, 1, 1), (second_norm, 0, 0), (out_project, 1, 1),
        (out_on, 0, 0), (first_norm, 1, 1), (out_tokens, 0, 0), (project, 1, 0), (feed, 1, 1), (middle, 1, 1),
        (second_norm, 1, 1), (attend, 1, 0), (out_on, 1, 1), (b_second_norm, 1, 1), (out_tokens, 1, 1),
        (out_project, 1, 0), (b_feed, 1, 1), (first_norm, 1, 0), (middle, 1, 1), (feed, 1, 0),
        (b_first_norm, 1, 1), (middle, 1, 0), (out_back, 1, 1), (second_norm, 1, 0), (b_second_norm, 1, 0),
        (b_attend, 1, 1), (out_on, 1, 0), (b_feed, 1, 0), (feed_weights, 1, 1), (middle, 1, 0),
        (in_project, 1, 1), (b_first_norm, 1, 0), (out_weights, 1, 1), (middle, 1, 1), (out_tokens, 1, 0),
        (out_back, 1, 0), (layer_input, 1, 1), (feed_0, 1, 1), (b_out_on, 1, 1), (b_attend, 1, 0),
        (b_tokens, 1, 1), (b_second_norm, 0, 1), (feed_1, 1, 1), (b_feed, 0, 1), (feed_2, 1, 1),
        (in_project, 1, 0), (in_weights, 1, 1), (feed_3, 1, 1), (middle, 0, 1), (feed_4, 1, 1),
        (middle, 1, 0), (b_first_norm, 0, 1), (layer_input, 1, 0), (vec_start, 1, 1), (out_back, 0, 1),
        (b_out_on, 1, 0), (feed_5, 1, 1), (out_sum_t, 1, 1), (b_tokens, 1, 0), (attn_0, 1, 1), (attn_1, 1, 1),
        (b_second_norm, 0, 0), (attn_2, 1, 1), (b_attend, 0, 1), (vec_sum_t, 1, 1), (b_feed, 0, 0),
        (feed_end, 1, 1), (out_sum_z, 1, 1), (middle, 0, 0), (feed_weights, 0, 1), (b_first_norm, 0, 0),
        (out_back, 0, 0), (in_project, 0, 1), (vec_sum_z, 1, 1), (middle, 0, 1), (feed_0, 0, 1),
        (feed_1, 0, 1), (b_attend, 0, 0), (out_end, 1, 1), (layer_input, 0, 1), (out_weights, 0, 1),
        (feed_2, 0, 1), (feed_3, 0, 1), (out_sum_t, 0, 1), (attn_end, 1, 1), (feed_4, 0, 1),
        (in_project, 0, 0), (b_out_on, 0, 1), (in_weights, 0, 1), (middle, 0, 0), (out_sum_z, 0, 1),
        (attn_0, 0, 1), (vec_start, 0, 1), (attn_1, 0, 1), (attn_2, 0, 1), (vec_end, 1, 1),
        (layer_input, 0, 0), (feed_5, 0, 1), (vec_sum_t, 0, 1), (b_tokens, 0, 1), (b_out_on, 0, 0),
        (b_tokens, 0, 0), (out_end, 0, 1), (vec_sum_z, 0, 1), (attn_end, 0, 1), (feed_end, 0, 1),
        (vec_end, 0, 1),
    )
    start()
    for step, layer, micro in schedule:
        step(layer, micro)
    finish()


def run_layers(n_z, x, g, small, wa, wo, wu, wd):
    micros, rows, width = x.shape
    cols, hidden = wo.shape[0], wu.shape[1]
    n_t = lax.axis_size("tensor")
    own, slab = rows // n_t, width // n_z
    pair = (2, rows)
    both = (2, 2, rows)
    anywhere, vmem = pl.BlockSpec(memory_space=pl.ANY), pl.BlockSpec(memory_space=pltpu.VMEM)
    ins = dict(
        x_in=anywhere, g_in=anywhere, items_in=vmem, send_in=vmem, recv_in=vmem, qv_in=vmem,
        bo_in=vmem, norm1_in=vmem, bu_in=vmem, bd_in=vmem, norm2_in=vmem, wa_in=anywhere, wo_in=anywhere,
        wu_in=anywhere, wd_in=anywhere,
    )
    outs = dict(
        acts=(anywhere, x.shape, bf16), grads=(anywhere, x.shape, bf16),
        g_up=(vmem, (slab, width), f32), g_down=(vmem, (slab, width), f32),
        g_attn=(vmem, (3, slab, cols), f32),
        g_out=(vmem, (slab, cols), f32),
        vec_out=(vmem, (8, width), f32), ent=(vmem, (micros, max(8, rows // CLUSTER), 128), f32),
    )
    sem = pltpu.SemaphoreType.DMA
    scratch = dict(
        x=((*pair, width), bf16), g=((*pair, width), bf16),
        wa=((2, 3 * cols, width), bf16), wo=((2, n_t, cols, width), bf16),
        wu=((2, width, hidden), bf16), wd=((2, hidden, width), bf16),
        idx=((2, 12, rows // 128, 1, 128), jnp.int32), par=((2, 8, width), f32),
        xp=((*both, width), bf16), grouped=((*both, 3 * cols), bf16), ms=((*pair, cols), bf16),
        mt=((2, 2, n_t, own, cols), bf16),
        n1=((2, 2, own, width), bf16), inv1=((2, 2, own, 128), f32), hfull=((*both, width), bf16),
        act=((*both, hidden), bf16), gp=((*both, hidden), bf16),
        n2=((2, 2, own, width), bf16), inv2=((2, 2, own, 128), f32),
        entropy=((2, 2, max(8, rows // CLUSTER), 128), f32),
        zs=((*pair, 3 * cols), bf16), zr=((*pair, 3 * cols), bf16),
        dmr=((*pair, cols), bf16),
        sum_src=((2, 6, own, width // 2), bf16), sum_dst=((2, 6, own, width // 2), bf16),
        sum_keep=((2, 2, own, width // 2), bf16), sum_own=((2, own, width), f32),
        hid=((2, own, width), f32), dres=((2, own, width), f32),
        ag=((*pair, width), bf16), db=((*pair, width), bf16), da=((2, own, width), bf16),
        dmt=((*pair, cols), bf16),
        gs_feed=((n_z, slab, 2 * width), bf16), gr_feed=((n_z, slab, 2 * width), bf16),
        gz_feed=((n_z - 1, slab, 2 * width), bf16),
        gs_attn=((n_z, slab, 3 * cols), bf16), gr_attn=((n_z, slab, 3 * cols), bf16),
        gz_attn=((n_z - 1, slab, 3 * cols), bf16),
        gs_out=((n_t, n_z, slab, cols), bf16), gr_out=((n_t, n_z, slab, cols), bf16),
        gt_out=((n_t - 1, n_z, slab, cols), bf16), gz_out=((n_z - 1, slab, cols), bf16),
        vec=((2, 8, width), f32), vec_came=((8, width), f32), vec_t=((n_t, 8, width), f32),
        vec_z=((n_z, 8, width), f32),
    )
    sems = dict(load_sem=(8,))
    for name, shape in dict(
        swap=(6,), z=(4, 2, n_z - 1), sum=(2, 6), gather=(5, 2, 6), out=(2, 2), gc=(2, n_z),
        gz=(4, n_z - 1), vc=(1,), vt=(n_t - 1,), vz=(n_z - 1,), en=(2,),
        wt=(n_t - 1,), wc=(n_t - 1,), ta=(2, n_t - 1), tb=(2, n_t - 1), oc=(n_t,), ot=(n_t - 1,),
    ).items():
        sems[name + "_s"] = shape
        sems[name + "_r"] = shape
    sems["out_l"] = (2, 2)
    names = [*ins, *outs, *scratch, *sems]
    return pl.pallas_call(
        functools.partial(layers_kernel, n_z, n_t, rows, width, cols, names),
        out_shape=[jax.ShapeDtypeStruct(shape, dtype) for _, shape, dtype in outs.values()],
        in_specs=list(ins.values()),
        out_specs=[spec for spec, _, _ in outs.values()],
        scratch_shapes=[
            *(pltpu.VMEM(shape, dtype) for shape, dtype in scratch.values()),
            *(sem(shape) for shape in sems.values()),
        ],
        compiler_params=pltpu.CompilerParams(
            collective_id=0, has_side_effects=True, vmem_limit_bytes=VMEM_LIMIT
        ),
        name="layers",
    )(x, g, *small, wa, wo, wu, wd)


def shards(
    inputs, out_grad, items, send_order, recv_order,
    attn_weight, qv_bias, out_weight, out_bias, norm_first,
    up_weight, up_bias, down_weight, down_bias, norm_second,
):
    micros, rows, width = inputs.shape
    n_z = lax.axis_size("dp")
    cols = attn_weight.shape[3]
    heads = cols // HEAD_DIM
    clusters = rows // CLUSTER

    small = (
        items[0], send_order[0], recv_order[0], qv_bias[0], out_bias, norm_first[0], up_bias,
        down_bias, norm_second[0],
    )
    wa = jnp.transpose(attn_weight[0], (1, 2, 0)).reshape(3 * cols, width)
    acts, grads, g_up, g_down, g_attn, g_out, vec, ent = run_layers(
        n_z, inputs, out_grad, small, wa, out_weight[0], up_weight[0], down_weight[0]
    )
    item_numbers = jnp.arange(ITEMS, dtype=jnp.int32)
    grid = items[0].reshape(micros, clusters, CLUSTER)
    occupancy = jnp.sum((grid[..., None] == item_numbers).astype(f32), axis=2)
    results = (
        acts, grads.astype(f32), ent[:, :clusters, :heads], occupancy,
        jnp.transpose(g_attn, (1, 0, 2)),
        jnp.stack([vec[7, :cols], vec[7, 2 * cols : 3 * cols]]), g_out.T,
        vec[5], vec[3:5], g_up, vec[6], g_down.T, vec[2], vec[0:2],
    )
    return tuple(value[None] for value in results)


def solution(mesh):
    return jax.shard_map(
        shards,
        mesh=mesh,
        in_specs=(
            P(None, "dp", None),
            P(None, "dp", None),
            P("section", None, "dp"),
            P("section", None, "dp", None),
            P("section", None, "dp", None),
            P("section", None, None, "tensor"),
            P("section", None, "tensor"),
            P("section", "tensor", None),
            P("section", None),
            P("section", None, None),
            P("section", None, "tensor"),
            P("section", "tensor"),
            P("section", "tensor", None),
            P("section", None),
            P("section", None, None),
        ),
        out_specs=(
            P("section", None, "dp", None),
            P("section", None, "dp", None),
            P("section", None, "dp", "tensor"),
            P("section", None, "dp", None),
            P("section", "dp", None, "tensor"),
            P("section", None, "tensor"),
            P("section", "tensor", "dp"),
            P("section", None),
            P("section", None, None),
            P("section", "dp", "tensor"),
            P("section", "tensor"),
            P("section", "tensor", "dp"),
            P("section", None),
            P("section", None, None),
        ),
        check_vma=False,
    )
```

```python
import functools

import jax
import jax.numpy as jnp
from jax import lax
from jax.experimental import pallas as pl
from jax.experimental.pallas import tpu as pltpu
from jax.sharding import PartitionSpec as P

HEAD_DIM = 64
CLUSTER = 128
ITEMS = 6
EPSILON = 1e-06
MESH = pl.DeviceIdType.MESH
VMEM_LIMIT = 63 * 1024 * 1024
bf16 = jnp.bfloat16
f32 = jnp.float32


def nn(a, b):
    return lax.dot_general(a, b, (((1,), (0,)), ((), ())), preferred_element_type=f32)


def nt(a, b):
    return lax.dot_general(a, b, (((1,), (1,)), ((), ())), preferred_element_type=f32)


def tn(a, b):
    return lax.dot_general(a, b, (((0,), (0,)), ((), ())), preferred_element_type=f32)


def loop(count, body):
    def step(index, carry):
        body(index)
        return carry

    lax.fori_loop(0, count, step, 0)


def rows_at(index, size):
    return pl.ds(pl.multiple_of(index * size, size), size)


class Bag:
    def __init__(self, names, values):
        self.__dict__.update(zip(names, values, strict=True))


def place_rows(row, first, count):
    numbers = lax.broadcasted_iota(jnp.int32, (count, row.shape[1]), 0) + first
    return (numbers == row).astype(bf16)


def by_head(block, heads):
    lane = lax.broadcasted_iota(jnp.int32, block.shape, 1) // HEAD_DIM
    return jnp.concatenate([jnp.where(lane == h, block, jnp.zeros_like(block)) for h in range(heads)])


def fold_heads(stacked, heads):
    count = stacked.shape[0] // heads
    lane = lax.broadcasted_iota(jnp.int32, (count, stacked.shape[1]), 1) // HEAD_DIM
    total = jnp.where(lane == 0, stacked[:count], 0.0)
    for h in range(1, heads):
        total = jnp.where(lane == h, stacked[h * count : (h + 1) * count], total)
    return total


def softmax_parts(scores, same):
    masked = jnp.where(same, scores, -1e30)
    centred = masked - jnp.max(masked, axis=-1, keepdims=True)
    grown = jnp.exp(centred)
    total = jnp.sum(grown, axis=-1, keepdims=True)
    return grown / total, centred, total


def same_item(row):
    wide = jnp.broadcast_to(row.astype(f32), (row.shape[1], row.shape[1]))
    return wide == wide.T


def normalise(values):
    centre = jnp.mean(values, axis=-1, keepdims=True)
    spread = values - centre
    second = jnp.mean(spread * spread, axis=-1, keepdims=True)
    inverse = lax.rsqrt(second + EPSILON)
    return spread * inverse, inverse


def norm_backward(grad, normed, inverse, gain):
    scaled = grad * gain
    first = jnp.mean(scaled, axis=-1, keepdims=True)
    second = jnp.mean(scaled * normed, axis=-1, keepdims=True)
    return inverse * (scaled - first - normed * second)


def column_sum(value):
    return jnp.sum(value.astype(f32), axis=0, keepdims=True)


def remote(src, dst, sems, device):
    return pltpu.make_async_remote_copy(
        src_ref=src, dst_ref=dst, send_sem=sems[0], recv_sem=sems[1],
        device_id=device, device_id_type=MESH,
    )


def layers_kernel(n_z, n_t, rows, width, cols, names, *refs):
    r = Bag(names, refs)
    heads, half_width = cols // HEAD_DIM, width // 2
    scale = HEAD_DIM**-0.5
    core, z, t = lax.axis_index("section"), lax.axis_index("dp"), lax.axis_index("tensor")
    other = {"section": 1 - core}
    step_x, step_y = 1 - 2 * lax.rem(t, 2), 2 - 4 * (t // 2)
    t_x, t_y = t + step_x, t + step_y
    t_far = t + step_x + step_y
    piece, own = rows // n_z, rows // n_t
    chunk_rows = max(piece, 128)
    chunks, per_chunk = rows // chunk_rows, chunk_rows // piece
    mine = rows_at(t, own)
    weights = ("wa", "wo", "wu", "wd")

    def load(i):
        if i < 2:
            return pltpu.make_async_copy(r.x_in.at[core * 2 + i], r.x.at[i], r.load_sem.at[i])
        if i < 4:
            return pltpu.make_async_copy(r.g_in.at[core * 2 + i - 2], r.g.at[i - 2], r.load_sem.at[i])
        if i == 5:
            return pltpu.make_async_copy(r.wo_in, r.wo.at[core, t], r.load_sem.at[i])
        name = weights[i - 4]
        return pltpu.make_async_copy(
            getattr(r, name + "_in"), getattr(r, name).at[core], r.load_sem.at[i]
        )

    def swap(i):
        sems = (r.swap_s.at[i], r.swap_r.at[i])
        if i == 4:
            return remote(r.idx.at[core], r.idx.at[core], sems, other)
        if i == 5:
            return remote(r.par.at[core], r.par.at[core], sems, other)
        if i == 1:
            return remote(r.wo_in, r.wo.at[core, t], sems, other)
        name = weights[i]
        return remote(getattr(r, name + "_in"), getattr(r, name).at[core], sems, other)

    def start():
        for i in (0, 4, 1, 5, 6, 7, 2, 3):
            load(i).start()
        for kind, index in enumerate((r.items_in, r.send_in, r.recv_in)):
            for i in range(4):
                for c in range(rows // 128):
                    cut = slice(c * 128, (c + 1) * 128)
                    row = index[i : i + 1, cut] if kind == 0 else index[i, :, cut]
                    r.idx[core, kind * 4 + i, c] = row
        r.par[core, 0:1, :] = jnp.zeros((1, width), f32)
        r.par[core, 0:1, :cols] = r.qv_in[0:1]
        r.par[core, 0:1, 2 * cols : 3 * cols] = r.qv_in[1:2]
        for first, value in ((1, r.bo_in), (2, r.norm1_in), (4, r.bu_in), (5, r.bd_in), (6, r.norm2_in)):
            r.par[core, first : first + value.shape[0], :] = value[...]
        r.vec[...] = jnp.zeros(r.vec.shape, f32)
        barrier = pltpu.get_barrier_semaphore()
        pl.semaphore_signal(barrier, inc=1, device_id=other, device_id_type=MESH)

        def greet_z(k):
            peer = lax.rem(z + 1 + k, n_z)
            pl.semaphore_signal(barrier, inc=1, device_id={"dp": peer}, device_id_type=MESH)

        def greet_t(k):
            peer = lax.rem(t + 1 + k, n_t)
            pl.semaphore_signal(barrier, inc=1, device_id={"tensor": peer}, device_id_type=MESH)

        loop(n_z - 1, greet_z)
        loop(n_t - 1, greet_t)
        pl.semaphore_wait(barrier, n_z + n_t - 1)
        for i in (4, 5, 0, 1):
            swap(i).start()
        for k in range(1, n_t):
            wo_copy(k).start()
        for i in (2, 3):
            swap(i).start()
        swap(4).wait()
        swap(5).wait()

    def wo_copy(k):
        return remote(
            r.wo_in, r.wo.at[core, t], (r.wt_s.at[k - 1], r.wt_r.at[k - 1]),
            {"tensor": lax.rem(t + k, n_t)},
        )

    def wo_on_copy(k):
        slab = r.wo.at[core, lax.rem(t - k + n_t, n_t)]
        return remote(slab, slab, (r.wc_s.at[k - 1], r.wc_r.at[k - 1]), other)

    def out_weight_on(l, m):
        load(5).wait()
        for k in range(1, n_t):
            wo_copy(k).wait_recv()
            wo_on_copy(k).start()

    asked = set()

    def need_weight(layer, i):
        if (layer, i) in asked:
            return
        asked.add((layer, i))

        if i != 1:

            @pl.when(core == layer)
            def _():
                load(4 + i).wait()

        @pl.when(core != layer)
        def _():
            swap(i).wait_recv()
            if i == 1:
                for k in range(1, n_t):
                    wo_on_copy(k).wait_recv()

    def index_cut(kind, layer, m, first, count):
        cuts = [
            r.idx[layer, kind * 4 + core * 2 + m, first // 128 + i] for i in range(count // 128)
        ]
        return cuts[0] if len(cuts) == 1 else jnp.concatenate(cuts, axis=1)

    def index_row(kind, layer, m):
        return index_cut(kind, layer, m, 0, rows)

    def par(layer, i, count=None):
        return r.par[layer, i : i + 1, : count or width]

    def z_copies(kind, m, k, src, dst, src_rest, dst_rest):
        peer = lax.rem(z + k, n_z)
        full = src.shape[1] // 128 * 128
        lanes = pl.ds(0, full)
        return [
            remote(
                src.at[rows_at(peer, piece), lanes], dst.at[rows_at(z, piece), lanes],
                (r.z_s.at[2 * kind, m, k - 1], r.z_r.at[2 * kind, m, k - 1]), {"dp": peer},
            ),
            remote(
                src_rest.at[peer], dst_rest.at[z],
                (r.z_s.at[2 * kind + 1, m, k - 1], r.z_r.at[2 * kind + 1, m, k - 1]), {"dp": peer},
            ),
        ]

    def z_chunk(kk):
        return lax.rem(z // per_chunk + 1 + kk, chunks)

    def z_send(kind, m, cc, rest, *refs):
        rest = rest.astype(f32)
        for j in range(per_chunk):
            upper = rest[j * piece : j * piece + piece // 2]
            lower = rest[j * piece + piece // 2 : (j + 1) * piece]
            refs[2][cc * per_chunk + j] = jnp.concatenate([upper, lower], axis=1).astype(bf16)

        def one(j):
            peer = cc * per_chunk + j
            k = lax.rem(peer - z + n_z, n_z)

            @pl.when(k > 0)
            def _():
                for copy in z_copies(kind, m, k, *refs):
                    copy.start()

        loop(per_chunk, one)

    def z_take(kind, m, src, dst, src_rest, dst_rest):
        def wait(k):
            for copy in z_copies(kind, m, k + 1, src, dst, src_rest, dst_rest):
                copy.wait()

        loop(n_z - 1, wait)
        full = src.shape[1] // 128 * 128
        here = rows_at(z, piece)
        dst[here, :full] = src[here, :full]
        dst_rest[z] = src_rest[z]

        def unpack(b):
            both = dst_rest[b].astype(f32)
            whole = jnp.concatenate([both[:, :HEAD_DIM], both[:, HEAD_DIM:]], axis=0)
            dst[rows_at(b, piece), full:] = whole.astype(bf16)

        loop(n_z, unpack)

    left, right = slice(0, half_width), slice(half_width, width)

    def sum_copy(m, j):
        peer = t_x if j in (0, 1, 5) else t_y
        return remote(
            r.sum_src.at[m, j], r.sum_dst.at[m, j], (r.sum_s.at[m, j], r.sum_r.at[m, j]),
            {"tensor": peer},
        )

    def sum_put(m, role, part):
        @pl.when(role == 0)
        def _():
            r.sum_own[m] = part

        @pl.when(role == 1)
        def _():
            r.sum_src[m, 1] = part[:, left].astype(bf16)
            r.sum_keep[m, 1] = part[:, right].astype(bf16)
            sum_copy(m, 1).start()

        @pl.when(role == 2)
        def _():
            r.sum_src[m, 3] = part[:, right].astype(bf16)
            r.sum_keep[m, 0] = part[:, left].astype(bf16)
            sum_copy(m, 3).start()

        @pl.when(role == 3)
        def _():
            r.sum_src[m, 0] = part[:, left].astype(bf16)
            sum_copy(m, 0).start()
            r.sum_src[m, 2] = part[:, right].astype(bf16)
            sum_copy(m, 2).start()

    def sum_mid(m):
        sum_copy(m, 0).wait_recv()
        r.sum_src[m, 4] = (r.sum_keep[m, 0].astype(f32) + r.sum_dst[m, 0].astype(f32)).astype(bf16)
        sum_copy(m, 4).start()
        sum_copy(m, 2).wait_recv()
        r.sum_src[m, 5] = (r.sum_keep[m, 1].astype(f32) + r.sum_dst[m, 2].astype(f32)).astype(bf16)
        sum_copy(m, 5).start()

    def sum_take(m):
        for j in (1, 3, 4, 5):
            sum_copy(m, j).wait_recv()
        for j in range(6):
            sum_copy(m, j).wait_send()
        added = jnp.concatenate(
            [
                r.sum_dst[m, 1].astype(f32) + r.sum_dst[m, 4].astype(f32),
                r.sum_dst[m, 3].astype(f32) + r.sum_dst[m, 5].astype(f32),
            ],
            axis=1,
        )
        return r.sum_own[m] + added

    def role_rows(role):
        return rows_at(t + lax.rem(role, 2) * step_x + (role // 2) * step_y, own)

    def gather_copy(kind, m, j, buf):
        first = (t, t, t, t, t_x, t_y)[j] * own
        low = j in (1, 2, 5)
        here = pl.ds(pl.multiple_of(first + (own // 2 if low else 0), own // 2), own // 2)
        return remote(
            buf.at[here], buf.at[here], (r.gather_s.at[kind, m, j], r.gather_r.at[kind, m, j]),
            {"tensor": t_x if j in (0, 1, 5) else t_y},
        )

    def gather_start(kind, m, buf):
        for j in (0, 2, 1, 3):
            gather_copy(kind, m, j, buf).start()

    def gather_on(kind, m, buf):
        gather_copy(kind, m, 0, buf).wait_recv()
        gather_copy(kind, m, 4, buf).start()
        gather_copy(kind, m, 2, buf).wait_recv()
        gather_copy(kind, m, 5, buf).start()

    def gather_near(kind, m, buf, j):
        gather_copy(kind, m, j, buf).wait_recv()

    def gather_far(kind, m, buf):
        gather_copy(kind, m, 4, buf).wait_recv()
        gather_copy(kind, m, 5, buf).wait_recv()

    def gather_rest(kind, m, buf):
        for j in (1, 3, 4, 5):
            gather_copy(kind, m, j, buf).wait_recv()
        gather_sent(kind, m, buf)

    def gather_sent(kind, m, buf):
        for j in range(6):
            gather_copy(kind, m, j, buf).wait_send()

    def gather_step(kind, m, role, buf):
        @pl.when(role == 1)
        def _():
            gather_on(kind, m, buf)
            gather_near(kind, m, buf, 1)

        @pl.when(role == 2)
        def _():
            gather_near(kind, m, buf, 3)

        @pl.when(role == 3)
        def _():
            gather_far(kind, m, buf)

    def out_local(kind, m, src, out):
        return pltpu.make_async_copy(src, out.at[core * 2 + m], r.out_l.at[kind, m])

    def out_away(kind, m, src, out):
        return remote(src, out.at[core * 2 + m], (r.out_s.at[kind, m], r.out_r.at[kind, m]), other)

    def out_start(kind, layer, m, src, out):
        @pl.when(core == layer)
        def _():
            out_local(kind, m, src, out).start()

        @pl.when(core != layer)
        def _():
            out_away(kind, m, src, out).start()

    def out_wait(kind, layer, m, src, out):
        @pl.when(core == layer)
        def _():
            out_local(kind, m, src, out).wait()

        @pl.when(core != layer)
        def _():
            out_away(kind, m, src, out).wait_send()

    rest_z, rest_m = 3 * cols - HEAD_DIM, cols - HEAD_DIM

    def z_big(m):
        return r.zs.at[m], r.zr.at[m], r.zs_rest.at[m], r.zr_rest.at[m]

    def z_home(m):
        return r.dmr.at[m], r.ms.at[m], r.ms_rest.at[m], r.mr_rest.at[m]

    def z_back(m):
        return r.dmt.at[m], r.dmr.at[m], r.ms_rest.at[m], r.mr_rest.at[m]

    def project(l, m):
        need_weight(l, 0)
        if l == 0:
            load(m).wait()

        def chunk(kk):
            cc = z_chunk(kk)
            here = rows_at(cc, chunk_rows)
            numbers = lax.broadcasted_iota(jnp.int32, (rows, chunk_rows), 0)
            pick = (numbers == index_cut(1, l, m, cc * chunk_rows, chunk_rows)).astype(bf16)
            moved = tn(pick, r.x[m]).astype(bf16)
            r.xp[l, m, here] = moved
            block = (nt(moved, r.wa[l]) + par(l, 0, 3 * cols)).astype(bf16)
            r.zs[m, here] = block[:, :rest_z]
            z_send(0, m, cc, block[:, rest_z:], *z_big(m))

        loop(chunks, chunk)

    def attend(l, m):
        z_take(0, m, *z_big(m))
        lane = lax.broadcasted_iota(jnp.int32, (1, 128), 1)

        def cluster(c):
            here = rows_at(c, CLUSTER)
            numbers = lax.broadcasted_iota(jnp.int32, (rows, CLUSTER), 0)
            pick = (numbers == index_cut(2, l, m, c * CLUSTER, CLUSTER)).astype(bf16)
            block = tn(pick, r.zr[m]).astype(bf16)
            r.grouped[l, m, here] = block
            queries, keys, values = (block[:, i * cols : (i + 1) * cols] for i in range(3))
            scores = nt(queries, by_head(keys, heads)) * scale
            same = same_item(index_cut(0, l, m, c * CLUSTER, CLUSTER))
            probs = []
            log_row = jnp.zeros((1, 128), f32)
            for h in range(heads):
                cut = slice(h * CLUSTER, (h + 1) * CLUSTER)
                prob, centred, total = softmax_parts(scores[:, cut], same)
                inner = jnp.sum(jnp.where(same, prob * centred, 0.0), axis=-1, keepdims=True)
                entropy = jnp.mean(jnp.log(total) - inner, axis=0, keepdims=True)
                log_row = jnp.where(lane == h, entropy, log_row)
                probs.append(prob.astype(bf16))
            r.entropy[l, m, pl.ds(c, 1)] = log_row
            mixed = nn(jnp.concatenate(probs, axis=1), by_head(values, heads))
            r.dmt[m, here] = mixed.astype(bf16)

        loop(rows // CLUSTER, cluster)

        def home(kk):
            cc = z_chunk(kk)
            here = rows_at(cc, chunk_rows)
            one_hot = place_rows(index_row(2, l, m), cc * chunk_rows, chunk_rows)
            block = nn(one_hot, r.dmt[m]).astype(bf16)
            r.dmr[m, here] = block
            z_send(1, m, cc, block[:, rest_m:], *z_home(m))

        loop(chunks, home)

    def heads_copy(l, m, k):
        peer = lax.rem(t + k, n_t)
        return remote(
            r.ms.at[m, rows_at(peer, own)], r.mt.at[l, m, t],
            (r.ta_s.at[m, k - 1], r.ta_r.at[m, k - 1]), {"tensor": peer},
        )

    def out_project(l, m):
        z_take(1, m, *z_home(m))
        for k in (2, 1, 3):
            heads_copy(l, m, k).start()
        r.mt[l, m, t] = r.ms[m, mine]

    def middle(l, m):
        sum_mid(m)

    def first_norm(l, m):
        need_weight(l, 1)
        for k in range(1, n_t):
            heads_copy(l, m, k).wait()
        total = r.xp[l, m, mine].astype(f32) + par(l, 1)
        for s in range(n_t):
            total = total + nn(r.mt[l, m, s], r.wo[l, s])
        normed, inverse = normalise(total)
        hidden = normed * par(l, 2) + par(l, 3)
        r.n1[l, m] = normed.astype(bf16)
        r.inv1[l, m] = jnp.broadcast_to(inverse, (own, 128))
        r.hid[m] = hidden
        r.hfull[l, m, mine] = hidden.astype(bf16)
        gather_start(0, m, r.hfull.at[l, m])

    def feed(l, m):
        need_weight(l, 2)
        need_weight(l, 3)

        def part(role):
            gather_step(0, m, role, r.hfull.at[l, m])
            here = role_rows(role)
            up = nn(r.hfull[l, m, here], r.wu[l]) + par(l, 4)
            square = up * up
            tanh = jnp.tanh(0.7978845608028654 * up * (1.0 + 0.044715 * square))
            half = 0.5 * (1.0 + tanh)
            slope = 0.7978845608028654 * (1.0 + 3 * 0.044715 * square)
            r.gp[l, m, here] = (half + 0.5 * up * (1.0 - tanh * tanh) * slope).astype(bf16)
            active = (up * half).astype(bf16)
            r.act[l, m, here] = active
            sum_put(m, role, nn(active, r.wd[l]))

        loop(n_t, part)

    def second_norm(l, m):
        gather_sent(0, m, r.hfull.at[l, m])
        total = sum_take(m) + par(l, 5)
        normed, inverse = normalise(r.hid[m] + total)
        r.n2[l, m] = normed.astype(bf16)
        r.inv2[l, m] = jnp.broadcast_to(inverse, (own, 128))
        r.ag[m, mine] = (normed * par(l, 6) + par(l, 7)).astype(bf16)
        gather_start(1, m, r.ag.at[m])

    def out_on(l, m):
        gather_on(1, m, r.ag.at[m])

    def to_tokens(l, m, dst, buf):
        def chunk(cc):
            one_hot = place_rows(index_row(1, l, m), cc * 128, 128)
            dst[m, rows_at(cc, 128)] = nn(one_hot, buf[m]).astype(bf16)

        loop(rows // 128, chunk)

    def out_tokens(l, m):
        gather_rest(1, m, r.ag.at[m])
        if l == 1:
            out_wait(0, 0, m, r.x.at[m], r.acts)
        to_tokens(l, m, r.x, r.ag)
        out_start(0, l, m, r.x.at[m], r.acts)

    def add_vec(l, index, value):
        r.vec[l, index : index + 1, : value.shape[1]] += value

    def b_second_norm(l, m):
        if l == 1:
            load(2 + m).wait()
        numbers = lax.broadcasted_iota(jnp.int32, (rows, own), 0)
        pick = (numbers == index_cut(1, l, m, t * own, own)).astype(bf16)
        up = tn(pick, r.g[m])
        normed = r.n2[l, m].astype(f32)
        down = norm_backward(up, normed, r.inv2[l, m][:, :1], par(l, 6))
        r.hid[m] = down
        low = down.astype(bf16)
        r.db[m, mine] = low
        gather_start(2, m, r.db.at[m])
        add_vec(l, 0, column_sum(up * normed))
        add_vec(l, 1, column_sum(up))
        add_vec(l, 2, column_sum(low))

    def b_feed(l, m):
        def part(role):
            gather_step(2, m, role, r.db.at[m])
            here = role_rows(role)
            low = (nt(r.db[m, here], r.wd[l]) * r.gp[l, m, here].astype(f32)).astype(bf16)
            r.gp[l, m, here] = low
            sum_put(m, role, nt(low, r.wu[l]))

        loop(n_t, part)

    def grad_slabs(ref, value, lanes):
        ref[:, :, lanes] = value.reshape(n_z, width // n_z, value.shape[1]).astype(bf16)

    def feed_weights(l, m):
        for i in range(2):
            gather_sent(2, i, r.db.at[i])
            add_vec(l, 6, column_sum(r.gp[l, i]))

        def block(c):
            cut = rows_at(c, 256)
            up = tn(r.hfull[l, 0], r.gp[l, 0, :, cut]) + tn(r.hfull[l, 1], r.gp[l, 1, :, cut])
            grad_slabs(r.gs_feed, up, cut)
            down = tn(r.db[0], r.act[l, 0, :, cut]) + tn(r.db[1], r.act[l, 1, :, cut])
            grad_slabs(r.gs_feed, down, pl.ds(pl.multiple_of(width + c * 256, 256), 256))

        loop(width // 256, block)
        grads_send(0, l, r.gs_feed, r.gr_feed)

    def b_first_norm(l, m):
        up = r.hid[m] + sum_take(m)
        normed = r.n1[l, m].astype(f32)
        down = norm_backward(up, normed, r.inv1[l, m][:, :1], par(l, 2))
        r.dres[m] = down
        low = down.astype(bf16)
        r.da[m] = low

        def part(kk):
            k = lax.rem(kk + 1, n_t)
            peer = lax.rem(t + k, n_t)
            block = nt(low, r.wo[l, peer]).astype(bf16)

            @pl.when(k > 0)
            def _():
                r.ms[m, rows_at(peer, own)] = block
                rows_copy(m, k).start()

            @pl.when(k == 0)
            def _():
                r.dmt[m, mine] = block

        loop(n_t, part)
        add_vec(l, 3, column_sum(up * normed))
        add_vec(l, 4, column_sum(up))
        add_vec(l, 5, column_sum(low))

    def rows_copy(m, k):
        peer = lax.rem(t + k, n_t)
        return remote(
            r.ms.at[m, rows_at(peer, own)], r.dmt.at[m, mine], (r.tb_s.at[m, k - 1], r.tb_r.at[m, k - 1]),
            {"tensor": peer},
        )

    def out_back(l, m):
        for k in range(1, n_t):
            rows_copy(m, k).wait()

        def chunk(kk):
            cc = z_chunk(kk)
            z_send(2, m, cc, r.dmt[m, rows_at(cc, chunk_rows), rest_m:], *z_back(m))

        loop(chunks, chunk)

    def out_weights(l, m):
        for s in range(n_t):
            value = tn(r.da[0], r.mt[l, 0, s]) + tn(r.da[1], r.mt[l, 1, s])
            r.gs_out[s] = value.reshape(n_z, width // n_z, cols).astype(bf16)

        @pl.when(core != l)
        def _():
            for k in range(n_t):
                out_core_copy(lax.rem(t + 1 + k, n_t)).start()

    def b_attend(l, m):
        z_take(2, m, *z_back(m))

        def cluster(c):
            here = rows_at(c, CLUSTER)
            numbers = lax.broadcasted_iota(jnp.int32, (rows, CLUSTER), 0)
            pick = (numbers == index_cut(2, l, m, c * CLUSTER, CLUSTER)).astype(bf16)
            dmix = tn(pick, r.dmr[m]).astype(bf16)
            block = r.grouped[l, m, here]
            queries, keys, values = (block[:, i * cols : (i + 1) * cols] for i in range(3))
            keys_by_head = by_head(keys, heads)
            scores = nt(queries, keys_by_head) * scale
            same = same_item(index_cut(0, l, m, c * CLUSTER, CLUSTER))
            dprob = nt(dmix, by_head(values, heads))
            probs, dscores = [], []
            for h in range(heads):
                cut = slice(h * CLUSTER, (h + 1) * CLUSTER)
                prob = softmax_parts(scores[:, cut], same)[0]
                outer = prob * dprob[:, cut]
                dscore = outer - prob * jnp.sum(outer, axis=-1, keepdims=True)
                probs.append(prob.astype(bf16))
                dscores.append(dscore.astype(bf16))
            prob_all = jnp.concatenate(probs, axis=1)
            dscore_all = jnp.concatenate(dscores, axis=1)
            dqueries = nn(dscore_all, keys_by_head) * scale
            dkeys = fold_heads(tn(dscore_all, queries), heads) * scale
            dvalues = fold_heads(tn(prob_all, dmix), heads)
            r.grouped[l, m, here] = jnp.concatenate([dqueries, dkeys, dvalues], axis=1).astype(bf16)

        loop(rows // CLUSTER, cluster)

        def home(kk):
            cc = z_chunk(kk)
            here = rows_at(cc, chunk_rows)
            one_hot = place_rows(index_row(2, l, m), cc * chunk_rows, chunk_rows)
            block = nn(one_hot, r.grouped[l, m]).astype(bf16)
            r.zs[m, here] = block[:, :rest_z]
            z_send(3, m, cc, block[:, rest_z:], *z_big(m))

        loop(chunks, home)

    def in_project(l, m):
        z_take(3, m, *z_big(m))

        def part(kk):
            role = 3 - kk
            sum_put(m, role, nn(r.zr[m, role_rows(role)], r.wa[l]))

        loop(n_t, part)

    def in_weights(l, m):
        for i in range(2):
            add_vec(l, 7, column_sum(r.zr[i]))
        for first in range(0, 3 * cols, 256):
            cut = slice(first, min(first + 256, 3 * cols))
            value = tn(r.xp[l, 0], r.zr[0, :, cut]) + tn(r.xp[l, 1], r.zr[1, :, cut])
            grad_slabs(r.gs_attn, value, cut)
        grads_send(1, l, r.gs_attn, r.gr_attn)

    def layer_input(l, m):
        r.ag[m, mine] = (r.dres[m] + sum_take(m)).astype(bf16)
        gather_start(4, m, r.ag.at[m])

    def b_out_on(l, m):
        gather_on(4, m, r.ag.at[m])

    def b_tokens(l, m):
        gather_rest(4, m, r.ag.at[m])
        if l == 0:
            out_wait(1, 1, m, r.g.at[m], r.grads)
        to_tokens(l, m, r.g, r.ag)
        out_start(1, l, m, r.g.at[m], r.grads)

    def grad_core_copy(kind, k, src, dst):
        return remote(src.at[k], dst.at[k], (r.gc_s.at[kind, k], r.gc_r.at[kind, k]), other)

    def grad_z_copy(kind, k, src, dst, lanes=slice(None)):
        peer = lax.rem(z + k, n_z)
        return remote(
            src.at[peer, :, lanes], dst.at[k - 1, :, lanes], (r.gz_s.at[kind, k - 1], r.gz_r.at[kind, k - 1]),
            {"dp": peer},
        )

    def grads_send(kind, l, src, dst):
        @pl.when(core != l)
        def _():
            loop(n_z, lambda k: grad_core_copy(kind, lax.rem(z + 1 + k, n_z), src, dst).start())

    def grads_add(kind, src, came, k, wait, lanes):
        peer = lax.rem(z + k, n_z)
        if wait:
            grad_core_copy(kind, peer, src, came).wait_recv()
        total = src[peer, :, lanes].astype(f32) + came[peer, :, lanes].astype(f32)
        src[peer, :, lanes] = total.astype(bf16)

    def grads_part(kind, sem, l, src, came, dst, part, wait, lanes):
        @pl.when(core == l)
        def _():
            first, last = part * (n_z - 1) // 3, (part + 1) * (n_z - 1) // 3

            def one(i):
                grads_add(kind, src, came, first + 1 + i, wait, lanes)
                grad_z_copy(sem, first + 1 + i, src, dst, lanes).start()

            loop(last - first, one)

    def grads_end(kind, sems, l, src, came, dst, outs):
        @pl.when(core == l)
        def _():
            lanes = src.shape[2] // len(sems)
            for i in range(len(sems)):
                grads_add(kind, src, came, 0, i == 0, slice(i * lanes, (i + 1) * lanes))
            cuts, first = [], 0
            for out in outs:
                cuts.append(slice(first, first + out.shape[-1]))
                first += out.shape[-1]
            for out, cut in zip(outs, cuts):
                out[...] = src[z, :, cut].astype(f32)

            def one(k):
                for i, sem in enumerate(sems):
                    grad_z_copy(sem, k + 1, src, dst, slice(i * lanes, (i + 1) * lanes)).wait()
                for out, cut in zip(outs, cuts):
                    out[...] += dst[k, :, cut].astype(f32)

            loop(n_z - 1, one)

        @pl.when(core != l)
        def _():
            loop(n_z, lambda k: grad_core_copy(kind, k, src, came).wait_send())

    def line_copy(half, c, slot, step):
        lanes = slice(half * width, (half + 1) * width)
        return remote(
            r.gs_feed.at[c, :, lanes], r.gz_feed.at[slot, :, lanes],
            (r.line_s.at[half, c], r.line_r.at[half, slot]), {"dp": z + step},
        )

    def line_add(half, c, slot, came):
        lanes = slice(half * width, (half + 1) * width)
        grads_add(0, r.gs_feed, r.gr_feed, c - z, half == 0, lanes)

        @pl.when(came)
        def _():
            line_copy(half, c, slot, 0).wait_recv()
            total = r.gs_feed[c, :, lanes].astype(f32) + r.gz_feed[slot, :, lanes].astype(f32)
            r.gs_feed[c, :, lanes] = total.astype(bf16)

    def line_part(half, part, l):
        @pl.when(core == l)
        def _():
            first, last = part * (n_z - 1) // 3, (part + 1) * (n_z - 1) // 3

            def one(i):
                far = n_z - 1 - first - i

                @pl.when(z + far < n_z)
                def _():
                    line_add(half, z + far, z + far, z > 0)
                    line_copy(half, z + far, z + far, 1).start()

                @pl.when(z - far >= 0)
                def _():
                    line_add(half, z - far, z - far, z < n_z - 1)
                    slot = jnp.where(far == 1, n_z, z - far)
                    line_copy(half, z - far, slot, -1).start()

            loop(last - first, one)

    def line_end(l):
        @pl.when(core == l)
        def _():
            for half, out in enumerate((r.g_up, r.g_down)):
                lanes = slice(half * width, (half + 1) * width)
                line_add(half, z, z, z > 0)
                out[...] = r.gs_feed[z, :, lanes].astype(f32)

                @pl.when(z < n_z - 1)
                def _():
                    line_copy(half, z, n_z, 0).wait_recv()
                    out[...] += r.gz_feed[n_z, :, lanes].astype(f32)

                def sent(k):
                    line_copy(half, lax.rem(z + 1 + k, n_z), 0, 0).wait_send()

                loop(n_z - 1, sent)

        @pl.when(core != l)
        def _():
            loop(n_z, lambda k: grad_core_copy(0, k, r.gs_feed, r.gr_feed).wait_send())

    def feed_part(i):
        return lambda l, m: line_part(i % 2, i // 2, l)

    def attn_part(i):
        return lambda l, m: grads_part(
            1, 2, l, r.gs_attn, r.gr_attn, r.gz_attn, i, True, slice(None)
        )

    feed_0, feed_1, feed_2, feed_3, feed_4, feed_5 = (feed_part(i) for i in range(6))
    attn_0, attn_1, attn_2 = (attn_part(i) for i in range(3))

    def feed_end(l, m):
        line_end(l)

    def attn_end(l, m):
        grads_end(1, (2,), l, r.gs_attn, r.gr_attn, r.gz_attn, tuple(r.g_attn.at[i] for i in range(3)))

    def out_core_copy(s):
        return remote(r.gs_out.at[s], r.gr_out.at[s], (r.oc_s.at[s], r.oc_r.at[s]), other)

    def out_t_copy(k):
        peer = lax.rem(t + k, n_t)
        return remote(
            r.gs_out.at[peer], r.gt_out.at[k - 1], (r.ot_s.at[k - 1], r.ot_r.at[k - 1]),
            {"tensor": peer},
        )

    def out_z_copy(k):
        peer = lax.rem(z + k, n_z)
        return remote(
            r.gs_out.at[t, peer], r.gz_out.at[k - 1], (r.gz_s.at[3, k - 1], r.gz_r.at[3, k - 1]),
            {"dp": peer},
        )

    def out_sum_t(l, m):
        @pl.when(core == l)
        def _():
            for kk in range(n_t):
                k = (kk + 1) % n_t
                s = lax.rem(t + k, n_t)
                out_core_copy(s).wait_recv()
                r.gs_out[s] = (r.gs_out[s].astype(f32) + r.gr_out[s].astype(f32)).astype(bf16)
                if k > 0:
                    out_t_copy(k).start()

    def out_sum_z(l, m):
        @pl.when(core == l)
        def _():
            for k in range(1, n_t):
                out_t_copy(k).wait()
            total = r.gs_out[t].astype(f32)
            for k in range(1, n_t):
                total = total + r.gt_out[k - 1].astype(f32)
            r.gs_out[t] = total.astype(bf16)
            loop(n_z - 1, lambda k: out_z_copy(k + 1).start())

        @pl.when(core != l)
        def _():
            for s in range(n_t):
                out_core_copy(s).wait_send()

    def out_end(l, m):
        @pl.when(core == l)
        def _():
            r.g_out[...] = r.gs_out[t, z].astype(f32)

            def one(k):
                out_z_copy(k + 1).wait()
                r.g_out[...] += r.gz_out[k].astype(f32)

            loop(n_z - 1, one)

    def vec_copy(l):
        return remote(r.vec.at[l], r.vec_came, (r.vc_s.at[0], r.vc_r.at[0]), other)

    def vec_t_copy(k):
        return remote(
            r.vec_t.at[t], r.vec_t.at[t], (r.vt_s.at[k - 1], r.vt_r.at[k - 1]),
            {"tensor": lax.rem(t + k, n_t)},
        )

    def vec_z_copy(k):
        return remote(
            r.vec_z.at[z], r.vec_z.at[z], (r.vz_s.at[k - 1], r.vz_r.at[k - 1]),
            {"dp": lax.rem(z + k, n_z)},
        )

    def entropy_copy(l, m):
        return remote(
            r.entropy.at[l, m], r.ent.at[core * 2 + m], (r.en_s.at[m], r.en_r.at[m]), other
        )

    def vec_start(l, m):
        @pl.when(core != l)
        def _():
            vec_copy(l).start()
            for i in range(2):
                entropy_copy(l, i).start()

    def vec_sum_t(l, m):
        @pl.when(core == l)
        def _():
            for i in range(2):
                r.ent[core * 2 + i] = r.entropy[l, i]
            vec_copy(l).wait_recv()
            r.vec_t[t] = r.vec[l] + r.vec_came[...]
            for k in range(1, n_t):
                vec_t_copy(k).start()

    def vec_sum_z(l, m):
        @pl.when(core == l)
        def _():
            for k in range(1, n_t):
                vec_t_copy(k).wait()
            total = r.vec_t[0]
            for k in range(1, n_t):
                total = total + r.vec_t[k]
            lane_rows = lax.broadcasted_iota(jnp.int32, total.shape, 0)
            r.vec_z[z] = jnp.where(lane_rows < 6, total, r.vec_t[t])
            loop(n_z - 1, lambda k: vec_z_copy(k + 1).start())

    def vec_end(l, m):
        @pl.when(core == l)
        def _():
            loop(n_z - 1, lambda k: vec_z_copy(k + 1).wait())
            r.vec_out[...] = r.vec_z[0]

            def one(k):
                r.vec_out[...] += r.vec_z[k + 1]

            loop(n_z - 1, one)

        @pl.when(core != l)
        def _():
            vec_copy(l).wait_send()
            for i in range(2):
                entropy_copy(l, i).wait_send()

    def finish():
        for m in range(2):
            out_wait(0, 1, m, r.x.at[m], r.acts)
            out_wait(1, 0, m, r.g.at[m], r.grads)
            for kind, out, src in ((0, r.acts, r.x), (1, r.grads, r.g)):
                out_away(kind, m, src.at[m], out).wait_recv()
            entropy_copy(0, m).wait_recv()
        for i in range(4):
            swap(i).wait_send()
        for k in range(1, n_t):
            wo_copy(k).wait_send()
            wo_on_copy(k).wait_send()

    schedule = (
        (project, 0, 1), (attend, 0, 1), (out_weight_on, 0, 0), (out_project, 0, 1), (project, 0, 0),
        (first_norm, 0, 1), (feed, 0, 1), (attend, 0, 0), (middle, 0, 1), (out_project, 0, 0),
        (second_norm, 0, 1), (out_on, 0, 1), (first_norm, 0, 0), (out_tokens, 0, 1), (project, 1, 1),
        (feed, 0, 0), (middle, 0, 0), (attend, 1, 1), (second_norm, 0, 0), (out_project, 1, 1),
        (out_on, 0, 0), (first_norm, 1, 1), (out_tokens, 0, 0), (project, 1, 0), (feed, 1, 1), (middle, 1, 1),
        (attend, 1, 0), (second_norm, 1, 1), (b_second_norm, 1, 1), (out_on, 1, 1), (out_project, 1, 0),
        (b_feed, 1, 1), (first_norm, 1, 0), (out_tokens, 1, 1), (middle, 1, 1), (feed, 1, 0),
        (b_first_norm, 1, 1), (middle, 1, 0), (out_back, 1, 1), (second_norm, 1, 0), (b_second_norm, 1, 0),
        (b_attend, 1, 1), (out_on, 1, 0), (b_feed, 1, 0), (in_project, 1, 1), (feed_weights, 1, 1),
        (middle, 1, 0), (middle, 1, 1), (b_first_norm, 1, 0), (out_weights, 1, 1), (layer_input, 1, 1),
        (out_back, 1, 0), (b_out_on, 1, 1), (b_tokens, 1, 1), (b_second_norm, 0, 1), (feed_0, 1, 1),
        (feed_1, 1, 1), (b_attend, 1, 0), (b_feed, 0, 1), (out_sum_t, 1, 1), (out_tokens, 1, 0),
        (feed_2, 1, 1), (in_project, 1, 0), (middle, 0, 1), (middle, 1, 0), (in_weights, 1, 1),
        (feed_3, 1, 1), (feed_4, 1, 1), (b_first_norm, 0, 1), (layer_input, 1, 0), (out_sum_z, 1, 1),
        (out_back, 0, 1), (b_out_on, 1, 0), (vec_start, 1, 1), (feed_5, 1, 1), (attn_0, 1, 1),
        (out_end, 1, 1), (b_tokens, 1, 0), (b_second_norm, 0, 0), (b_attend, 0, 1), (vec_sum_t, 1, 1),
        (feed_end, 1, 1), (b_feed, 0, 0), (attn_1, 1, 1), (feed_weights, 0, 1), (feed_0, 0, 1),
        (middle, 0, 0), (vec_sum_z, 1, 1), (feed_1, 0, 1), (in_project, 0, 1), (attn_2, 1, 1),
        (b_first_norm, 0, 0), (out_weights, 0, 1), (feed_2, 0, 1), (middle, 0, 1), (vec_end, 1, 1),
        (out_sum_t, 0, 1), (out_back, 0, 0), (feed_3, 0, 1), (b_attend, 0, 0), (layer_input, 0, 1),
        (feed_4, 0, 1), (out_sum_z, 0, 1), (attn_end, 1, 1), (in_project, 0, 0), (in_weights, 0, 1),
        (b_out_on, 0, 1), (vec_start, 0, 1), (attn_0, 0, 1), (attn_1, 0, 1), (vec_sum_t, 0, 1),
        (middle, 0, 0), (vec_sum_z, 0, 1), (out_end, 0, 1), (layer_input, 0, 0), (attn_2, 0, 1),
        (b_tokens, 0, 1), (feed_5, 0, 1), (vec_end, 0, 1), (b_out_on, 0, 0), (attn_end, 0, 1),
        (b_tokens, 0, 0), (feed_end, 0, 1),
    )
    start()
    for step, layer, micro in schedule:
        step(layer, micro)
    finish()


def run_layers(n_z, x, g, small, wa, wo, wu, wd):
    micros, rows, width = x.shape
    cols, hidden = wo.shape[0], wu.shape[1]
    n_t = lax.axis_size("tensor")
    own, slab = rows // n_t, width // n_z
    pair = (2, rows)
    both = (2, 2, rows)
    anywhere, vmem = pl.BlockSpec(memory_space=pl.ANY), pl.BlockSpec(memory_space=pltpu.VMEM)
    ins = dict(
        x_in=anywhere, g_in=anywhere, items_in=vmem, send_in=vmem, recv_in=vmem, qv_in=vmem,
        bo_in=vmem, norm1_in=vmem, bu_in=vmem, bd_in=vmem, norm2_in=vmem, wa_in=anywhere, wo_in=anywhere,
        wu_in=anywhere, wd_in=anywhere,
    )
    outs = dict(
        acts=(anywhere, x.shape, bf16), grads=(anywhere, x.shape, bf16),
        g_up=(vmem, (slab, width), f32), g_down=(vmem, (slab, width), f32),
        g_attn=(vmem, (3, slab, cols), f32),
        g_out=(vmem, (slab, cols), f32),
        vec_out=(vmem, (8, width), f32), ent=(vmem, (micros, max(8, rows // CLUSTER), 128), f32),
    )
    sem = pltpu.SemaphoreType.DMA
    scratch = dict(
        x=((*pair, width), bf16), g=((*pair, width), bf16),
        wa=((2, 3 * cols, width), bf16), wo=((2, n_t, cols, width), bf16),
        wu=((2, width, hidden), bf16), wd=((2, hidden, width), bf16),
        idx=((2, 12, rows // 128, 1, 128), jnp.int32), par=((2, 8, width), f32),
        xp=((*both, width), bf16), grouped=((*both, 3 * cols), bf16), ms=((*pair, cols), bf16),
        mt=((2, 2, n_t, own, cols), bf16),
        n1=((2, 2, own, width), bf16), inv1=((2, 2, own, 128), f32), hfull=((*both, width), bf16),
        act=((*both, hidden), bf16), gp=((*both, hidden), bf16),
        n2=((2, 2, own, width), bf16), inv2=((2, 2, own, 128), f32),
        entropy=((2, 2, max(8, rows // CLUSTER), 128), f32),
        zs=((*pair, 3 * cols - HEAD_DIM), bf16), zs_rest=((2, n_z, rows // n_z // 2, 128), bf16),
        zr_rest=((2, n_z, rows // n_z // 2, 128), bf16), ms_rest=((2, n_z, rows // n_z // 2, 128), bf16),
        mr_rest=((2, n_z, rows // n_z // 2, 128), bf16), zr=((*pair, 3 * cols), bf16),
        dmr=((*pair, cols), bf16),
        sum_src=((2, 6, own, width // 2), bf16), sum_dst=((2, 6, own, width // 2), bf16),
        sum_keep=((2, 2, own, width // 2), bf16), sum_own=((2, own, width), f32),
        hid=((2, own, width), f32), dres=((2, own, width), f32),
        ag=((*pair, width), bf16), db=((*pair, width), bf16), da=((2, own, width), bf16),
        dmt=((*pair, cols), bf16),
        gs_feed=((n_z, slab, 2 * width), bf16), gr_feed=((n_z, slab, 2 * width), bf16),
        gz_feed=((n_z + 1, slab, 2 * width), bf16),
        gs_attn=((n_z, slab, 3 * cols), bf16), gr_attn=((n_z, slab, 3 * cols), bf16),
        gz_attn=((n_z - 1, slab, 3 * cols), bf16),
        gs_out=((n_t, n_z, slab, cols), bf16), gr_out=((n_t, n_z, slab, cols), bf16),
        gt_out=((n_t - 1, n_z, slab, cols), bf16), gz_out=((n_z - 1, slab, cols), bf16),
        vec=((2, 8, width), f32), vec_came=((8, width), f32), vec_t=((n_t, 8, width), f32),
        vec_z=((n_z, 8, width), f32),
    )
    sems = dict(load_sem=(8,))
    for name, shape in dict(
        swap=(6,), z=(8, 2, n_z - 1), sum=(2, 6), gather=(5, 2, 6), out=(2, 2), gc=(2, n_z),
        gz=(4, n_z - 1), line=(2, n_z + 1), vc=(1,), vt=(n_t - 1,), vz=(n_z - 1,), en=(2,),
        wt=(n_t - 1,), wc=(n_t - 1,), ta=(2, n_t - 1), tb=(2, n_t - 1), oc=(n_t,), ot=(n_t - 1,),
    ).items():
        sems[name + "_s"] = shape
        sems[name + "_r"] = shape
    sems["out_l"] = (2, 2)
    names = [*ins, *outs, *scratch, *sems]
    return pl.pallas_call(
        functools.partial(layers_kernel, n_z, n_t, rows, width, cols, names),
        out_shape=[jax.ShapeDtypeStruct(shape, dtype) for _, shape, dtype in outs.values()],
        in_specs=list(ins.values()),
        out_specs=[spec for spec, _, _ in outs.values()],
        scratch_shapes=[
            *(pltpu.VMEM(shape, dtype) for shape, dtype in scratch.values()),
            *(sem(shape) for shape in sems.values()),
        ],
        compiler_params=pltpu.CompilerParams(
            collective_id=0, has_side_effects=True, vmem_limit_bytes=VMEM_LIMIT
        ),
        name="layers",
    )(x, g, *small, wa, wo, wu, wd)


def shards(
    inputs, out_grad, items, send_order, recv_order,
    attn_weight, qv_bias, out_weight, out_bias, norm_first,
    up_weight, up_bias, down_weight, down_bias, norm_second,
):
    micros, rows, width = inputs.shape
    n_z = lax.axis_size("dp")
    cols = attn_weight.shape[3]
    heads = cols // HEAD_DIM
    clusters = rows // CLUSTER

    small = (
        items[0], send_order[0], recv_order[0], qv_bias[0], out_bias, norm_first[0], up_bias,
        down_bias, norm_second[0],
    )
    wa = jnp.transpose(attn_weight[0], (1, 2, 0)).reshape(3 * cols, width)
    acts, grads, g_up, g_down, g_attn, g_out, vec, ent = run_layers(
        n_z, inputs, out_grad, small, wa, out_weight[0], up_weight[0], down_weight[0]
    )
    item_numbers = jnp.arange(ITEMS, dtype=jnp.int32)
    grid = items[0].reshape(micros, clusters, CLUSTER)
    occupancy = jnp.sum((grid[..., None] == item_numbers).astype(f32), axis=2)
    results = (
        acts, grads.astype(f32), ent[:, :clusters, :heads], occupancy,
        jnp.transpose(g_attn, (1, 0, 2)),
        jnp.stack([vec[7, :cols], vec[7, 2 * cols : 3 * cols]]), g_out.T,
        vec[5], vec[3:5], g_up, vec[6], g_down.T, vec[2], vec[0:2],
    )
    return tuple(value[None] for value in results)


def solution(mesh):
    return jax.shard_map(
        shards,
        mesh=mesh,
        in_specs=(
            P(None, "dp", None),
            P(None, "dp", None),
            P("section", None, "dp"),
            P("section", None, "dp", None),
            P("section", None, "dp", None),
            P("section", None, None, "tensor"),
            P("section", None, "tensor"),
            P("section", "tensor", None),
            P("section", None),
            P("section", None, None),
            P("section", None, "tensor"),
            P("section", "tensor"),
            P("section", "tensor", None),
            P("section", None),
            P("section", None, None),
        ),
        out_specs=(
            P("section", None, "dp", None),
            P("section", None, "dp", None),
            P("section", None, "dp", "tensor"),
            P("section", None, "dp", None),
            P("section", "dp", None, "tensor"),
            P("section", None, "tensor"),
            P("section", "tensor", "dp"),
            P("section", None),
            P("section", None, None),
            P("section", "dp", "tensor"),
            P("section", "tensor"),
            P("section", "tensor", "dp"),
            P("section", None),
            P("section", None, None),
        ),
        check_vma=False,
    )
```

```python
import functools

import jax
import jax.numpy as jnp
from jax import lax
from jax.experimental import pallas as pl
from jax.experimental.pallas import tpu as pltpu
from jax.sharding import PartitionSpec as P

HEAD_DIM = 64
CLUSTER = 128
ITEMS = 6
EPSILON = 1e-06
MESH = pl.DeviceIdType.MESH
VMEM_LIMIT = 63 * 1024 * 1024
bf16 = jnp.bfloat16
f32 = jnp.float32


def nn(a, b):
    return lax.dot_general(a, b, (((1,), (0,)), ((), ())), preferred_element_type=f32)


def nt(a, b):
    return lax.dot_general(a, b, (((1,), (1,)), ((), ())), preferred_element_type=f32)


def tn(a, b):
    return lax.dot_general(a, b, (((0,), (0,)), ((), ())), preferred_element_type=f32)


def loop(count, body):
    def step(index, carry):
        body(index)
        return carry

    lax.fori_loop(0, count, step, 0)


def rows_at(index, size):
    return pl.ds(pl.multiple_of(index * size, size), size)


class Bag:
    def __init__(self, names, values):
        self.__dict__.update(zip(names, values, strict=True))


def place_rows(row, first, count):
    numbers = lax.broadcasted_iota(jnp.int32, (count, row.shape[1]), 0) + first
    return (numbers == row).astype(bf16)


def by_head(block, heads):
    lane = lax.broadcasted_iota(jnp.int32, block.shape, 1) // HEAD_DIM
    return jnp.concatenate([jnp.where(lane == h, block, jnp.zeros_like(block)) for h in range(heads)])


def fold_heads(stacked, heads):
    count = stacked.shape[0] // heads
    lane = lax.broadcasted_iota(jnp.int32, (count, stacked.shape[1]), 1) // HEAD_DIM
    total = jnp.where(lane == 0, stacked[:count], 0.0)
    for h in range(1, heads):
        total = jnp.where(lane == h, stacked[h * count : (h + 1) * count], total)
    return total


def softmax_parts(scores, same):
    masked = jnp.where(same, scores, -1e30)
    centred = masked - jnp.max(masked, axis=-1, keepdims=True)
    grown = jnp.exp(centred)
    total = jnp.sum(grown, axis=-1, keepdims=True)
    return grown / total, centred, total


def same_item(row):
    wide = jnp.broadcast_to(row.astype(f32), (row.shape[1], row.shape[1]))
    return wide == wide.T


def normalise(values):
    centre = jnp.mean(values, axis=-1, keepdims=True)
    spread = values - centre
    second = jnp.mean(spread * spread, axis=-1, keepdims=True)
    inverse = lax.rsqrt(second + EPSILON)
    return spread * inverse, inverse


def norm_backward(grad, normed, inverse, gain):
    scaled = grad * gain
    first = jnp.mean(scaled, axis=-1, keepdims=True)
    second = jnp.mean(scaled * normed, axis=-1, keepdims=True)
    return inverse * (scaled - first - normed * second)


def column_sum(value):
    return jnp.sum(value.astype(f32), axis=0, keepdims=True)


def remote(src, dst, sems, device):
    return pltpu.make_async_remote_copy(
        src_ref=src, dst_ref=dst, send_sem=sems[0], recv_sem=sems[1],
        device_id=device, device_id_type=MESH,
    )


def layers_kernel(n_z, n_t, rows, width, cols, names, *refs):
    r = Bag(names, refs)
    heads, half_width = cols // HEAD_DIM, width // 2
    scale = HEAD_DIM**-0.5
    core, z, t = lax.axis_index("section"), lax.axis_index("dp"), lax.axis_index("tensor")
    other = {"section": 1 - core}
    step_x, step_y = 1 - 2 * lax.rem(t, 2), 2 - 4 * (t // 2)
    t_x, t_y = t + step_x, t + step_y
    t_far = t + step_x + step_y
    piece, own = rows // n_z, rows // n_t
    chunk_rows = max(piece, 128)
    chunks, per_chunk = rows // chunk_rows, chunk_rows // piece
    mine = rows_at(t, own)
    weights = ("wa", "wo", "wu", "wd")

    def load(i):
        if i < 2:
            return pltpu.make_async_copy(r.x_in.at[core * 2 + i], r.x.at[i], r.load_sem.at[i])
        if i < 4:
            return pltpu.make_async_copy(r.g_in.at[core * 2 + i - 2], r.g.at[i - 2], r.load_sem.at[i])
        if i == 5:
            return pltpu.make_async_copy(r.wo_in, r.wo.at[core, t], r.load_sem.at[i])
        name = weights[i - 4]
        return pltpu.make_async_copy(
            getattr(r, name + "_in"), getattr(r, name).at[core], r.load_sem.at[i]
        )

    def swap(i):
        sems = (r.swap_s.at[i], r.swap_r.at[i])
        if i == 4:
            return remote(r.idx.at[core], r.idx.at[core], sems, other)
        if i == 5:
            return remote(r.par.at[core], r.par.at[core], sems, other)
        if i == 1:
            return remote(r.wo_in, r.wo.at[core, t], sems, other)
        name = weights[i]
        return remote(getattr(r, name + "_in"), getattr(r, name).at[core], sems, other)

    def start():
        for i in (0, 4, 1, 5, 6, 7, 2, 3):
            load(i).start()
        for kind, index in enumerate((r.items_in, r.send_in, r.recv_in)):
            for i in range(4):
                for c in range(rows // 128):
                    cut = slice(c * 128, (c + 1) * 128)
                    row = index[i : i + 1, cut] if kind == 0 else index[i, :, cut]
                    r.idx[core, kind * 4 + i, c] = row
        r.par[core, 0:1, :] = jnp.zeros((1, width), f32)
        r.par[core, 0:1, :cols] = r.qv_in[0:1]
        r.par[core, 0:1, 2 * cols : 3 * cols] = r.qv_in[1:2]
        for first, value in ((1, r.bo_in), (2, r.norm1_in), (4, r.bu_in), (5, r.bd_in), (6, r.norm2_in)):
            r.par[core, first : first + value.shape[0], :] = value[...]
        r.vec[...] = jnp.zeros(r.vec.shape, f32)
        barrier = pltpu.get_barrier_semaphore()
        pl.semaphore_signal(barrier, inc=1, device_id=other, device_id_type=MESH)

        def greet_z(k):
            peer = lax.rem(z + 1 + k, n_z)
            pl.semaphore_signal(barrier, inc=1, device_id={"dp": peer}, device_id_type=MESH)

        def greet_t(k):
            peer = lax.rem(t + 1 + k, n_t)
            pl.semaphore_signal(barrier, inc=1, device_id={"tensor": peer}, device_id_type=MESH)

        loop(n_z - 1, greet_z)
        loop(n_t - 1, greet_t)
        pl.semaphore_wait(barrier, n_z + n_t - 1)
        for i in (4, 5, 0, 1):
            swap(i).start()
        for k in range(1, n_t):
            wo_copy(k).start()
        for i in (2, 3):
            swap(i).start()
        swap(4).wait()
        swap(5).wait()

    def wo_copy(k):
        return remote(
            r.wo_in, r.wo.at[core, t], (r.wt_s.at[k - 1], r.wt_r.at[k - 1]),
            {"tensor": lax.rem(t + k, n_t)},
        )

    def wo_on_copy(k):
        slab = r.wo.at[core, lax.rem(t - k + n_t, n_t)]
        return remote(slab, slab, (r.wc_s.at[k - 1], r.wc_r.at[k - 1]), other)

    def out_weight_on(l, m):
        load(5).wait()
        for k in range(1, n_t):
            wo_copy(k).wait_recv()
            wo_on_copy(k).start()

    asked = set()

    def need_weight(layer, i):
        if (layer, i) in asked:
            return
        asked.add((layer, i))

        if i != 1:

            @pl.when(core == layer)
            def _():
                load(4 + i).wait()

        @pl.when(core != layer)
        def _():
            swap(i).wait_recv()
            if i == 1:
                for k in range(1, n_t):
                    wo_on_copy(k).wait_recv()

    def index_cut(kind, layer, m, first, count):
        cuts = [
            r.idx[layer, kind * 4 + core * 2 + m, first // 128 + i] for i in range(count // 128)
        ]
        return cuts[0] if len(cuts) == 1 else jnp.concatenate(cuts, axis=1)

    def index_row(kind, layer, m):
        return index_cut(kind, layer, m, 0, rows)

    def par(layer, i, count=None):
        return r.par[layer, i : i + 1, : count or width]

    def z_copies(kind, m, k, src, dst, src_rest, dst_rest):
        peer = lax.rem(z + k, n_z)
        full = src.shape[1] // 128 * 128
        lanes = pl.ds(0, full)
        return [
            remote(
                src.at[rows_at(peer, piece), lanes], dst.at[rows_at(z, piece), lanes],
                (r.z_s.at[2 * kind, m, k - 1], r.z_r.at[2 * kind, m, k - 1]), {"dp": peer},
            ),
            remote(
                src_rest.at[peer], dst_rest.at[z],
                (r.z_s.at[2 * kind + 1, m, k - 1], r.z_r.at[2 * kind + 1, m, k - 1]), {"dp": peer},
            ),
        ]

    def z_chunk(kk):
        return lax.rem(z // per_chunk + 1 + kk, chunks)

    def z_send(kind, m, cc, rest, *refs):
        rest = rest.astype(f32)
        for j in range(per_chunk):
            upper = rest[j * piece : j * piece + piece // 2]
            lower = rest[j * piece + piece // 2 : (j + 1) * piece]
            refs[2][cc * per_chunk + j] = jnp.concatenate([upper, lower], axis=1).astype(bf16)

        def one(j):
            peer = cc * per_chunk + j
            k = lax.rem(peer - z + n_z, n_z)

            @pl.when(k > 0)
            def _():
                for copy in z_copies(kind, m, k, *refs):
                    copy.start()

        loop(per_chunk, one)

    def z_take(kind, m, src, dst, src_rest, dst_rest):
        def wait(k):
            for copy in z_copies(kind, m, k + 1, src, dst, src_rest, dst_rest):
                copy.wait()

        loop(n_z - 1, wait)
        full = src.shape[1] // 128 * 128
        here = rows_at(z, piece)
        dst[here, :full] = src[here, :full]
        dst_rest[z] = src_rest[z]

        def unpack(b):
            both = dst_rest[b].astype(f32)
            whole = jnp.concatenate([both[:, :HEAD_DIM], both[:, HEAD_DIM:]], axis=0)
            dst[rows_at(b, piece), full:] = whole.astype(bf16)

        loop(n_z, unpack)

    left, right = slice(0, half_width), slice(half_width, width)

    def sum_copy(m, j):
        peer = t_x if j in (0, 1, 5) else t_y
        return remote(
            r.sum_src.at[m, j], r.sum_dst.at[m, j], (r.sum_s.at[m, j], r.sum_r.at[m, j]),
            {"tensor": peer},
        )

    def sum_put(m, role, part):
        @pl.when(role == 0)
        def _():
            r.sum_own[m] = part

        @pl.when(role == 1)
        def _():
            r.sum_src[m, 1] = part[:, left].astype(bf16)
            r.sum_keep[m, 1] = part[:, right].astype(bf16)
            sum_copy(m, 1).start()

        @pl.when(role == 2)
        def _():
            r.sum_src[m, 3] = part[:, right].astype(bf16)
            r.sum_keep[m, 0] = part[:, left].astype(bf16)
            sum_copy(m, 3).start()

        @pl.when(role == 3)
        def _():
            r.sum_src[m, 0] = part[:, left].astype(bf16)
            sum_copy(m, 0).start()
            r.sum_src[m, 2] = part[:, right].astype(bf16)
            sum_copy(m, 2).start()

    def sum_mid(m):
        sum_copy(m, 0).wait_recv()
        r.sum_src[m, 4] = (r.sum_keep[m, 0].astype(f32) + r.sum_dst[m, 0].astype(f32)).astype(bf16)
        sum_copy(m, 4).start()
        sum_copy(m, 2).wait_recv()
        r.sum_src[m, 5] = (r.sum_keep[m, 1].astype(f32) + r.sum_dst[m, 2].astype(f32)).astype(bf16)
        sum_copy(m, 5).start()

    def sum_take(m):
        for j in (1, 3, 4, 5):
            sum_copy(m, j).wait_recv()
        for j in range(6):
            sum_copy(m, j).wait_send()
        added = jnp.concatenate(
            [
                r.sum_dst[m, 1].astype(f32) + r.sum_dst[m, 4].astype(f32),
                r.sum_dst[m, 3].astype(f32) + r.sum_dst[m, 5].astype(f32),
            ],
            axis=1,
        )
        return r.sum_own[m] + added

    def role_rows(role):
        return rows_at(t + lax.rem(role, 2) * step_x + (role // 2) * step_y, own)

    def gather_copy(kind, m, j, buf):
        first = (t, t, t, t, t_x, t_y)[j] * own
        low = j in (1, 2, 5)
        here = pl.ds(pl.multiple_of(first + (own // 2 if low else 0), own // 2), own // 2)
        return remote(
            buf.at[here], buf.at[here], (r.gather_s.at[kind, m, j], r.gather_r.at[kind, m, j]),
            {"tensor": t_x if j in (0, 1, 5) else t_y},
        )

    def gather_start(kind, m, buf):
        for j in (0, 2, 1, 3):
            gather_copy(kind, m, j, buf).start()

    def gather_on(kind, m, buf):
        gather_copy(kind, m, 0, buf).wait_recv()
        gather_copy(kind, m, 4, buf).start()
        gather_copy(kind, m, 2, buf).wait_recv()
        gather_copy(kind, m, 5, buf).start()

    def gather_near(kind, m, buf, j):
        gather_copy(kind, m, j, buf).wait_recv()

    def gather_far(kind, m, buf):
        gather_copy(kind, m, 4, buf).wait_recv()
        gather_copy(kind, m, 5, buf).wait_recv()

    def gather_rest(kind, m, buf):
        for j in (1, 3, 4, 5):
            gather_copy(kind, m, j, buf).wait_recv()
        gather_sent(kind, m, buf)

    def gather_sent(kind, m, buf):
        for j in range(6):
            gather_copy(kind, m, j, buf).wait_send()

    def gather_step(kind, m, role, buf):
        @pl.when(role == 1)
        def _():
            gather_on(kind, m, buf)
            gather_near(kind, m, buf, 1)

        @pl.when(role == 2)
        def _():
            gather_near(kind, m, buf, 3)

        @pl.when(role == 3)
        def _():
            gather_far(kind, m, buf)

    def out_local(kind, m, src, out):
        return pltpu.make_async_copy(src, out.at[core * 2 + m], r.out_l.at[kind, m])

    def out_away(kind, m, src, out):
        return remote(src, out.at[core * 2 + m], (r.out_s.at[kind, m], r.out_r.at[kind, m]), other)

    def out_start(kind, layer, m, src, out):
        @pl.when(core == layer)
        def _():
            out_local(kind, m, src, out).start()

        @pl.when(core != layer)
        def _():
            out_away(kind, m, src, out).start()

    def out_wait(kind, layer, m, src, out):
        @pl.when(core == layer)
        def _():
            out_local(kind, m, src, out).wait()

        @pl.when(core != layer)
        def _():
            out_away(kind, m, src, out).wait_send()

    rest_z, rest_m = 3 * cols - HEAD_DIM, cols - HEAD_DIM

    def z_big(m):
        return r.zs.at[m], r.zr.at[m], r.zs_rest.at[m], r.zr_rest.at[m]

    def z_home(m):
        return r.dmr.at[m], r.ms.at[m], r.ms_rest.at[m], r.mr_rest.at[m]

    def z_back(m):
        return r.dmt.at[m], r.dmr.at[m], r.ms_rest.at[m], r.mr_rest.at[m]

    def project(l, m):
        need_weight(l, 0)
        if l == 0:
            load(m).wait()

        def chunk(kk):
            cc = z_chunk(kk)
            here = rows_at(cc, chunk_rows)
            numbers = lax.broadcasted_iota(jnp.int32, (rows, chunk_rows), 0)
            pick = (numbers == index_cut(1, l, m, cc * chunk_rows, chunk_rows)).astype(bf16)
            moved = tn(pick, r.x[m]).astype(bf16)
            r.xp[l, m, here] = moved
            block = (nt(moved, r.wa[l]) + par(l, 0, 3 * cols)).astype(bf16)
            r.zs[m, here] = block[:, :rest_z]
            z_send(0, m, cc, block[:, rest_z:], *z_big(m))

        loop(chunks, chunk)

    def attend(l, m):
        z_take(0, m, *z_big(m))
        lane = lax.broadcasted_iota(jnp.int32, (1, 128), 1)

        def cluster(c):
            here = rows_at(c, CLUSTER)
            numbers = lax.broadcasted_iota(jnp.int32, (rows, CLUSTER), 0)
            pick = (numbers == index_cut(2, l, m, c * CLUSTER, CLUSTER)).astype(bf16)
            block = tn(pick, r.zr[m]).astype(bf16)
            r.grouped[l, m, here] = block
            queries, keys, values = (block[:, i * cols : (i + 1) * cols] for i in range(3))
            scores = nt(queries, by_head(keys, heads)) * scale
            same = same_item(index_cut(0, l, m, c * CLUSTER, CLUSTER))
            probs = []
            log_row = jnp.zeros((1, 128), f32)
            for h in range(heads):
                cut = slice(h * CLUSTER, (h + 1) * CLUSTER)
                prob, centred, total = softmax_parts(scores[:, cut], same)
                inner = jnp.sum(jnp.where(same, prob * centred, 0.0), axis=-1, keepdims=True)
                entropy = jnp.mean(jnp.log(total) - inner, axis=0, keepdims=True)
                log_row = jnp.where(lane == h, entropy, log_row)
                probs.append(prob.astype(bf16))
            r.entropy[l, m, pl.ds(c, 1)] = log_row
            mixed = nn(jnp.concatenate(probs, axis=1), by_head(values, heads))
            r.dmt[m, here] = mixed.astype(bf16)

        loop(rows // CLUSTER, cluster)

        def home(kk):
            cc = z_chunk(kk)
            here = rows_at(cc, chunk_rows)
            one_hot = place_rows(index_row(2, l, m), cc * chunk_rows, chunk_rows)
            block = nn(one_hot, r.dmt[m]).astype(bf16)
            r.dmr[m, here] = block
            z_send(1, m, cc, block[:, rest_m:], *z_home(m))

        loop(chunks, home)

    def heads_copy(l, m, k):
        peer = lax.rem(t + k, n_t)
        return remote(
            r.ms.at[m, rows_at(peer, own)], r.mt.at[l, m, t],
            (r.ta_s.at[m, k - 1], r.ta_r.at[m, k - 1]), {"tensor": peer},
        )

    def out_project(l, m):
        z_take(1, m, *z_home(m))
        for k in (2, 1, 3):
            heads_copy(l, m, k).start()
        r.mt[l, m, t] = r.ms[m, mine]

    def middle(l, m):
        sum_mid(m)

    def first_norm(l, m):
        need_weight(l, 1)
        for k in range(1, n_t):
            heads_copy(l, m, k).wait()
        total = r.xp[l, m, mine].astype(f32) + par(l, 1)
        for s in range(n_t):
            total = total + nn(r.mt[l, m, s], r.wo[l, s])
        normed, inverse = normalise(total)
        hidden = normed * par(l, 2) + par(l, 3)
        r.n1[l, m] = normed.astype(bf16)
        r.inv1[l, m] = jnp.broadcast_to(inverse, (own, 128))
        r.hid[m] = hidden
        r.hfull[l, m, mine] = hidden.astype(bf16)
        gather_start(0, m, r.hfull.at[l, m])

    def feed(l, m):
        need_weight(l, 2)
        need_weight(l, 3)

        def part(role):
            gather_step(0, m, role, r.hfull.at[l, m])
            here = role_rows(role)
            up = nn(r.hfull[l, m, here], r.wu[l]) + par(l, 4)
            square = up * up
            tanh = jnp.tanh(0.7978845608028654 * up * (1.0 + 0.044715 * square))
            half = 0.5 * (1.0 + tanh)
            slope = 0.7978845608028654 * (1.0 + 3 * 0.044715 * square)
            r.gp[l, m, here] = (half + 0.5 * up * (1.0 - tanh * tanh) * slope).astype(bf16)
            active = (up * half).astype(bf16)
            r.act[l, m, here] = active
            sum_put(m, role, nn(active, r.wd[l]))

        loop(n_t, part)

    def second_norm(l, m):
        gather_sent(0, m, r.hfull.at[l, m])
        total = sum_take(m) + par(l, 5)
        normed, inverse = normalise(r.hid[m] + total)
        r.n2[l, m] = normed.astype(bf16)
        r.inv2[l, m] = jnp.broadcast_to(inverse, (own, 128))
        r.ag[m, mine] = (normed * par(l, 6) + par(l, 7)).astype(bf16)
        gather_start(1, m, r.ag.at[m])

    def out_on(l, m):
        gather_on(1, m, r.ag.at[m])

    def to_tokens(l, m, dst, buf):
        def chunk(cc):
            one_hot = place_rows(index_row(1, l, m), cc * 128, 128)
            dst[m, rows_at(cc, 128)] = nn(one_hot, buf[m]).astype(bf16)

        loop(rows // 128, chunk)

    def out_tokens(l, m):
        gather_rest(1, m, r.ag.at[m])
        if l == 1:
            out_wait(0, 0, m, r.x.at[m], r.acts)
        to_tokens(l, m, r.x, r.ag)
        out_start(0, l, m, r.x.at[m], r.acts)

    def add_vec(l, index, value):
        r.vec[l, index : index + 1, : value.shape[1]] += value

    def b_second_norm(l, m):
        if l == 1:
            load(2 + m).wait()
        numbers = lax.broadcasted_iota(jnp.int32, (rows, own), 0)
        pick = (numbers == index_cut(1, l, m, t * own, own)).astype(bf16)
        up = tn(pick, r.g[m])
        normed = r.n2[l, m].astype(f32)
        down = norm_backward(up, normed, r.inv2[l, m][:, :1], par(l, 6))
        r.hid[m] = down
        low = down.astype(bf16)
        r.db[m, mine] = low
        gather_start(2, m, r.db.at[m])
        add_vec(l, 0, column_sum(up * normed))
        add_vec(l, 1, column_sum(up))
        add_vec(l, 2, column_sum(low))

    def b_feed(l, m):
        def part(role):
            gather_step(2, m, role, r.db.at[m])
            here = role_rows(role)
            low = (nt(r.db[m, here], r.wd[l]) * r.gp[l, m, here].astype(f32)).astype(bf16)
            r.gp[l, m, here] = low
            sum_put(m, role, nt(low, r.wu[l]))

        loop(n_t, part)

    def grad_slabs(ref, value, lanes):
        ref[:, :, lanes] = value.reshape(n_z, width // n_z, value.shape[1]).astype(bf16)

    def feed_weights(l, m):
        for i in range(2):
            gather_sent(2, i, r.db.at[i])
            add_vec(l, 6, column_sum(r.gp[l, i]))

        def block(c):
            cut = rows_at(c, 256)
            up = tn(r.hfull[l, 0], r.gp[l, 0, :, cut]) + tn(r.hfull[l, 1], r.gp[l, 1, :, cut])
            grad_slabs(r.gs_feed, up, cut)
            down = tn(r.db[0], r.act[l, 0, :, cut]) + tn(r.db[1], r.act[l, 1, :, cut])
            grad_slabs(r.gs_feed, down, pl.ds(pl.multiple_of(width + c * 256, 256), 256))

        loop(width // 256, block)
        grads_send(0, l, r.gs_feed, r.gr_feed)

    def b_first_norm(l, m):
        up = r.hid[m] + sum_take(m)
        normed = r.n1[l, m].astype(f32)
        down = norm_backward(up, normed, r.inv1[l, m][:, :1], par(l, 2))
        r.dres[m] = down
        low = down.astype(bf16)
        r.da[m] = low

        def part(kk):
            k = lax.rem(kk + 1, n_t)
            peer = lax.rem(t + k, n_t)
            block = nt(low, r.wo[l, peer]).astype(bf16)

            @pl.when(k > 0)
            def _():
                r.ms[m, rows_at(peer, own)] = block
                rows_copy(m, k).start()

            @pl.when(k == 0)
            def _():
                r.dmt[m, mine] = block

        loop(n_t, part)
        add_vec(l, 3, column_sum(up * normed))
        add_vec(l, 4, column_sum(up))
        add_vec(l, 5, column_sum(low))

    def rows_copy(m, k):
        peer = lax.rem(t + k, n_t)
        return remote(
            r.ms.at[m, rows_at(peer, own)], r.dmt.at[m, mine], (r.tb_s.at[m, k - 1], r.tb_r.at[m, k - 1]),
            {"tensor": peer},
        )

    def out_back(l, m):
        for k in range(1, n_t):
            rows_copy(m, k).wait()

        def chunk(kk):
            cc = z_chunk(kk)
            z_send(2, m, cc, r.dmt[m, rows_at(cc, chunk_rows), rest_m:], *z_back(m))

        loop(chunks, chunk)

    def out_weights(l, m):
        for s in range(n_t):
            value = tn(r.da[0], r.mt[l, 0, s]) + tn(r.da[1], r.mt[l, 1, s])
            r.gs_out[s] = value.reshape(n_z, width // n_z, cols).astype(bf16)

        @pl.when(core != l)
        def _():
            for k in range(n_t):
                out_core_copy(lax.rem(t + 1 + k, n_t)).start()

    def b_attend(l, m):
        z_take(2, m, *z_back(m))

        def cluster(c):
            here = rows_at(c, CLUSTER)
            numbers = lax.broadcasted_iota(jnp.int32, (rows, CLUSTER), 0)
            pick = (numbers == index_cut(2, l, m, c * CLUSTER, CLUSTER)).astype(bf16)
            dmix = tn(pick, r.dmr[m]).astype(bf16)
            block = r.grouped[l, m, here]
            queries, keys, values = (block[:, i * cols : (i + 1) * cols] for i in range(3))
            keys_by_head = by_head(keys, heads)
            scores = nt(queries, keys_by_head) * scale
            same = same_item(index_cut(0, l, m, c * CLUSTER, CLUSTER))
            dprob = nt(dmix, by_head(values, heads))
            probs, dscores = [], []
            for h in range(heads):
                cut = slice(h * CLUSTER, (h + 1) * CLUSTER)
                prob = softmax_parts(scores[:, cut], same)[0]
                outer = prob * dprob[:, cut]
                dscore = outer - prob * jnp.sum(outer, axis=-1, keepdims=True)
                probs.append(prob.astype(bf16))
                dscores.append(dscore.astype(bf16))
            prob_all = jnp.concatenate(probs, axis=1)
            dscore_all = jnp.concatenate(dscores, axis=1)
            dqueries = nn(dscore_all, keys_by_head) * scale
            dkeys = fold_heads(tn(dscore_all, queries), heads) * scale
            dvalues = fold_heads(tn(prob_all, dmix), heads)
            r.grouped[l, m, here] = jnp.concatenate([dqueries, dkeys, dvalues], axis=1).astype(bf16)

        loop(rows // CLUSTER, cluster)

        def home(kk):
            cc = z_chunk(kk)
            here = rows_at(cc, chunk_rows)
            one_hot = place_rows(index_row(2, l, m), cc * chunk_rows, chunk_rows)
            block = nn(one_hot, r.grouped[l, m]).astype(bf16)
            r.zs[m, here] = block[:, :rest_z]
            z_send(3, m, cc, block[:, rest_z:], *z_big(m))

        loop(chunks, home)

    def in_project(l, m):
        z_take(3, m, *z_big(m))

        def part(kk):
            role = 3 - kk
            sum_put(m, role, nn(r.zr[m, role_rows(role)], r.wa[l]))

        loop(n_t, part)

    def in_weights(l, m):
        for i in range(2):
            add_vec(l, 7, column_sum(r.zr[i]))
        for first in range(0, 3 * cols, 256):
            cut = slice(first, min(first + 256, 3 * cols))
            value = tn(r.xp[l, 0], r.zr[0, :, cut]) + tn(r.xp[l, 1], r.zr[1, :, cut])
            grad_slabs(r.gs_attn, value, cut)
        grads_send(1, l, r.gs_attn, r.gr_attn)

    def layer_input(l, m):
        r.ag[m, mine] = (r.dres[m] + sum_take(m)).astype(bf16)
        gather_start(4, m, r.ag.at[m])

    def b_out_on(l, m):
        gather_on(4, m, r.ag.at[m])

    def b_tokens(l, m):
        gather_rest(4, m, r.ag.at[m])
        if l == 0:
            out_wait(1, 1, m, r.g.at[m], r.grads)
        to_tokens(l, m, r.g, r.ag)
        out_start(1, l, m, r.g.at[m], r.grads)

    def grad_core_copy(kind, k, src, dst):
        return remote(src.at[k], dst.at[k], (r.gc_s.at[kind, k], r.gc_r.at[kind, k]), other)

    def grad_z_copy(kind, k, src, dst, lanes=slice(None)):
        peer = lax.rem(z + k, n_z)
        return remote(
            src.at[peer, :, lanes], dst.at[k - 1, :, lanes], (r.gz_s.at[kind, k - 1], r.gz_r.at[kind, k - 1]),
            {"dp": peer},
        )

    def grads_send(kind, l, src, dst):
        @pl.when(core != l)
        def _():
            loop(n_z, lambda k: grad_core_copy(kind, lax.rem(z + 1 + k, n_z), src, dst).start())

    def grads_add(kind, src, came, k, wait, lanes):
        peer = lax.rem(z + k, n_z)
        if wait:
            grad_core_copy(kind, peer, src, came).wait_recv()
        total = src[peer, :, lanes].astype(f32) + came[peer, :, lanes].astype(f32)
        src[peer, :, lanes] = total.astype(bf16)

    def grads_part(kind, sem, l, src, came, dst, part, wait, lanes):
        @pl.when(core == l)
        def _():
            first, last = part * (n_z - 1) // 3, (part + 1) * (n_z - 1) // 3

            def one(i):
                grads_add(kind, src, came, first + 1 + i, wait, lanes)
                grad_z_copy(sem, first + 1 + i, src, dst, lanes).start()

            loop(last - first, one)

    def grads_end(kind, sems, l, src, came, dst, outs):
        @pl.when(core == l)
        def _():
            lanes = src.shape[2] // len(sems)
            for i in range(len(sems)):
                grads_add(kind, src, came, 0, i == 0, slice(i * lanes, (i + 1) * lanes))
            cuts, first = [], 0
            for out in outs:
                cuts.append(slice(first, first + out.shape[-1]))
                first += out.shape[-1]
            for out, cut in zip(outs, cuts):
                out[...] = src[z, :, cut].astype(f32)

            def one(k):
                for i, sem in enumerate(sems):
                    grad_z_copy(sem, k + 1, src, dst, slice(i * lanes, (i + 1) * lanes)).wait()
                for out, cut in zip(outs, cuts):
                    out[...] += dst[k, :, cut].astype(f32)

            loop(n_z - 1, one)

        @pl.when(core != l)
        def _():
            loop(n_z, lambda k: grad_core_copy(kind, k, src, came).wait_send())

    def line_copy(half, c, slot, step):
        lanes = slice(half * width, (half + 1) * width)
        return remote(
            r.gs_feed.at[c, :, lanes], r.gz_feed.at[slot, :, lanes],
            (r.line_s.at[half, c], r.line_r.at[half, slot]), {"dp": z + step},
        )

    def line_add(half, c, slot, came):
        lanes = slice(half * width, (half + 1) * width)
        grads_add(0, r.gs_feed, r.gr_feed, c - z, half == 0, lanes)

        @pl.when(came)
        def _():
            line_copy(half, c, slot, 0).wait_recv()
            total = r.gs_feed[c, :, lanes].astype(f32) + r.gz_feed[slot, :, lanes].astype(f32)
            r.gs_feed[c, :, lanes] = total.astype(bf16)

    def line_part(half, part, l):
        @pl.when(core == l)
        def _():
            first, last = part * (n_z - 1) // 3, (part + 1) * (n_z - 1) // 3

            def one(i):
                far = n_z - 1 - first - i

                @pl.when(z + far < n_z)
                def _():
                    line_add(half, z + far, z + far, z > 0)
                    line_copy(half, z + far, z + far, 1).start()

                @pl.when(z - far >= 0)
                def _():
                    line_add(half, z - far, z - far, z < n_z - 1)
                    slot = jnp.where(far == 1, n_z, z - far)
                    line_copy(half, z - far, slot, -1).start()

            loop(last - first, one)

    def line_end(l):
        @pl.when(core == l)
        def _():
            for half, out in enumerate((r.g_up, r.g_down)):
                lanes = slice(half * width, (half + 1) * width)
                line_add(half, z, z, z > 0)
                out[...] = r.gs_feed[z, :, lanes].astype(f32)

                @pl.when(z < n_z - 1)
                def _():
                    line_copy(half, z, n_z, 0).wait_recv()
                    out[...] += r.gz_feed[n_z, :, lanes].astype(f32)

                def sent(k):
                    line_copy(half, lax.rem(z + 1 + k, n_z), 0, 0).wait_send()

                loop(n_z - 1, sent)

        @pl.when(core != l)
        def _():
            loop(n_z, lambda k: grad_core_copy(0, k, r.gs_feed, r.gr_feed).wait_send())

    def feed_part(i):
        return lambda l, m: line_part(i % 2, i // 2, l)

    def attn_part(i):
        return lambda l, m: grads_part(
            1, 2, l, r.gs_attn, r.gr_attn, r.gz_attn, i, True, slice(None)
        )

    feed_0, feed_1, feed_2, feed_3, feed_4, feed_5 = (feed_part(i) for i in range(6))
    attn_0, attn_1, attn_2 = (attn_part(i) for i in range(3))

    def feed_end(l, m):
        line_end(l)

    def attn_end(l, m):
        grads_end(1, (2,), l, r.gs_attn, r.gr_attn, r.gz_attn, tuple(r.g_attn.at[i] for i in range(3)))

    def out_core_copy(s):
        return remote(r.gs_out.at[s], r.gr_out.at[s], (r.oc_s.at[s], r.oc_r.at[s]), other)

    def out_t_copy(k):
        peer = lax.rem(t + k, n_t)
        return remote(
            r.gs_out.at[peer], r.gt_out.at[k - 1], (r.ot_s.at[k - 1], r.ot_r.at[k - 1]),
            {"tensor": peer},
        )

    def out_z_copy(k):
        peer = lax.rem(z + k, n_z)
        return remote(
            r.gs_out.at[t, peer], r.gz_out.at[k - 1], (r.gz_s.at[3, k - 1], r.gz_r.at[3, k - 1]),
            {"dp": peer},
        )

    def out_sum_t(l, m):
        @pl.when(core == l)
        def _():
            for kk in range(n_t):
                k = (kk + 1) % n_t
                s = lax.rem(t + k, n_t)
                out_core_copy(s).wait_recv()
                r.gs_out[s] = (r.gs_out[s].astype(f32) + r.gr_out[s].astype(f32)).astype(bf16)
                if k > 0:
                    out_t_copy(k).start()

    def out_sum_z(l, m):
        @pl.when(core == l)
        def _():
            for k in range(1, n_t):
                out_t_copy(k).wait()
            total = r.gs_out[t].astype(f32)
            for k in range(1, n_t):
                total = total + r.gt_out[k - 1].astype(f32)
            r.gs_out[t] = total.astype(bf16)
            loop(n_z - 1, lambda k: out_z_copy(k + 1).start())

        @pl.when(core != l)
        def _():
            for s in range(n_t):
                out_core_copy(s).wait_send()

    def out_end(l, m):
        @pl.when(core == l)
        def _():
            r.g_out[...] = r.gs_out[t, z].astype(f32)

            def one(k):
                out_z_copy(k + 1).wait()
                r.g_out[...] += r.gz_out[k].astype(f32)

            loop(n_z - 1, one)

    def vec_copy(l):
        return remote(r.vec.at[l], r.vec_came, (r.vc_s.at[0], r.vc_r.at[0]), other)

    def vec_t_copy(k):
        return remote(
            r.vec_t.at[t], r.vec_t.at[t], (r.vt_s.at[k - 1], r.vt_r.at[k - 1]),
            {"tensor": lax.rem(t + k, n_t)},
        )

    def vec_z_copy(k):
        return remote(
            r.vec_z.at[z], r.vec_z.at[z], (r.vz_s.at[k - 1], r.vz_r.at[k - 1]),
            {"dp": lax.rem(z + k, n_z)},
        )

    def entropy_copy(l, m):
        return remote(
            r.entropy.at[l, m], r.ent.at[core * 2 + m], (r.en_s.at[m], r.en_r.at[m]), other
        )

    def vec_start(l, m):
        @pl.when(core != l)
        def _():
            vec_copy(l).start()
            for i in range(2):
                entropy_copy(l, i).start()

    def vec_sum_t(l, m):
        @pl.when(core == l)
        def _():
            for i in range(2):
                r.ent[core * 2 + i] = r.entropy[l, i]
            vec_copy(l).wait_recv()
            r.vec_t[t] = r.vec[l] + r.vec_came[...]
            for k in range(1, n_t):
                vec_t_copy(k).start()

    def vec_sum_z(l, m):
        @pl.when(core == l)
        def _():
            for k in range(1, n_t):
                vec_t_copy(k).wait()
            total = r.vec_t[0]
            for k in range(1, n_t):
                total = total + r.vec_t[k]
            lane_rows = lax.broadcasted_iota(jnp.int32, total.shape, 0)
            r.vec_z[z] = jnp.where(lane_rows < 6, total, r.vec_t[t])
            loop(n_z - 1, lambda k: vec_z_copy(k + 1).start())

    def vec_end(l, m):
        @pl.when(core == l)
        def _():
            loop(n_z - 1, lambda k: vec_z_copy(k + 1).wait())
            r.vec_out[...] = r.vec_z[0]

            def one(k):
                r.vec_out[...] += r.vec_z[k + 1]

            loop(n_z - 1, one)

        @pl.when(core != l)
        def _():
            vec_copy(l).wait_send()
            for i in range(2):
                entropy_copy(l, i).wait_send()

    def finish():
        for m in range(2):
            out_wait(0, 1, m, r.x.at[m], r.acts)
            out_wait(1, 0, m, r.g.at[m], r.grads)
            for kind, out, src in ((0, r.acts, r.x), (1, r.grads, r.g)):
                out_away(kind, m, src.at[m], out).wait_recv()
            entropy_copy(0, m).wait_recv()
        for i in range(4):
            swap(i).wait_send()
        for k in range(1, n_t):
            wo_copy(k).wait_send()
            wo_on_copy(k).wait_send()

    schedule = (
        (project, 0, 1), (attend, 0, 1), (out_weight_on, 0, 0), (out_project, 0, 1), (project, 0, 0),
        (first_norm, 0, 1), (feed, 0, 1), (attend, 0, 0), (middle, 0, 1), (out_project, 0, 0),
        (second_norm, 0, 1), (out_on, 0, 1), (first_norm, 0, 0), (out_tokens, 0, 1), (project, 1, 1),
        (feed, 0, 0), (middle, 0, 0), (attend, 1, 1), (second_norm, 0, 0), (out_project, 1, 1),
        (out_on, 0, 0), (first_norm, 1, 1), (out_tokens, 0, 0), (project, 1, 0), (feed, 1, 1), (middle, 1, 1),
        (attend, 1, 0), (second_norm, 1, 1), (b_second_norm, 1, 1), (out_on, 1, 1), (out_project, 1, 0),
        (b_feed, 1, 1), (first_norm, 1, 0), (out_tokens, 1, 1), (middle, 1, 1), (feed, 1, 0),
        (b_first_norm, 1, 1), (middle, 1, 0), (out_back, 1, 1), (second_norm, 1, 0), (b_second_norm, 1, 0),
        (b_attend, 1, 1), (out_on, 1, 0), (b_feed, 1, 0), (in_project, 1, 1), (feed_weights, 1, 1),
        (middle, 1, 0), (middle, 1, 1), (b_first_norm, 1, 0), (out_weights, 1, 1), (layer_input, 1, 1),
        (out_back, 1, 0), (b_out_on, 1, 1), (b_tokens, 1, 1), (b_second_norm, 0, 1), (feed_0, 1, 1),
        (feed_1, 1, 1), (b_attend, 1, 0), (b_feed, 0, 1), (out_sum_t, 1, 1), (out_tokens, 1, 0),
        (feed_2, 1, 1), (in_project, 1, 0), (middle, 0, 1), (middle, 1, 0), (in_weights, 1, 1),
        (feed_3, 1, 1), (feed_4, 1, 1), (b_first_norm, 0, 1), (layer_input, 1, 0), (out_sum_z, 1, 1),
        (out_back, 0, 1), (b_out_on, 1, 0), (vec_start, 1, 1), (feed_5, 1, 1), (attn_0, 1, 1),
        (out_end, 1, 1), (b_tokens, 1, 0), (b_second_norm, 0, 0), (b_attend, 0, 1), (vec_sum_t, 1, 1),
        (feed_end, 1, 1), (b_feed, 0, 0), (attn_1, 1, 1), (feed_weights, 0, 1), (feed_0, 0, 1),
        (middle, 0, 0), (vec_sum_z, 1, 1), (feed_1, 0, 1), (in_project, 0, 1), (attn_2, 1, 1),
        (b_first_norm, 0, 0), (out_weights, 0, 1), (feed_2, 0, 1), (middle, 0, 1), (vec_end, 1, 1),
        (out_sum_t, 0, 1), (out_back, 0, 0), (feed_3, 0, 1), (b_attend, 0, 0), (layer_input, 0, 1),
        (feed_4, 0, 1), (out_sum_z, 0, 1), (attn_end, 1, 1), (in_project, 0, 0), (in_weights, 0, 1),
        (b_out_on, 0, 1), (vec_start, 0, 1), (attn_0, 0, 1), (attn_1, 0, 1), (vec_sum_t, 0, 1),
        (middle, 0, 0), (vec_sum_z, 0, 1), (out_end, 0, 1), (layer_input, 0, 0), (attn_2, 0, 1),
        (b_tokens, 0, 1), (feed_5, 0, 1), (vec_end, 0, 1), (b_out_on, 0, 0), (attn_end, 0, 1),
        (b_tokens, 0, 0), (feed_end, 0, 1),
    )
    start()
    for step, layer, micro in schedule:
        step(layer, micro)
    finish()


def run_layers(n_z, x, g, small, wa, wo, wu, wd):
    micros, rows, width = x.shape
    cols, hidden = wo.shape[0], wu.shape[1]
    n_t = lax.axis_size("tensor")
    own, slab = rows // n_t, width // n_z
    pair = (2, rows)
    both = (2, 2, rows)
    anywhere, vmem = pl.BlockSpec(memory_space=pl.ANY), pl.BlockSpec(memory_space=pltpu.VMEM)
    ins = dict(
        x_in=anywhere, g_in=anywhere, items_in=vmem, send_in=vmem, recv_in=vmem, qv_in=vmem,
        bo_in=vmem, norm1_in=vmem, bu_in=vmem, bd_in=vmem, norm2_in=vmem, wa_in=anywhere, wo_in=anywhere,
        wu_in=anywhere, wd_in=anywhere,
    )
    outs = dict(
        acts=(anywhere, x.shape, bf16), grads=(anywhere, x.shape, bf16),
        g_up=(vmem, (slab, width), f32), g_down=(vmem, (slab, width), f32),
        g_attn=(vmem, (3, slab, cols), f32),
        g_out=(vmem, (slab, cols), f32),
        vec_out=(vmem, (8, width), f32), ent=(vmem, (micros, max(8, rows // CLUSTER), 128), f32),
    )
    sem = pltpu.SemaphoreType.DMA
    scratch = dict(
        x=((*pair, width), bf16), g=((*pair, width), bf16),
        wa=((2, 3 * cols, width), bf16), wo=((2, n_t, cols, width), bf16),
        wu=((2, width, hidden), bf16), wd=((2, hidden, width), bf16),
        idx=((2, 12, rows // 128, 1, 128), jnp.int32), par=((2, 8, width), f32),
        xp=((*both, width), bf16), grouped=((*both, 3 * cols), bf16), ms=((*pair, cols), bf16),
        mt=((2, 2, n_t, own, cols), bf16),
        n1=((2, 2, own, width), bf16), inv1=((2, 2, own, 128), f32), hfull=((*both, width), bf16),
        act=((*both, hidden), bf16), gp=((*both, hidden), bf16),
        n2=((2, 2, own, width), bf16), inv2=((2, 2, own, 128), f32),
        entropy=((2, 2, max(8, rows // CLUSTER), 128), f32),
        zs=((*pair, 3 * cols - HEAD_DIM), bf16), zs_rest=((2, n_z, rows // n_z // 2, 128), bf16),
        zr_rest=((2, n_z, rows // n_z // 2, 128), bf16), ms_rest=((2, n_z, rows // n_z // 2, 128), bf16),
        mr_rest=((2, n_z, rows // n_z // 2, 128), bf16), zr=((*pair, 3 * cols), bf16),
        dmr=((*pair, cols), bf16),
        sum_src=((2, 6, own, width // 2), bf16), sum_dst=((2, 6, own, width // 2), bf16),
        sum_keep=((2, 2, own, width // 2), bf16), sum_own=((2, own, width), f32),
        hid=((2, own, width), f32), dres=((2, own, width), f32),
        ag=((*pair, width), bf16), db=((*pair, width), bf16), da=((2, own, width), bf16),
        dmt=((*pair, cols), bf16),
        gs_feed=((n_z, slab, 2 * width), bf16), gr_feed=((n_z, slab, 2 * width), bf16),
        gz_feed=((n_z + 1, slab, 2 * width), bf16),
        gs_attn=((n_z, slab, 3 * cols), bf16), gr_attn=((n_z, slab, 3 * cols), bf16),
        gz_attn=((n_z - 1, slab, 3 * cols), bf16),
        gs_out=((n_t, n_z, slab, cols), bf16), gr_out=((n_t, n_z, slab, cols), bf16),
        gt_out=((n_t - 1, n_z, slab, cols), bf16), gz_out=((n_z - 1, slab, cols), bf16),
        vec=((2, 8, width), f32), vec_came=((8, width), f32), vec_t=((n_t, 8, width), f32),
        vec_z=((n_z, 8, width), f32),
    )
    sems = dict(load_sem=(8,))
    for name, shape in dict(
        swap=(6,), z=(8, 2, n_z - 1), sum=(2, 6), gather=(5, 2, 6), out=(2, 2), gc=(2, n_z),
        gz=(4, n_z - 1), line=(2, n_z + 1), vc=(1,), vt=(n_t - 1,), vz=(n_z - 1,), en=(2,),
        wt=(n_t - 1,), wc=(n_t - 1,), ta=(2, n_t - 1), tb=(2, n_t - 1), oc=(n_t,), ot=(n_t - 1,),
    ).items():
        sems[name + "_s"] = shape
        sems[name + "_r"] = shape
    sems["out_l"] = (2, 2)
    names = [*ins, *outs, *scratch, *sems]
    return pl.pallas_call(
        functools.partial(layers_kernel, n_z, n_t, rows, width, cols, names),
        out_shape=[jax.ShapeDtypeStruct(shape, dtype) for _, shape, dtype in outs.values()],
        in_specs=list(ins.values()),
        out_specs=[spec for spec, _, _ in outs.values()],
        scratch_shapes=[
            *(pltpu.VMEM(shape, dtype) for shape, dtype in scratch.values()),
            *(sem(shape) for shape in sems.values()),
        ],
        compiler_params=pltpu.CompilerParams(
            collective_id=0, has_side_effects=True, vmem_limit_bytes=VMEM_LIMIT
        ),
        name="layers",
    )(x, g, *small, wa, wo, wu, wd)


def outputs_kernel(
    items, acts, grads, g_up, g_down, g_attn, g_out, vec, ent,
    acts_out, grads_out, ent_out, occ_out, attn_out, qv_out, out_out, out_b, norm1, up_out, up_b, down_out,
    down_b, norm2,
):
    acts_out[...] = acts[...]
    grads_out[...] = grads[...].astype(f32)

    @pl.when(pl.program_id(0) == 0)
    def _():
        heads, micros, clusters = ent_out.shape
        cols = qv_out.shape[1]
        for m in range(micros):
            ent_out[:, m, :] = ent[m].T[:heads, :clusters]
        lane = lax.broadcasted_iota(jnp.int32, (items.shape[0], ITEMS), 1)
        for c in range(clusters):
            row = jnp.zeros(lane.shape, f32)
            labels = items[:, c * CLUSTER : (c + 1) * CLUSTER]
            for i in range(ITEMS):
                count = jnp.sum((labels == i).astype(f32), axis=1, keepdims=True)
                row = jnp.where(lane == i, count, row)
            occ_out[:, c, :] = row
        attn_out[...] = g_attn[...]
        out_out[...] = g_out[...].T
        up_out[...] = g_up[...]
        down_out[...] = g_down[...]
        qv_out[0:1] = vec[7:8, :cols]
        qv_out[1:2] = vec[7:8, 2 * cols : 3 * cols]
        norm2[...] = vec[0:2]
        down_b[...] = vec[2:3]
        norm1[...] = vec[3:5]
        out_b[...] = vec[5:6]
        up_b[...] = vec[6:7]


def finish_outputs(items, acts, grads, g_up, g_down, g_attn, g_out, vec, ent):
    micros, rows, width = acts.shape
    clusters, (slab, cols) = rows // CLUSTER, g_out.shape
    part = pl.BlockSpec((2, rows, width), lambda i: (i, 0, 0))
    whole = pl.BlockSpec(memory_space=pltpu.VMEM)
    shapes = [
        (acts.shape, bf16), (acts.shape, f32), ((cols // HEAD_DIM, micros, clusters), f32),
        ((micros, clusters, ITEMS), f32), (g_attn.shape, f32), ((2, cols), f32), ((cols, slab), f32),
        ((1, width), f32), ((2, width), f32), (g_up.shape, f32), ((1, width), f32), (g_down.shape, f32),
        ((1, width), f32), ((2, width), f32),
    ]

    small = (g_up, g_down, g_attn, g_out, vec, ent)
    return pl.pallas_call(
        outputs_kernel,
        grid=(micros // 2,),
        out_shape=[jax.ShapeDtypeStruct(shape, dtype) for shape, dtype in shapes],
        in_specs=[whole, part, part, *([whole] * len(small))],
        out_specs=[part, part, *([whole] * (len(shapes) - 2))],
        compiler_params=pltpu.CompilerParams(vmem_limit_bytes=VMEM_LIMIT),
        name="outputs",
    )(items, acts, grads, *small)


def shards(
    inputs, out_grad, items, send_order, recv_order,
    attn_weight, qv_bias, out_weight, out_bias, norm_first,
    up_weight, up_bias, down_weight, down_bias, norm_second,
):
    micros, rows, width = inputs.shape
    n_z = lax.axis_size("dp")
    cols = attn_weight.shape[3]
    small = (
        items[0], send_order[0], recv_order[0], qv_bias[0], out_bias, norm_first[0], up_bias,
        down_bias, norm_second[0],
    )
    wa = jnp.transpose(attn_weight[0], (1, 2, 0)).reshape(3 * cols, width)
    acts, grads, g_up, g_down, g_attn, g_out, vec, ent = run_layers(
        n_z, inputs, out_grad, small, wa, out_weight[0], up_weight[0], down_weight[0]
    )
    (
        acts, grads, entropy, occupancy, attn, qv, out_w, out_b, norm1, up, up_b, down, down_b, norm2,
    ) = finish_outputs(items[0], acts, grads, g_up, g_down, g_attn, g_out, vec, ent)
    results = (
        acts, grads, jnp.transpose(entropy, (1, 2, 0)), occupancy, jnp.transpose(attn, (1, 0, 2)), qv, out_w, out_b[0], norm1, up,
        up_b[0], down.T, down_b[0], norm2,
    )
    return tuple(value[None] for value in results)


def solution(mesh):
    return jax.shard_map(
        shards,
        mesh=mesh,
        in_specs=(
            P(None, "dp", None),
            P(None, "dp", None),
            P("section", None, "dp"),
            P("section", None, "dp", None),
            P("section", None, "dp", None),
            P("section", None, None, "tensor"),
            P("section", None, "tensor"),
            P("section", "tensor", None),
            P("section", None),
            P("section", None, None),
            P("section", None, "tensor"),
            P("section", "tensor"),
            P("section", "tensor", None),
            P("section", None),
            P("section", None, None),
        ),
        out_specs=(
            P("section", None, "dp", None),
            P("section", None, "dp", None),
            P("section", None, "dp", "tensor"),
            P("section", None, "dp", None),
            P("section", "dp", None, "tensor"),
            P("section", None, "tensor"),
            P("section", "tensor", "dp"),
            P("section", None),
            P("section", None, None),
            P("section", "dp", "tensor"),
            P("section", "tensor"),
            P("section", "tensor", "dp"),
            P("section", None),
            P("section", None, None),
        ),
        check_vma=False,
    )
```

```python
import functools

import jax
import jax.numpy as jnp
from jax import lax
from jax.experimental import pallas as pl
from jax.experimental.pallas import tpu as pltpu
from jax.sharding import PartitionSpec as P

HEAD_DIM = 64
CLUSTER = 128
ITEMS = 6
EPSILON = 1e-06
MESH = pl.DeviceIdType.MESH
VMEM_LIMIT = 63 * 1024 * 1024
bf16 = jnp.bfloat16
f32 = jnp.float32


def nn(a, b):
    return lax.dot_general(a, b, (((1,), (0,)), ((), ())), preferred_element_type=f32)


def nt(a, b):
    return lax.dot_general(a, b, (((1,), (1,)), ((), ())), preferred_element_type=f32)


def tn(a, b):
    return lax.dot_general(a, b, (((0,), (0,)), ((), ())), preferred_element_type=f32)


def loop(count, body):
    def step(index, carry):
        body(index)
        return carry

    lax.fori_loop(0, count, step, 0)


def rows_at(index, size):
    return pl.ds(pl.multiple_of(index * size, size), size)


class Bag:
    def __init__(self, names, values):
        self.__dict__.update(zip(names, values, strict=True))


def place_rows(row, first, count):
    numbers = lax.broadcasted_iota(jnp.int32, (count, row.shape[1]), 0) + first
    return (numbers == row).astype(bf16)


def by_head(block, heads):
    lane = lax.broadcasted_iota(jnp.int32, block.shape, 1) // HEAD_DIM
    return jnp.concatenate([jnp.where(lane == h, block, jnp.zeros_like(block)) for h in range(heads)])


def fold_heads(stacked, heads):
    count = stacked.shape[0] // heads
    lane = lax.broadcasted_iota(jnp.int32, (count, stacked.shape[1]), 1) // HEAD_DIM
    total = jnp.where(lane == 0, stacked[:count], 0.0)
    for h in range(1, heads):
        total = jnp.where(lane == h, stacked[h * count : (h + 1) * count], total)
    return total


def softmax_parts(scores, same):
    masked = jnp.where(same, scores, -1e30)
    centred = masked - jnp.max(masked, axis=-1, keepdims=True)
    grown = jnp.exp(centred)
    total = jnp.sum(grown, axis=-1, keepdims=True)
    return grown / total, centred, total


def same_item(row):
    wide = jnp.broadcast_to(row.astype(f32), (row.shape[1], row.shape[1]))
    return wide == wide.T


def normalise(values):
    centre = jnp.mean(values, axis=-1, keepdims=True)
    spread = values - centre
    second = jnp.mean(spread * spread, axis=-1, keepdims=True)
    inverse = lax.rsqrt(second + EPSILON)
    return spread * inverse, inverse


def norm_backward(grad, normed, inverse, gain):
    scaled = grad * gain
    first = jnp.mean(scaled, axis=-1, keepdims=True)
    second = jnp.mean(scaled * normed, axis=-1, keepdims=True)
    return inverse * (scaled - first - normed * second)


def column_sum(value):
    return jnp.sum(value.astype(f32), axis=0, keepdims=True)


def remote(src, dst, sems, device):
    return pltpu.make_async_remote_copy(
        src_ref=src, dst_ref=dst, send_sem=sems[0], recv_sem=sems[1],
        device_id=device, device_id_type=MESH,
    )


def layers_kernel(n_z, n_t, rows, width, cols, names, *refs):
    r = Bag(names, refs)
    heads, half_width = cols // HEAD_DIM, width // 2
    scale = HEAD_DIM**-0.5
    core, z, t = lax.axis_index("section"), lax.axis_index("dp"), lax.axis_index("tensor")
    other = {"section": 1 - core}
    step_x, step_y = 1 - 2 * lax.rem(t, 2), 2 - 4 * (t // 2)
    t_x, t_y = t + step_x, t + step_y
    t_far = t + step_x + step_y
    piece, own = rows // n_z, rows // n_t
    chunk_rows = max(piece, 128)
    chunks, per_chunk = rows // chunk_rows, chunk_rows // piece
    mine = rows_at(t, own)
    weights = ("wa", "wo", "wu", "wd")

    def load(i):
        if i < 2:
            return pltpu.make_async_copy(r.x_in.at[core * 2 + i], r.x.at[i], r.load_sem.at[i])
        if i < 4:
            return pltpu.make_async_copy(r.g_in.at[core * 2 + i - 2], r.g.at[i - 2], r.load_sem.at[i])
        if i == 5:
            return pltpu.make_async_copy(r.wo_in, r.wo.at[core, t], r.load_sem.at[i])
        name = weights[i - 4]
        return pltpu.make_async_copy(
            getattr(r, name + "_in"), getattr(r, name).at[core], r.load_sem.at[i]
        )

    def swap(i):
        sems = (r.swap_s.at[i], r.swap_r.at[i])
        if i == 4:
            return remote(r.idx.at[core], r.idx.at[core], sems, other)
        if i == 5:
            return remote(r.par.at[core], r.par.at[core], sems, other)
        if i == 1:
            return remote(r.wo_in, r.wo.at[core, t], sems, other)
        name = weights[i]
        return remote(getattr(r, name + "_in"), getattr(r, name).at[core], sems, other)

    def start():
        for i in (0, 4, 1, 5, 6, 7, 2, 3):
            load(i).start()
        for kind, index in enumerate((r.items_in, r.send_in, r.recv_in)):
            for i in range(4):
                for c in range(rows // 128):
                    cut = slice(c * 128, (c + 1) * 128)
                    row = index[i : i + 1, cut] if kind == 0 else index[i, :, cut]
                    r.idx[core, kind * 4 + i, c] = row
        r.par[core, 0:1, :] = jnp.zeros((1, width), f32)
        r.par[core, 0:1, :cols] = r.qv_in[0:1]
        r.par[core, 0:1, 2 * cols : 3 * cols] = r.qv_in[1:2]
        for first, value in ((1, r.bo_in), (2, r.norm1_in), (4, r.bu_in), (5, r.bd_in), (6, r.norm2_in)):
            r.par[core, first : first + value.shape[0], :] = value[...]
        r.vec[...] = jnp.zeros(r.vec.shape, f32)
        barrier = pltpu.get_barrier_semaphore()
        pl.semaphore_signal(barrier, inc=1, device_id=other, device_id_type=MESH)

        def greet_z(k):
            peer = lax.rem(z + 1 + k, n_z)
            pl.semaphore_signal(barrier, inc=1, device_id={"dp": peer}, device_id_type=MESH)

        def greet_t(k):
            peer = lax.rem(t + 1 + k, n_t)
            pl.semaphore_signal(barrier, inc=1, device_id={"tensor": peer}, device_id_type=MESH)

        loop(n_z - 1, greet_z)
        loop(n_t - 1, greet_t)
        pl.semaphore_wait(barrier, n_z + n_t - 1)
        for i in (4, 5, 0, 1):
            swap(i).start()
        for k in range(1, n_t):
            wo_copy(k).start()
        for i in (2, 3):
            swap(i).start()

    def need_small(layer):
        if layer in asked:
            return
        asked.add(layer)

        @pl.when(core != layer)
        def _():
            swap(4).wait_recv()
            swap(5).wait_recv()

    def wo_copy(k):
        return remote(
            r.wo_in, r.wo.at[core, t], (r.wt_s.at[k - 1], r.wt_r.at[k - 1]),
            {"tensor": lax.rem(t + k, n_t)},
        )

    def wo_on_copy(k):
        slab = r.wo.at[core, lax.rem(t - k + n_t, n_t)]
        return remote(slab, slab, (r.wc_s.at[k - 1], r.wc_r.at[k - 1]), other)

    def out_weight_on(l, m):
        load(5).wait()
        for k in range(1, n_t):
            wo_copy(k).wait_recv()
            wo_on_copy(k).start()

    asked = set()

    def need_weight(layer, i):
        if (layer, i) in asked:
            return
        asked.add((layer, i))

        if i != 1:

            @pl.when(core == layer)
            def _():
                load(4 + i).wait()

        @pl.when(core != layer)
        def _():
            swap(i).wait_recv()
            if i == 1:
                for k in range(1, n_t):
                    wo_on_copy(k).wait_recv()

    def index_cut(kind, layer, m, first, count):
        cuts = [
            r.idx[layer, kind * 4 + core * 2 + m, first // 128 + i] for i in range(count // 128)
        ]
        return cuts[0] if len(cuts) == 1 else jnp.concatenate(cuts, axis=1)

    def index_row(kind, layer, m):
        return index_cut(kind, layer, m, 0, rows)

    def par(layer, i, count=None):
        return r.par[layer, i : i + 1, : count or width]

    def z_copies(kind, m, k, src, dst, src_rest, dst_rest):
        peer = lax.rem(z + k, n_z)
        full = src.shape[1] // 128 * 128
        lanes = pl.ds(0, full)
        return [
            remote(
                src.at[rows_at(peer, piece), lanes], dst.at[rows_at(z, piece), lanes],
                (r.z_s.at[2 * kind, m, k - 1], r.z_r.at[2 * kind, m, k - 1]), {"dp": peer},
            ),
            remote(
                src_rest.at[peer], dst_rest.at[z],
                (r.z_s.at[2 * kind + 1, m, k - 1], r.z_r.at[2 * kind + 1, m, k - 1]), {"dp": peer},
            ),
        ]

    def z_chunk(kk):
        return lax.rem(z // per_chunk + 1 + kk, chunks)

    def z_send(kind, m, cc, rest, *refs):
        rest = rest.astype(f32)
        for j in range(per_chunk):
            upper = rest[j * piece : j * piece + piece // 2]
            lower = rest[j * piece + piece // 2 : (j + 1) * piece]
            refs[2][cc * per_chunk + j] = jnp.concatenate([upper, lower], axis=1).astype(bf16)

        def one(j):
            peer = cc * per_chunk + j
            k = lax.rem(peer - z + n_z, n_z)

            @pl.when(k > 0)
            def _():
                for copy in z_copies(kind, m, k, *refs):
                    copy.start()

        loop(per_chunk, one)

    def z_take(kind, m, src, dst, src_rest, dst_rest):
        def wait(k):
            for copy in z_copies(kind, m, k + 1, src, dst, src_rest, dst_rest):
                copy.wait()

        loop(n_z - 1, wait)
        full = src.shape[1] // 128 * 128
        here = rows_at(z, piece)
        dst[here, :full] = src[here, :full]
        dst_rest[z] = src_rest[z]

        def unpack(b):
            both = dst_rest[b].astype(f32)
            whole = jnp.concatenate([both[:, :HEAD_DIM], both[:, HEAD_DIM:]], axis=0)
            dst[rows_at(b, piece), full:] = whole.astype(bf16)

        loop(n_z, unpack)

    left, right = slice(0, half_width), slice(half_width, width)

    def sum_copy(m, j):
        peer = t_x if j in (0, 1, 5) else t_y
        return remote(
            r.sum_src.at[m, j], r.sum_dst.at[m, j], (r.sum_s.at[m, j], r.sum_r.at[m, j]),
            {"tensor": peer},
        )

    def sum_put(m, role, part):
        @pl.when(role == 0)
        def _():
            r.sum_own[m] = part

        @pl.when(role == 1)
        def _():
            r.sum_src[m, 1] = part[:, left].astype(bf16)
            r.sum_keep[m, 1] = part[:, right].astype(bf16)
            sum_copy(m, 1).start()

        @pl.when(role == 2)
        def _():
            r.sum_src[m, 3] = part[:, right].astype(bf16)
            r.sum_keep[m, 0] = part[:, left].astype(bf16)
            sum_copy(m, 3).start()

        @pl.when(role == 3)
        def _():
            r.sum_src[m, 0] = part[:, left].astype(bf16)
            sum_copy(m, 0).start()
            r.sum_src[m, 2] = part[:, right].astype(bf16)
            sum_copy(m, 2).start()

    def sum_mid(m):
        sum_copy(m, 0).wait_recv()
        r.sum_src[m, 4] = (r.sum_keep[m, 0].astype(f32) + r.sum_dst[m, 0].astype(f32)).astype(bf16)
        sum_copy(m, 4).start()
        sum_copy(m, 2).wait_recv()
        r.sum_src[m, 5] = (r.sum_keep[m, 1].astype(f32) + r.sum_dst[m, 2].astype(f32)).astype(bf16)
        sum_copy(m, 5).start()

    def sum_take(m):
        for j in (1, 3, 4, 5):
            sum_copy(m, j).wait_recv()
        for j in range(6):
            sum_copy(m, j).wait_send()
        added = jnp.concatenate(
            [
                r.sum_dst[m, 1].astype(f32) + r.sum_dst[m, 4].astype(f32),
                r.sum_dst[m, 3].astype(f32) + r.sum_dst[m, 5].astype(f32),
            ],
            axis=1,
        )
        return r.sum_own[m] + added

    def role_rows(role):
        return rows_at(t + lax.rem(role, 2) * step_x + (role // 2) * step_y, own)

    def gather_copy(kind, m, j, buf):
        first = (t, t, t, t, t_x, t_y)[j] * own
        low = j in (1, 2, 5)
        here = pl.ds(pl.multiple_of(first + (own // 2 if low else 0), own // 2), own // 2)
        return remote(
            buf.at[here], buf.at[here], (r.gather_s.at[kind, m, j], r.gather_r.at[kind, m, j]),
            {"tensor": t_x if j in (0, 1, 5) else t_y},
        )

    def gather_start(kind, m, buf):
        for j in (0, 2, 1, 3):
            gather_copy(kind, m, j, buf).start()

    def gather_on(kind, m, buf):
        gather_copy(kind, m, 0, buf).wait_recv()
        gather_copy(kind, m, 4, buf).start()
        gather_copy(kind, m, 2, buf).wait_recv()
        gather_copy(kind, m, 5, buf).start()

    def gather_near(kind, m, buf, j):
        gather_copy(kind, m, j, buf).wait_recv()

    def gather_far(kind, m, buf):
        gather_copy(kind, m, 4, buf).wait_recv()
        gather_copy(kind, m, 5, buf).wait_recv()

    def gather_rest(kind, m, buf):
        for j in (1, 3, 4, 5):
            gather_copy(kind, m, j, buf).wait_recv()
        gather_sent(kind, m, buf)

    def gather_sent(kind, m, buf):
        for j in range(6):
            gather_copy(kind, m, j, buf).wait_send()

    def gather_step(kind, m, role, buf):
        @pl.when(role == 1)
        def _():
            gather_on(kind, m, buf)
            gather_near(kind, m, buf, 1)

        @pl.when(role == 2)
        def _():
            gather_near(kind, m, buf, 3)

        @pl.when(role == 3)
        def _():
            gather_far(kind, m, buf)

    def out_local(kind, m, src, out):
        return pltpu.make_async_copy(src, out.at[core * 2 + m], r.out_l.at[kind, m])

    def out_away(kind, m, src, out):
        return remote(src, out.at[core * 2 + m], (r.out_s.at[kind, m], r.out_r.at[kind, m]), other)

    def out_start(kind, layer, m, src, out):
        @pl.when(core == layer)
        def _():
            out_local(kind, m, src, out).start()

        @pl.when(core != layer)
        def _():
            out_away(kind, m, src, out).start()

    def out_wait(kind, layer, m, src, out):
        @pl.when(core == layer)
        def _():
            out_local(kind, m, src, out).wait()

        @pl.when(core != layer)
        def _():
            out_away(kind, m, src, out).wait_send()

    rest_z, rest_m = 3 * cols - HEAD_DIM, cols - HEAD_DIM

    def z_big(m):
        return r.zs.at[m], r.zr.at[m], r.zs_rest.at[m], r.zr_rest.at[m]

    def z_home(m):
        return r.dmr.at[m], r.ms.at[m], r.ms_rest.at[m], r.mr_rest.at[m]

    def z_back(m):
        return r.dmt.at[m], r.dmr.at[m], r.ms_rest.at[m], r.mr_rest.at[m]

    def project(l, m):
        need_small(l)
        need_weight(l, 0)
        if l == 0:
            load(m).wait()

        def chunk(kk):
            cc = z_chunk(kk)
            here = rows_at(cc, chunk_rows)
            numbers = lax.broadcasted_iota(jnp.int32, (rows, chunk_rows), 0)
            pick = (numbers == index_cut(1, l, m, cc * chunk_rows, chunk_rows)).astype(bf16)
            moved = tn(pick, r.x[m]).astype(bf16)
            r.xp[l, m, here] = moved
            block = (nt(moved, r.wa[l]) + par(l, 0, 3 * cols)).astype(bf16)
            r.zs[m, here] = block[:, :rest_z]
            z_send(0, m, cc, block[:, rest_z:], *z_big(m))

        loop(chunks, chunk)

    def attend(l, m):
        z_take(0, m, *z_big(m))
        lane = lax.broadcasted_iota(jnp.int32, (1, 128), 1)

        def cluster(c):
            here = rows_at(c, CLUSTER)
            numbers = lax.broadcasted_iota(jnp.int32, (rows, CLUSTER), 0)
            pick = (numbers == index_cut(2, l, m, c * CLUSTER, CLUSTER)).astype(bf16)
            block = tn(pick, r.zr[m]).astype(bf16)
            r.grouped[l, m, here] = block
            queries, keys, values = (block[:, i * cols : (i + 1) * cols] for i in range(3))
            scores = nt(queries, by_head(keys, heads)) * scale
            same = same_item(index_cut(0, l, m, c * CLUSTER, CLUSTER))
            probs = []
            log_row = jnp.zeros((1, 128), f32)
            for h in range(heads):
                cut = slice(h * CLUSTER, (h + 1) * CLUSTER)
                prob, centred, total = softmax_parts(scores[:, cut], same)
                inner = jnp.sum(jnp.where(same, prob * centred, 0.0), axis=-1, keepdims=True)
                entropy = jnp.mean(jnp.log(total) - inner, axis=0, keepdims=True)
                log_row = jnp.where(lane == h, entropy, log_row)
                probs.append(prob.astype(bf16))
            r.entropy[l, m, pl.ds(c, 1)] = log_row
            mixed = nn(jnp.concatenate(probs, axis=1), by_head(values, heads))
            r.dmt[m, here] = mixed.astype(bf16)

        loop(rows // CLUSTER, cluster)

        def home(kk):
            cc = z_chunk(kk)
            here = rows_at(cc, chunk_rows)
            one_hot = place_rows(index_row(2, l, m), cc * chunk_rows, chunk_rows)
            block = nn(one_hot, r.dmt[m]).astype(bf16)
            r.dmr[m, here] = block
            z_send(1, m, cc, block[:, rest_m:], *z_home(m))

        loop(chunks, home)

    def heads_copy(l, m, k):
        peer = lax.rem(t + k, n_t)
        return remote(
            r.ms.at[m, rows_at(peer, own)], r.mt.at[l, m, t],
            (r.ta_s.at[m, k - 1], r.ta_r.at[m, k - 1]), {"tensor": peer},
        )

    def out_project(l, m):
        z_take(1, m, *z_home(m))
        for k in (2, 1, 3):
            heads_copy(l, m, k).start()
        r.mt[l, m, t] = r.ms[m, mine]

    def middle(l, m):
        sum_mid(m)

    def first_norm(l, m):
        need_weight(l, 1)
        for k in range(1, n_t):
            heads_copy(l, m, k).wait()
        total = r.xp[l, m, mine].astype(f32) + par(l, 1)
        for s in range(n_t):
            total = total + nn(r.mt[l, m, s], r.wo[l, s])
        normed, inverse = normalise(total)
        hidden = normed * par(l, 2) + par(l, 3)
        r.n1[l, m] = normed.astype(bf16)
        r.inv1[l, m] = jnp.broadcast_to(inverse, (own, 128))
        r.hid[m] = hidden
        r.hfull[l, m, mine] = hidden.astype(bf16)
        gather_start(0, m, r.hfull.at[l, m])

    def feed(l, m):
        need_weight(l, 2)
        need_weight(l, 3)

        def part(role):
            gather_step(0, m, role, r.hfull.at[l, m])
            here = role_rows(role)
            up = nn(r.hfull[l, m, here], r.wu[l]) + par(l, 4)
            square = up * up
            tanh = jnp.tanh(0.7978845608028654 * up * (1.0 + 0.044715 * square))
            half = 0.5 * (1.0 + tanh)
            slope = 0.7978845608028654 * (1.0 + 3 * 0.044715 * square)
            r.gp[l, m, here] = (half + 0.5 * up * (1.0 - tanh * tanh) * slope).astype(bf16)
            active = (up * half).astype(bf16)
            r.act[l, m, here] = active
            sum_put(m, role, nn(active, r.wd[l]))

        loop(n_t, part)

    def second_norm(l, m):
        gather_sent(0, m, r.hfull.at[l, m])
        total = sum_take(m) + par(l, 5)
        normed, inverse = normalise(r.hid[m] + total)
        r.n2[l, m] = normed.astype(bf16)
        r.inv2[l, m] = jnp.broadcast_to(inverse, (own, 128))
        r.ag[m, mine] = (normed * par(l, 6) + par(l, 7)).astype(bf16)
        gather_start(1, m, r.ag.at[m])

    def out_on(l, m):
        gather_on(1, m, r.ag.at[m])

    def to_tokens(l, m, dst, buf):
        def chunk(cc):
            one_hot = place_rows(index_row(1, l, m), cc * 128, 128)
            dst[m, rows_at(cc, 128)] = nn(one_hot, buf[m]).astype(bf16)

        loop(rows // 128, chunk)

    def out_tokens(l, m):
        gather_rest(1, m, r.ag.at[m])
        if l == 1:
            out_wait(0, 0, m, r.x.at[m], r.acts)
        to_tokens(l, m, r.x, r.ag)
        out_start(0, l, m, r.x.at[m], r.acts)

    def add_vec(l, index, value):
        r.vec[l, index : index + 1, : value.shape[1]] += value

    def b_second_norm(l, m):
        if l == 1:
            load(2 + m).wait()
        numbers = lax.broadcasted_iota(jnp.int32, (rows, own), 0)
        pick = (numbers == index_cut(1, l, m, t * own, own)).astype(bf16)
        up = tn(pick, r.g[m])
        normed = r.n2[l, m].astype(f32)
        down = norm_backward(up, normed, r.inv2[l, m][:, :1], par(l, 6))
        r.hid[m] = down
        low = down.astype(bf16)
        r.db[m, mine] = low
        gather_start(2, m, r.db.at[m])
        add_vec(l, 0, column_sum(up * normed))
        add_vec(l, 1, column_sum(up))
        add_vec(l, 2, column_sum(low))

    def b_feed(l, m):
        def part(role):
            gather_step(2, m, role, r.db.at[m])
            here = role_rows(role)
            low = (nt(r.db[m, here], r.wd[l]) * r.gp[l, m, here].astype(f32)).astype(bf16)
            r.gp[l, m, here] = low
            sum_put(m, role, nt(low, r.wu[l]))

        loop(n_t, part)

    def grad_slabs(ref, value, lanes):
        ref[:, :, lanes] = value.reshape(n_z, width // n_z, value.shape[1]).astype(bf16)

    def feed_weights(l, m):
        for i in range(2):
            gather_sent(2, i, r.db.at[i])
            add_vec(l, 6, column_sum(r.gp[l, i]))

        def block(c):
            cut = rows_at(c, 256)
            up = tn(r.hfull[l, 0], r.gp[l, 0, :, cut]) + tn(r.hfull[l, 1], r.gp[l, 1, :, cut])
            grad_slabs(r.gs_feed, up, cut)
            down = tn(r.db[0], r.act[l, 0, :, cut]) + tn(r.db[1], r.act[l, 1, :, cut])
            grad_slabs(r.gs_feed, down, pl.ds(pl.multiple_of(width + c * 256, 256), 256))

        loop(width // 256, block)
        grads_send(0, l, r.gs_feed, r.gr_feed)

    def b_first_norm(l, m):
        up = r.hid[m] + sum_take(m)
        normed = r.n1[l, m].astype(f32)
        down = norm_backward(up, normed, r.inv1[l, m][:, :1], par(l, 2))
        r.dres[m] = down
        low = down.astype(bf16)
        r.da[m] = low

        def part(kk):
            k = lax.rem(kk + 1, n_t)
            peer = lax.rem(t + k, n_t)
            block = nt(low, r.wo[l, peer]).astype(bf16)

            @pl.when(k > 0)
            def _():
                r.ms[m, rows_at(peer, own)] = block
                rows_copy(m, k).start()

            @pl.when(k == 0)
            def _():
                r.dmt[m, mine] = block

        loop(n_t, part)
        add_vec(l, 3, column_sum(up * normed))
        add_vec(l, 4, column_sum(up))
        add_vec(l, 5, column_sum(low))

    def rows_copy(m, k):
        peer = lax.rem(t + k, n_t)
        return remote(
            r.ms.at[m, rows_at(peer, own)], r.dmt.at[m, mine], (r.tb_s.at[m, k - 1], r.tb_r.at[m, k - 1]),
            {"tensor": peer},
        )

    def out_back(l, m):
        for k in range(1, n_t):
            rows_copy(m, k).wait()

        def chunk(kk):
            cc = z_chunk(kk)
            z_send(2, m, cc, r.dmt[m, rows_at(cc, chunk_rows), rest_m:], *z_back(m))

        loop(chunks, chunk)

    def out_weights(l, m):
        for s in range(n_t):
            value = tn(r.da[0], r.mt[l, 0, s]) + tn(r.da[1], r.mt[l, 1, s])
            r.gs_out[s] = value.reshape(n_z, width // n_z, cols).astype(bf16)

        @pl.when(core != l)
        def _():
            for k in range(n_t):
                out_core_copy(lax.rem(t + 1 + k, n_t)).start()

    def b_attend(l, m):
        z_take(2, m, *z_back(m))

        def cluster(c):
            here = rows_at(c, CLUSTER)
            numbers = lax.broadcasted_iota(jnp.int32, (rows, CLUSTER), 0)
            pick = (numbers == index_cut(2, l, m, c * CLUSTER, CLUSTER)).astype(bf16)
            dmix = tn(pick, r.dmr[m]).astype(bf16)
            block = r.grouped[l, m, here]
            queries, keys, values = (block[:, i * cols : (i + 1) * cols] for i in range(3))
            keys_by_head = by_head(keys, heads)
            scores = nt(queries, keys_by_head) * scale
            same = same_item(index_cut(0, l, m, c * CLUSTER, CLUSTER))
            dprob = nt(dmix, by_head(values, heads))
            probs, dscores = [], []
            for h in range(heads):
                cut = slice(h * CLUSTER, (h + 1) * CLUSTER)
                prob = softmax_parts(scores[:, cut], same)[0]
                outer = prob * dprob[:, cut]
                dscore = outer - prob * jnp.sum(outer, axis=-1, keepdims=True)
                probs.append(prob.astype(bf16))
                dscores.append(dscore.astype(bf16))
            prob_all = jnp.concatenate(probs, axis=1)
            dscore_all = jnp.concatenate(dscores, axis=1)
            dqueries = nn(dscore_all, keys_by_head) * scale
            dkeys = fold_heads(tn(dscore_all, queries), heads) * scale
            dvalues = fold_heads(tn(prob_all, dmix), heads)
            r.grouped[l, m, here] = jnp.concatenate([dqueries, dkeys, dvalues], axis=1).astype(bf16)

        loop(rows // CLUSTER, cluster)

        def home(kk):
            cc = z_chunk(kk)
            here = rows_at(cc, chunk_rows)
            one_hot = place_rows(index_row(2, l, m), cc * chunk_rows, chunk_rows)
            block = nn(one_hot, r.grouped[l, m]).astype(bf16)
            r.zs[m, here] = block[:, :rest_z]
            z_send(3, m, cc, block[:, rest_z:], *z_big(m))

        loop(chunks, home)

    def in_project(l, m):
        z_take(3, m, *z_big(m))

        def part(kk):
            role = 3 - kk
            sum_put(m, role, nn(r.zr[m, role_rows(role)], r.wa[l]))

        loop(n_t, part)

    def in_weights(l, m):
        for i in range(2):
            add_vec(l, 7, column_sum(r.zr[i]))
        for first in range(0, 3 * cols, 256):
            cut = slice(first, min(first + 256, 3 * cols))
            value = tn(r.xp[l, 0], r.zr[0, :, cut]) + tn(r.xp[l, 1], r.zr[1, :, cut])
            grad_slabs(r.gs_attn, value, cut)
        grads_send(1, l, r.gs_attn, r.gr_attn)

    def layer_input(l, m):
        r.ag[m, mine] = (r.dres[m] + sum_take(m)).astype(bf16)
        gather_start(4, m, r.ag.at[m])

    def b_out_on(l, m):
        gather_on(4, m, r.ag.at[m])

    def b_tokens(l, m):
        gather_rest(4, m, r.ag.at[m])
        if l == 0:
            out_wait(1, 1, m, r.g.at[m], r.grads)
        to_tokens(l, m, r.g, r.ag)
        out_start(1, l, m, r.g.at[m], r.grads)

    def grad_core_copy(kind, k, src, dst):
        return remote(src.at[k], dst.at[k], (r.gc_s.at[kind, k], r.gc_r.at[kind, k]), other)

    def grad_z_copy(kind, k, src, dst, lanes=slice(None)):
        peer = lax.rem(z + k, n_z)
        return remote(
            src.at[peer, :, lanes], dst.at[k - 1, :, lanes], (r.gz_s.at[kind, k - 1], r.gz_r.at[kind, k - 1]),
            {"dp": peer},
        )

    def grads_send(kind, l, src, dst):
        @pl.when(core != l)
        def _():
            loop(n_z, lambda k: grad_core_copy(kind, lax.rem(z + 1 + k, n_z), src, dst).start())

    def grads_add(kind, src, came, k, wait, lanes):
        peer = lax.rem(z + k, n_z)
        if wait:
            grad_core_copy(kind, peer, src, came).wait_recv()
        total = src[peer, :, lanes].astype(f32) + came[peer, :, lanes].astype(f32)
        src[peer, :, lanes] = total.astype(bf16)

    def grads_part(kind, sem, l, src, came, dst, part, wait, lanes):
        @pl.when(core == l)
        def _():
            first, last = part * (n_z - 1) // 3, (part + 1) * (n_z - 1) // 3

            def one(i):
                grads_add(kind, src, came, first + 1 + i, wait, lanes)
                grad_z_copy(sem, first + 1 + i, src, dst, lanes).start()

            loop(last - first, one)

    def grads_end(kind, sems, l, src, came, dst, outs):
        @pl.when(core == l)
        def _():
            lanes = src.shape[2] // len(sems)
            for i in range(len(sems)):
                grads_add(kind, src, came, 0, i == 0, slice(i * lanes, (i + 1) * lanes))
            cuts, first = [], 0
            for out in outs:
                cuts.append(slice(first, first + out.shape[-1]))
                first += out.shape[-1]
            for out, cut in zip(outs, cuts):
                out[...] = src[z, :, cut].astype(f32)

            def one(k):
                for i, sem in enumerate(sems):
                    grad_z_copy(sem, k + 1, src, dst, slice(i * lanes, (i + 1) * lanes)).wait()
                for out, cut in zip(outs, cuts):
                    out[...] += dst[k, :, cut].astype(f32)

            loop(n_z - 1, one)

        @pl.when(core != l)
        def _():
            loop(n_z, lambda k: grad_core_copy(kind, k, src, came).wait_send())

    def line_copy(half, c, slot, step):
        lanes = slice(half * width, (half + 1) * width)
        return remote(
            r.gs_feed.at[c, :, lanes], r.gz_feed.at[slot, :, lanes],
            (r.line_s.at[half, c], r.line_r.at[half, slot]), {"dp": z + step},
        )

    def line_add(half, c, slot, came):
        lanes = slice(half * width, (half + 1) * width)
        grads_add(0, r.gs_feed, r.gr_feed, c - z, half == 0, lanes)

        @pl.when(came)
        def _():
            line_copy(half, c, slot, 0).wait_recv()
            total = r.gs_feed[c, :, lanes].astype(f32) + r.gz_feed[slot, :, lanes].astype(f32)
            r.gs_feed[c, :, lanes] = total.astype(bf16)

    def line_part(half, part, l):
        @pl.when(core == l)
        def _():
            first, last = part * (n_z - 1) // 3, (part + 1) * (n_z - 1) // 3

            def one(i):
                far = n_z - 1 - first - i

                @pl.when(z + far < n_z)
                def _():
                    line_add(half, z + far, z + far, z > 0)
                    line_copy(half, z + far, z + far, 1).start()

                @pl.when(z - far >= 0)
                def _():
                    line_add(half, z - far, z - far, z < n_z - 1)
                    slot = jnp.where(far == 1, n_z, z - far)
                    line_copy(half, z - far, slot, -1).start()

            loop(last - first, one)

    def line_end(l):
        @pl.when(core == l)
        def _():
            for half, out in enumerate((r.g_up, r.g_down)):
                lanes = slice(half * width, (half + 1) * width)
                line_add(half, z, z, z > 0)
                out[...] = r.gs_feed[z, :, lanes].astype(f32)

                @pl.when(z < n_z - 1)
                def _():
                    line_copy(half, z, n_z, 0).wait_recv()
                    out[...] += r.gz_feed[n_z, :, lanes].astype(f32)

                def sent(k):
                    line_copy(half, lax.rem(z + 1 + k, n_z), 0, 0).wait_send()

                loop(n_z - 1, sent)

        @pl.when(core != l)
        def _():
            loop(n_z, lambda k: grad_core_copy(0, k, r.gs_feed, r.gr_feed).wait_send())

    def feed_part(i):
        return lambda l, m: line_part(i % 2, i // 2, l)

    def attn_part(i):
        return lambda l, m: grads_part(
            1, 2, l, r.gs_attn, r.gr_attn, r.gz_attn, i, True, slice(None)
        )

    feed_0, feed_1, feed_2, feed_3, feed_4, feed_5 = (feed_part(i) for i in range(6))
    attn_0, attn_1, attn_2 = (attn_part(i) for i in range(3))

    def feed_end(l, m):
        line_end(l)

    def attn_end(l, m):
        grads_end(1, (2,), l, r.gs_attn, r.gr_attn, r.gz_attn, tuple(r.g_attn.at[i] for i in range(3)))

    def out_core_copy(s):
        return remote(r.gs_out.at[s], r.gr_out.at[s], (r.oc_s.at[s], r.oc_r.at[s]), other)

    def out_t_copy(k):
        peer = lax.rem(t + k, n_t)
        return remote(
            r.gs_out.at[peer], r.gt_out.at[k - 1], (r.ot_s.at[k - 1], r.ot_r.at[k - 1]),
            {"tensor": peer},
        )

    def out_z_copy(k):
        peer = lax.rem(z + k, n_z)
        return remote(
            r.gs_out.at[t, peer], r.gz_out.at[k - 1], (r.gz_s.at[3, k - 1], r.gz_r.at[3, k - 1]),
            {"dp": peer},
        )

    def out_sum_t(l, m):
        @pl.when(core == l)
        def _():
            for kk in range(n_t):
                k = (kk + 1) % n_t
                s = lax.rem(t + k, n_t)
                out_core_copy(s).wait_recv()
                r.gs_out[s] = (r.gs_out[s].astype(f32) + r.gr_out[s].astype(f32)).astype(bf16)
                if k > 0:
                    out_t_copy(k).start()

    def out_sum_z(l, m):
        @pl.when(core == l)
        def _():
            for k in range(1, n_t):
                out_t_copy(k).wait()
            total = r.gs_out[t].astype(f32)
            for k in range(1, n_t):
                total = total + r.gt_out[k - 1].astype(f32)
            r.gs_out[t] = total.astype(bf16)
            loop(n_z - 1, lambda k: out_z_copy(k + 1).start())

        @pl.when(core != l)
        def _():
            for s in range(n_t):
                out_core_copy(s).wait_send()

    def out_end(l, m):
        @pl.when(core == l)
        def _():
            r.g_out[...] = r.gs_out[t, z].astype(f32)

            def one(k):
                out_z_copy(k + 1).wait()
                r.g_out[...] += r.gz_out[k].astype(f32)

            loop(n_z - 1, one)

    def vec_copy(l):
        return remote(r.vec.at[l], r.vec_came, (r.vc_s.at[0], r.vc_r.at[0]), other)

    def vec_t_copy(k):
        return remote(
            r.vec_t.at[t], r.vec_t.at[t], (r.vt_s.at[k - 1], r.vt_r.at[k - 1]),
            {"tensor": lax.rem(t + k, n_t)},
        )

    def vec_z_copy(k):
        return remote(
            r.vec_z.at[z], r.vec_z.at[z], (r.vz_s.at[k - 1], r.vz_r.at[k - 1]),
            {"dp": lax.rem(z + k, n_z)},
        )

    def entropy_copy(l, m):
        return remote(
            r.entropy.at[l, m], r.ent.at[core * 2 + m], (r.en_s.at[m], r.en_r.at[m]), other
        )

    def vec_start(l, m):
        @pl.when(core != l)
        def _():
            vec_copy(l).start()
            for i in range(2):
                entropy_copy(l, i).start()

    def vec_sum_t(l, m):
        @pl.when(core == l)
        def _():
            for i in range(2):
                r.ent[core * 2 + i] = r.entropy[l, i]
            vec_copy(l).wait_recv()
            r.vec_t[t] = r.vec[l] + r.vec_came[...]
            for k in range(1, n_t):
                vec_t_copy(k).start()

    def vec_sum_z(l, m):
        @pl.when(core == l)
        def _():
            for k in range(1, n_t):
                vec_t_copy(k).wait()
            total = r.vec_t[0]
            for k in range(1, n_t):
                total = total + r.vec_t[k]
            lane_rows = lax.broadcasted_iota(jnp.int32, total.shape, 0)
            r.vec_z[z] = jnp.where(lane_rows < 6, total, r.vec_t[t])
            loop(n_z - 1, lambda k: vec_z_copy(k + 1).start())

    def vec_end(l, m):
        @pl.when(core == l)
        def _():
            loop(n_z - 1, lambda k: vec_z_copy(k + 1).wait())
            r.vec_out[...] = r.vec_z[0]

            def one(k):
                r.vec_out[...] += r.vec_z[k + 1]

            loop(n_z - 1, one)

        @pl.when(core != l)
        def _():
            vec_copy(l).wait_send()
            for i in range(2):
                entropy_copy(l, i).wait_send()

    def finish():
        for m in range(2):
            out_wait(0, 1, m, r.x.at[m], r.acts)
            out_wait(1, 0, m, r.g.at[m], r.grads)
            for kind, out, src in ((0, r.acts, r.x), (1, r.grads, r.g)):
                out_away(kind, m, src.at[m], out).wait_recv()
            entropy_copy(0, m).wait_recv()
        for i in range(6):
            swap(i).wait_send()
        for k in range(1, n_t):
            wo_copy(k).wait_send()
            wo_on_copy(k).wait_send()

    schedule = (
        (project, 0, 1), (attend, 0, 1), (out_weight_on, 0, 0), (out_project, 0, 1), (project, 0, 0),
        (first_norm, 0, 1), (feed, 0, 1), (attend, 0, 0), (middle, 0, 1), (out_project, 0, 0),
        (second_norm, 0, 1), (out_on, 0, 1), (first_norm, 0, 0), (out_tokens, 0, 1), (project, 1, 1),
        (feed, 0, 0), (middle, 0, 0), (attend, 1, 1), (second_norm, 0, 0), (out_project, 1, 1),
        (out_on, 0, 0), (first_norm, 1, 1), (out_tokens, 0, 0), (project, 1, 0), (feed, 1, 1), (middle, 1, 1),
        (attend, 1, 0), (second_norm, 1, 1), (b_second_norm, 1, 1), (out_on, 1, 1), (out_project, 1, 0),
        (b_feed, 1, 1), (first_norm, 1, 0), (out_tokens, 1, 1), (middle, 1, 1), (feed, 1, 0),
        (b_first_norm, 1, 1), (middle, 1, 0), (out_back, 1, 1), (second_norm, 1, 0), (b_second_norm, 1, 0),
        (b_attend, 1, 1), (out_on, 1, 0), (b_feed, 1, 0), (in_project, 1, 1), (feed_weights, 1, 1),
        (middle, 1, 0), (middle, 1, 1), (b_first_norm, 1, 0), (out_weights, 1, 1), (layer_input, 1, 1),
        (out_back, 1, 0), (b_out_on, 1, 1), (b_tokens, 1, 1), (b_second_norm, 0, 1), (feed_0, 1, 1),
        (feed_1, 1, 1), (b_attend, 1, 0), (b_feed, 0, 1), (out_sum_t, 1, 1), (out_tokens, 1, 0),
        (feed_2, 1, 1), (in_project, 1, 0), (middle, 0, 1), (middle, 1, 0), (in_weights, 1, 1),
        (feed_3, 1, 1), (feed_4, 1, 1), (b_first_norm, 0, 1), (layer_input, 1, 0), (out_sum_z, 1, 1),
        (out_back, 0, 1), (b_out_on, 1, 0), (vec_start, 1, 1), (feed_5, 1, 1), (attn_0, 1, 1),
        (out_end, 1, 1), (b_tokens, 1, 0), (b_second_norm, 0, 0), (b_attend, 0, 1), (vec_sum_t, 1, 1),
        (feed_end, 1, 1), (b_feed, 0, 0), (attn_1, 1, 1), (feed_weights, 0, 1), (feed_0, 0, 1),
        (middle, 0, 0), (vec_sum_z, 1, 1), (feed_1, 0, 1), (in_project, 0, 1), (attn_2, 1, 1),
        (b_first_norm, 0, 0), (out_weights, 0, 1), (feed_2, 0, 1), (middle, 0, 1), (vec_end, 1, 1),
        (out_sum_t, 0, 1), (out_back, 0, 0), (feed_3, 0, 1), (b_attend, 0, 0), (layer_input, 0, 1),
        (feed_4, 0, 1), (out_sum_z, 0, 1), (attn_end, 1, 1), (in_project, 0, 0), (in_weights, 0, 1),
        (b_out_on, 0, 1), (vec_start, 0, 1), (attn_0, 0, 1), (attn_1, 0, 1), (attn_2, 0, 1),
        (vec_sum_t, 0, 1), (middle, 0, 0), (layer_input, 0, 0), (b_tokens, 0, 1), (feed_5, 0, 1),
        (b_out_on, 0, 0), (vec_sum_z, 0, 1), (out_end, 0, 1), (b_tokens, 0, 0), (attn_end, 0, 1),
        (feed_end, 0, 1), (vec_end, 0, 1),
    )
    start()
    for step, layer, micro in schedule:
        step(layer, micro)
    finish()


def run_layers(n_z, x, g, small, wa, wo, wu, wd):
    micros, rows, width = x.shape
    cols, hidden = wo.shape[0], wu.shape[1]
    n_t = lax.axis_size("tensor")
    own, slab = rows // n_t, width // n_z
    pair = (2, rows)
    both = (2, 2, rows)
    anywhere, vmem = pl.BlockSpec(memory_space=pl.ANY), pl.BlockSpec(memory_space=pltpu.VMEM)
    ins = dict(
        x_in=anywhere, g_in=anywhere, items_in=vmem, send_in=vmem, recv_in=vmem, qv_in=vmem,
        bo_in=vmem, norm1_in=vmem, bu_in=vmem, bd_in=vmem, norm2_in=vmem, wa_in=anywhere, wo_in=anywhere,
        wu_in=anywhere, wd_in=anywhere,
    )
    outs = dict(
        acts=(anywhere, x.shape, bf16), grads=(anywhere, x.shape, bf16),
        g_up=(vmem, (slab, width), f32), g_down=(vmem, (slab, width), f32),
        g_attn=(vmem, (3, slab, cols), f32),
        g_out=(vmem, (slab, cols), f32),
        vec_out=(vmem, (8, width), f32), ent=(vmem, (micros, max(8, rows // CLUSTER), 128), f32),
    )
    sem = pltpu.SemaphoreType.DMA
    scratch = dict(
        x=((*pair, width), bf16), g=((*pair, width), bf16),
        wa=((2, 3 * cols, width), bf16), wo=((2, n_t, cols, width), bf16),
        wu=((2, width, hidden), bf16), wd=((2, hidden, width), bf16),
        idx=((2, 12, rows // 128, 1, 128), jnp.int32), par=((2, 8, width), f32),
        xp=((*both, width), bf16), grouped=((*both, 3 * cols), bf16), ms=((*pair, cols), bf16),
        mt=((2, 2, n_t, own, cols), bf16),
        n1=((2, 2, own, width), bf16), inv1=((2, 2, own, 128), f32), hfull=((*both, width), bf16),
        act=((*both, hidden), bf16), gp=((*both, hidden), bf16),
        n2=((2, 2, own, width), bf16), inv2=((2, 2, own, 128), f32),
        entropy=((2, 2, max(8, rows // CLUSTER), 128), f32),
        zs=((*pair, 3 * cols - HEAD_DIM), bf16), zs_rest=((2, n_z, rows // n_z // 2, 128), bf16),
        zr_rest=((2, n_z, rows // n_z // 2, 128), bf16), ms_rest=((2, n_z, rows // n_z // 2, 128), bf16),
        mr_rest=((2, n_z, rows // n_z // 2, 128), bf16), zr=((*pair, 3 * cols), bf16),
        dmr=((*pair, cols), bf16),
        sum_src=((2, 6, own, width // 2), bf16), sum_dst=((2, 6, own, width // 2), bf16),
        sum_keep=((2, 2, own, width // 2), bf16), sum_own=((2, own, width), f32),
        hid=((2, own, width), f32), dres=((2, own, width), f32),
        ag=((*pair, width), bf16), db=((*pair, width), bf16), da=((2, own, width), bf16),
        dmt=((*pair, cols), bf16),
        gs_feed=((n_z, slab, 2 * width), bf16), gr_feed=((n_z, slab, 2 * width), bf16),
        gz_feed=((n_z + 1, slab, 2 * width), bf16),
        gs_attn=((n_z, slab, 3 * cols), bf16), gr_attn=((n_z, slab, 3 * cols), bf16),
        gz_attn=((n_z - 1, slab, 3 * cols), bf16),
        gs_out=((n_t, n_z, slab, cols), bf16), gr_out=((n_t, n_z, slab, cols), bf16),
        gt_out=((n_t - 1, n_z, slab, cols), bf16), gz_out=((n_z - 1, slab, cols), bf16),
        vec=((2, 8, width), f32), vec_came=((8, width), f32), vec_t=((n_t, 8, width), f32),
        vec_z=((n_z, 8, width), f32),
    )
    sems = dict(load_sem=(8,))
    for name, shape in dict(
        swap=(6,), z=(8, 2, n_z - 1), sum=(2, 6), gather=(5, 2, 6), out=(2, 2), gc=(2, n_z),
        gz=(4, n_z - 1), line=(2, n_z + 1), vc=(1,), vt=(n_t - 1,), vz=(n_z - 1,), en=(2,),
        wt=(n_t - 1,), wc=(n_t - 1,), ta=(2, n_t - 1), tb=(2, n_t - 1), oc=(n_t,), ot=(n_t - 1,),
    ).items():
        sems[name + "_s"] = shape
        sems[name + "_r"] = shape
    sems["out_l"] = (2, 2)
    names = [*ins, *outs, *scratch, *sems]
    return pl.pallas_call(
        functools.partial(layers_kernel, n_z, n_t, rows, width, cols, names),
        out_shape=[jax.ShapeDtypeStruct(shape, dtype) for _, shape, dtype in outs.values()],
        in_specs=list(ins.values()),
        out_specs=[spec for spec, _, _ in outs.values()],
        scratch_shapes=[
            *(pltpu.VMEM(shape, dtype) for shape, dtype in scratch.values()),
            *(sem(shape) for shape in sems.values()),
        ],
        compiler_params=pltpu.CompilerParams(
            collective_id=0, has_side_effects=True, vmem_limit_bytes=VMEM_LIMIT
        ),
        name="layers",
    )(x, g, *small, wa, wo, wu, wd)


def outputs_kernel(
    items, acts, grads, g_up, g_down, g_attn, g_out, vec, ent,
    acts_out, grads_out, ent_out, occ_out, attn_out, qv_out, out_out, out_b, norm1, up_out, up_b, down_out,
    down_b, norm2,
):
    acts_out[...] = acts[...]
    grads_out[...] = grads[...].astype(f32)

    @pl.when(pl.program_id(0) == 0)
    def _():
        heads, micros, clusters = ent_out.shape
        cols = qv_out.shape[1]
        for m in range(micros):
            ent_out[:, m, :] = ent[m].T[:heads, :clusters]
        lane = lax.broadcasted_iota(jnp.int32, (items.shape[0], ITEMS), 1)
        for c in range(clusters):
            row = jnp.zeros(lane.shape, f32)
            labels = items[:, c * CLUSTER : (c + 1) * CLUSTER]
            for i in range(ITEMS):
                count = jnp.sum((labels == i).astype(f32), axis=1, keepdims=True)
                row = jnp.where(lane == i, count, row)
            occ_out[:, c, :] = row
        attn_out[...] = g_attn[...]
        out_out[...] = g_out[...].T
        up_out[...] = g_up[...]
        down_out[...] = g_down[...]
        qv_out[0:1] = vec[7:8, :cols]
        qv_out[1:2] = vec[7:8, 2 * cols : 3 * cols]
        norm2[...] = vec[0:2]
        down_b[...] = vec[2:3]
        norm1[...] = vec[3:5]
        out_b[...] = vec[5:6]
        up_b[...] = vec[6:7]


def finish_outputs(items, acts, grads, g_up, g_down, g_attn, g_out, vec, ent):
    micros, rows, width = acts.shape
    clusters, (slab, cols) = rows // CLUSTER, g_out.shape
    part = pl.BlockSpec((2, rows, width), lambda i: (i, 0, 0))
    whole = pl.BlockSpec(memory_space=pltpu.VMEM)
    shapes = [
        (acts.shape, bf16), (acts.shape, f32), ((cols // HEAD_DIM, micros, clusters), f32),
        ((micros, clusters, ITEMS), f32), (g_attn.shape, f32), ((2, cols), f32), ((cols, slab), f32),
        ((1, width), f32), ((2, width), f32), (g_up.shape, f32), ((1, width), f32), (g_down.shape, f32),
        ((1, width), f32), ((2, width), f32),
    ]

    small = (g_up, g_down, g_attn, g_out, vec, ent)
    return pl.pallas_call(
        outputs_kernel,
        grid=(micros // 2,),
        out_shape=[jax.ShapeDtypeStruct(shape, dtype) for shape, dtype in shapes],
        in_specs=[whole, part, part, *([whole] * len(small))],
        out_specs=[part, part, *([whole] * (len(shapes) - 2))],
        compiler_params=pltpu.CompilerParams(vmem_limit_bytes=VMEM_LIMIT),
        name="outputs",
    )(items, acts, grads, *small)


def shards(
    inputs, out_grad, items, send_order, recv_order,
    attn_weight, qv_bias, out_weight, out_bias, norm_first,
    up_weight, up_bias, down_weight, down_bias, norm_second,
):
    micros, rows, width = inputs.shape
    n_z = lax.axis_size("dp")
    cols = attn_weight.shape[3]
    small = (
        items[0], send_order[0], recv_order[0], qv_bias[0], out_bias, norm_first[0], up_bias,
        down_bias, norm_second[0],
    )
    wa = jnp.transpose(attn_weight[0], (1, 2, 0)).reshape(3 * cols, width)
    acts, grads, g_up, g_down, g_attn, g_out, vec, ent = run_layers(
        n_z, inputs, out_grad, small, wa, out_weight[0], up_weight[0], down_weight[0]
    )
    (
        acts, grads, entropy, occupancy, attn, qv, out_w, out_b, norm1, up, up_b, down, down_b, norm2,
    ) = finish_outputs(items[0], acts, grads, g_up, g_down, g_attn, g_out, vec, ent)
    results = (
        acts, grads, jnp.transpose(entropy, (1, 2, 0)), occupancy, jnp.transpose(attn, (1, 0, 2)), qv, out_w, out_b[0], norm1, up,
        up_b[0], down.T, down_b[0], norm2,
    )
    return tuple(value[None] for value in results)


def solution(mesh):
    return jax.shard_map(
        shards,
        mesh=mesh,
        in_specs=(
            P(None, "dp", None),
            P(None, "dp", None),
            P("section", None, "dp"),
            P("section", None, "dp", None),
            P("section", None, "dp", None),
            P("section", None, None, "tensor"),
            P("section", None, "tensor"),
            P("section", "tensor", None),
            P("section", None),
            P("section", None, None),
            P("section", None, "tensor"),
            P("section", "tensor"),
            P("section", "tensor", None),
            P("section", None),
            P("section", None, None),
        ),
        out_specs=(
            P("section", None, "dp", None),
            P("section", None, "dp", None),
            P("section", None, "dp", "tensor"),
            P("section", None, "dp", None),
            P("section", "dp", None, "tensor"),
            P("section", None, "tensor"),
            P("section", "tensor", "dp"),
            P("section", None),
            P("section", None, None),
            P("section", "dp", "tensor"),
            P("section", "tensor"),
            P("section", "tensor", "dp"),
            P("section", None),
            P("section", None, None),
        ),
        check_vma=False,
    )
```

```python
import functools

import jax
import jax.numpy as jnp
from jax import lax
from jax.experimental import pallas as pl
from jax.experimental.pallas import tpu as pltpu
from jax.sharding import PartitionSpec as P

HEAD_DIM = 64
CLUSTER = 128
ITEMS = 6
EPSILON = 1e-06
MESH = pl.DeviceIdType.MESH
VMEM_LIMIT = 63 * 1024 * 1024
bf16 = jnp.bfloat16
f32 = jnp.float32


def nn(a, b):
    return lax.dot_general(a, b, (((1,), (0,)), ((), ())), preferred_element_type=f32)


def nt(a, b):
    return lax.dot_general(a, b, (((1,), (1,)), ((), ())), preferred_element_type=f32)


def tn(a, b):
    return lax.dot_general(a, b, (((0,), (0,)), ((), ())), preferred_element_type=f32)


def loop(count, body):
    def step(index, carry):
        body(index)
        return carry

    lax.fori_loop(0, count, step, 0)


def rows_at(index, size):
    return pl.ds(pl.multiple_of(index * size, size), size)


class Bag:
    def __init__(self, names, values):
        self.__dict__.update(zip(names, values, strict=True))


def place_rows(row, first, count):
    numbers = lax.broadcasted_iota(jnp.int32, (count, row.shape[1]), 0) + first
    return (numbers == row).astype(bf16)


def by_head(block, heads):
    lane = lax.broadcasted_iota(jnp.int32, block.shape, 1) // HEAD_DIM
    return jnp.concatenate([jnp.where(lane == h, block, jnp.zeros_like(block)) for h in range(heads)])


def fold_heads(stacked, heads):
    count = stacked.shape[0] // heads
    lane = lax.broadcasted_iota(jnp.int32, (count, stacked.shape[1]), 1) // HEAD_DIM
    total = jnp.where(lane == 0, stacked[:count], 0.0)
    for h in range(1, heads):
        total = jnp.where(lane == h, stacked[h * count : (h + 1) * count], total)
    return total


def softmax_parts(scores, same):
    masked = jnp.where(same, scores, -1e30)
    centred = masked - jnp.max(masked, axis=-1, keepdims=True)
    grown = jnp.exp(centred)
    total = jnp.sum(grown, axis=-1, keepdims=True)
    return grown / total, centred, total


def same_item(row):
    wide = jnp.broadcast_to(row.astype(f32), (row.shape[1], row.shape[1]))
    return wide == wide.T


def normalise(values):
    centre = jnp.mean(values, axis=-1, keepdims=True)
    spread = values - centre
    second = jnp.mean(spread * spread, axis=-1, keepdims=True)
    inverse = lax.rsqrt(second + EPSILON)
    return spread * inverse, inverse


def norm_backward(grad, normed, inverse, gain):
    scaled = grad * gain
    first = jnp.mean(scaled, axis=-1, keepdims=True)
    second = jnp.mean(scaled * normed, axis=-1, keepdims=True)
    return inverse * (scaled - first - normed * second)


def column_sum(value):
    return jnp.sum(value.astype(f32), axis=0, keepdims=True)


def remote(src, dst, sems, device):
    return pltpu.make_async_remote_copy(
        src_ref=src, dst_ref=dst, send_sem=sems[0], recv_sem=sems[1],
        device_id=device, device_id_type=MESH,
    )


def layers_kernel(n_z, n_t, rows, width, cols, names, *refs):
    r = Bag(names, refs)
    heads, half_width = cols // HEAD_DIM, width // 2
    scale = HEAD_DIM**-0.5
    core, z, t = lax.axis_index("section"), lax.axis_index("dp"), lax.axis_index("tensor")
    other = {"section": 1 - core}
    step_x, step_y = 1 - 2 * lax.rem(t, 2), 2 - 4 * (t // 2)
    t_x, t_y = t + step_x, t + step_y
    t_far = t + step_x + step_y
    piece, own = rows // n_z, rows // n_t
    chunk_rows = max(piece, 128)
    chunks, per_chunk = rows // chunk_rows, chunk_rows // piece
    mine = rows_at(t, own)
    weights = ("wa", "wo", "wu", "wd")

    def load(i):
        if i < 2:
            return pltpu.make_async_copy(r.x_in.at[core * 2 + i], r.x.at[i], r.load_sem.at[i])
        if i < 4:
            return pltpu.make_async_copy(r.g_in.at[core * 2 + i - 2], r.g.at[i - 2], r.load_sem.at[i])
        if i == 5:
            return pltpu.make_async_copy(r.wo_in, r.wo.at[core, t], r.load_sem.at[i])
        name = weights[i - 4]
        return pltpu.make_async_copy(
            getattr(r, name + "_in"), getattr(r, name).at[core], r.load_sem.at[i]
        )

    def swap(i):
        sems = (r.swap_s.at[i], r.swap_r.at[i])
        if i == 4:
            return remote(r.idx.at[core], r.idx.at[core], sems, other)
        if i == 5:
            return remote(r.par.at[core], r.par.at[core], sems, other)
        if i == 1:
            return remote(r.wo_in, r.wo.at[core, t], sems, other)
        name = weights[i]
        return remote(getattr(r, name + "_in"), getattr(r, name).at[core], sems, other)

    def start():
        for i in (0, 4, 1, 5, 6, 7, 2, 3):
            load(i).start()
        for kind, index in enumerate((r.items_in, r.send_in, r.recv_in)):
            for i in range(4):
                for c in range(rows // 128):
                    cut = slice(c * 128, (c + 1) * 128)
                    row = index[i : i + 1, cut] if kind == 0 else index[i, :, cut]
                    r.idx[core, kind * 4 + i, c] = row
        r.par[core, 0:1, :] = jnp.zeros((1, width), f32)
        r.par[core, 0:1, :cols] = r.qv_in[0:1]
        r.par[core, 0:1, 2 * cols : 3 * cols] = r.qv_in[1:2]
        for first, value in ((1, r.bo_in), (2, r.norm1_in), (4, r.bu_in), (5, r.bd_in), (6, r.norm2_in)):
            r.par[core, first : first + value.shape[0], :] = value[...]
        r.vec[...] = jnp.zeros(r.vec.shape, f32)
        barrier = pltpu.get_barrier_semaphore()
        pl.semaphore_signal(barrier, inc=1, device_id=other, device_id_type=MESH)

        def greet_z(k):
            peer = lax.rem(z + 1 + k, n_z)
            pl.semaphore_signal(barrier, inc=1, device_id={"dp": peer}, device_id_type=MESH)

        def greet_t(k):
            peer = lax.rem(t + 1 + k, n_t)
            pl.semaphore_signal(barrier, inc=1, device_id={"tensor": peer}, device_id_type=MESH)

        loop(n_z - 1, greet_z)
        loop(n_t - 1, greet_t)
        pl.semaphore_wait(barrier, n_z + n_t - 1)
        for i in (4, 5, 0, 1):
            swap(i).start()
        for k in range(1, n_t):
            wo_copy(k).start()
        for i in (2, 3):
            swap(i).start()

    def need_small(layer):
        if layer in asked:
            return
        asked.add(layer)

        @pl.when(core != layer)
        def _():
            swap(4).wait_recv()
            swap(5).wait_recv()

    def wo_copy(k):
        return remote(
            r.wo_in, r.wo.at[core, t], (r.wt_s.at[k - 1], r.wt_r.at[k - 1]),
            {"tensor": lax.rem(t + k, n_t)},
        )

    def wo_on_copy(k):
        slab = r.wo.at[core, lax.rem(t - k + n_t, n_t)]
        return remote(slab, slab, (r.wc_s.at[k - 1], r.wc_r.at[k - 1]), other)

    def out_weight_on(l, m):
        load(5).wait()
        for k in range(1, n_t):
            wo_copy(k).wait_recv()
            wo_on_copy(k).start()

    asked = set()

    def need_weight(layer, i):
        if (layer, i) in asked:
            return
        asked.add((layer, i))

        if i != 1:

            @pl.when(core == layer)
            def _():
                load(4 + i).wait()

        @pl.when(core != layer)
        def _():
            swap(i).wait_recv()
            if i == 1:
                for k in range(1, n_t):
                    wo_on_copy(k).wait_recv()

    def index_cut(kind, layer, m, first, count):
        cuts = [
            r.idx[layer, kind * 4 + core * 2 + m, first // 128 + i] for i in range(count // 128)
        ]
        return cuts[0] if len(cuts) == 1 else jnp.concatenate(cuts, axis=1)

    def index_row(kind, layer, m):
        return index_cut(kind, layer, m, 0, rows)

    def par(layer, i, count=None):
        return r.par[layer, i : i + 1, : count or width]

    def z_copies(kind, m, k, src, dst, src_rest, dst_rest):
        peer = lax.rem(z + k, n_z)
        full = src.shape[1] // 128 * 128
        lanes = pl.ds(0, full)
        return [
            remote(
                src.at[rows_at(peer, piece), lanes], dst.at[rows_at(z, piece), lanes],
                (r.z_s.at[2 * kind, m, k - 1], r.z_r.at[2 * kind, m, k - 1]), {"dp": peer},
            ),
            remote(
                src_rest.at[peer], dst_rest.at[z],
                (r.z_s.at[2 * kind + 1, m, k - 1], r.z_r.at[2 * kind + 1, m, k - 1]), {"dp": peer},
            ),
        ]

    def z_chunk(kk):
        return lax.rem(z // per_chunk + 1 + kk, chunks)

    def z_send(kind, m, cc, rest, *refs):
        rest = rest.astype(f32)
        for j in range(per_chunk):
            upper = rest[j * piece : j * piece + piece // 2]
            lower = rest[j * piece + piece // 2 : (j + 1) * piece]
            refs[2][cc * per_chunk + j] = jnp.concatenate([upper, lower], axis=1).astype(bf16)

        def one(j):
            peer = cc * per_chunk + j
            k = lax.rem(peer - z + n_z, n_z)

            @pl.when(k > 0)
            def _():
                for copy in z_copies(kind, m, k, *refs):
                    copy.start()

        loop(per_chunk, one)

    def z_take(kind, m, src, dst, src_rest, dst_rest):
        def wait(k):
            for copy in z_copies(kind, m, k + 1, src, dst, src_rest, dst_rest):
                copy.wait()

        loop(n_z - 1, wait)
        full = src.shape[1] // 128 * 128
        here = rows_at(z, piece)
        dst[here, :full] = src[here, :full]
        dst_rest[z] = src_rest[z]

        def unpack(b):
            both = dst_rest[b].astype(f32)
            whole = jnp.concatenate([both[:, :HEAD_DIM], both[:, HEAD_DIM:]], axis=0)
            dst[rows_at(b, piece), full:] = whole.astype(bf16)

        loop(n_z, unpack)

    left, right = slice(0, half_width), slice(half_width, width)

    def sum_copy(m, j):
        peer = t_x if j in (0, 1, 5) else t_y
        return remote(
            r.sum_src.at[m, j], r.sum_dst.at[m, j], (r.sum_s.at[m, j], r.sum_r.at[m, j]),
            {"tensor": peer},
        )

    def sum_put(m, role, part):
        @pl.when(role == 0)
        def _():
            r.sum_own[m] = part

        @pl.when(role == 1)
        def _():
            r.sum_src[m, 1] = part[:, left].astype(bf16)
            r.sum_keep[m, 1] = part[:, right].astype(bf16)
            sum_copy(m, 1).start()

        @pl.when(role == 2)
        def _():
            r.sum_src[m, 3] = part[:, right].astype(bf16)
            r.sum_keep[m, 0] = part[:, left].astype(bf16)
            sum_copy(m, 3).start()

        @pl.when(role == 3)
        def _():
            r.sum_src[m, 0] = part[:, left].astype(bf16)
            sum_copy(m, 0).start()
            r.sum_src[m, 2] = part[:, right].astype(bf16)
            sum_copy(m, 2).start()

    def sum_mid(m):
        sum_copy(m, 0).wait_recv()
        r.sum_src[m, 4] = (r.sum_keep[m, 0].astype(f32) + r.sum_dst[m, 0].astype(f32)).astype(bf16)
        sum_copy(m, 4).start()
        sum_copy(m, 2).wait_recv()
        r.sum_src[m, 5] = (r.sum_keep[m, 1].astype(f32) + r.sum_dst[m, 2].astype(f32)).astype(bf16)
        sum_copy(m, 5).start()

    def sum_take(m):
        for j in (1, 3, 4, 5):
            sum_copy(m, j).wait_recv()
        for j in range(6):
            sum_copy(m, j).wait_send()
        added = jnp.concatenate(
            [
                r.sum_dst[m, 1].astype(f32) + r.sum_dst[m, 4].astype(f32),
                r.sum_dst[m, 3].astype(f32) + r.sum_dst[m, 5].astype(f32),
            ],
            axis=1,
        )
        return r.sum_own[m] + added

    def role_rows(role):
        return rows_at(t + lax.rem(role, 2) * step_x + (role // 2) * step_y, own)

    def gather_copy(kind, m, j, buf):
        first = (t, t, t, t, t_x, t_y)[j] * own
        low = j in (1, 2, 5)
        here = pl.ds(pl.multiple_of(first + (own // 2 if low else 0), own // 2), own // 2)
        return remote(
            buf.at[here], buf.at[here], (r.gather_s.at[kind, m, j], r.gather_r.at[kind, m, j]),
            {"tensor": t_x if j in (0, 1, 5) else t_y},
        )

    def gather_start(kind, m, buf):
        for j in (0, 2, 1, 3):
            gather_copy(kind, m, j, buf).start()

    def gather_on(kind, m, buf):
        gather_copy(kind, m, 0, buf).wait_recv()
        gather_copy(kind, m, 4, buf).start()
        gather_copy(kind, m, 2, buf).wait_recv()
        gather_copy(kind, m, 5, buf).start()

    def gather_near(kind, m, buf, j):
        gather_copy(kind, m, j, buf).wait_recv()

    def gather_far(kind, m, buf):
        gather_copy(kind, m, 4, buf).wait_recv()
        gather_copy(kind, m, 5, buf).wait_recv()

    def gather_rest(kind, m, buf):
        for j in (1, 3, 4, 5):
            gather_copy(kind, m, j, buf).wait_recv()
        gather_sent(kind, m, buf)

    def gather_sent(kind, m, buf):
        for j in range(6):
            gather_copy(kind, m, j, buf).wait_send()

    def gather_step(kind, m, role, buf, sent_on):
        @pl.when(role == 1)
        def _():
            if not sent_on:
                gather_on(kind, m, buf)
            gather_near(kind, m, buf, 1)

        @pl.when(role == 2)
        def _():
            gather_near(kind, m, buf, 3)

        @pl.when(role == 3)
        def _():
            gather_far(kind, m, buf)

    def out_local(kind, m, src, out):
        return pltpu.make_async_copy(src, out.at[core * 2 + m], r.out_l.at[kind, m])

    def out_away(kind, m, src, out):
        return remote(src, out.at[core * 2 + m], (r.out_s.at[kind, m], r.out_r.at[kind, m]), other)

    def out_start(kind, layer, m, src, out):
        @pl.when(core == layer)
        def _():
            out_local(kind, m, src, out).start()

        @pl.when(core != layer)
        def _():
            out_away(kind, m, src, out).start()

    def out_wait(kind, layer, m, src, out):
        @pl.when(core == layer)
        def _():
            out_local(kind, m, src, out).wait()

        @pl.when(core != layer)
        def _():
            out_away(kind, m, src, out).wait_send()

    rest_z, rest_m = 3 * cols - HEAD_DIM, cols - HEAD_DIM

    def z_big(m):
        return r.zs.at[m], r.zr.at[m], r.zs_rest.at[m], r.zr_rest.at[m]

    def z_home(m):
        return r.dmr.at[m], r.ms.at[m], r.ms_rest.at[m], r.mr_rest.at[m]

    def z_back(m):
        return r.dmt.at[m], r.dmr.at[m], r.ms_rest.at[m], r.mr_rest.at[m]

    def project(l, m):
        need_small(l)
        need_weight(l, 0)
        if l == 0:
            load(m).wait()

        def chunk(kk):
            cc = z_chunk(kk)
            here = rows_at(cc, chunk_rows)
            numbers = lax.broadcasted_iota(jnp.int32, (rows, chunk_rows), 0)
            pick = (numbers == index_cut(1, l, m, cc * chunk_rows, chunk_rows)).astype(bf16)
            moved = tn(pick, r.x[m]).astype(bf16)
            r.xp[l, m, here] = moved
            block = (nt(moved, r.wa[l]) + par(l, 0, 3 * cols)).astype(bf16)
            r.zs[m, here] = block[:, :rest_z]
            z_send(0, m, cc, block[:, rest_z:], *z_big(m))

        loop(chunks, chunk)

    def attend(l, m):
        z_take(0, m, *z_big(m))
        lane = lax.broadcasted_iota(jnp.int32, (1, 128), 1)

        def cluster(c):
            here = rows_at(c, CLUSTER)
            numbers = lax.broadcasted_iota(jnp.int32, (rows, CLUSTER), 0)
            pick = (numbers == index_cut(2, l, m, c * CLUSTER, CLUSTER)).astype(bf16)
            block = tn(pick, r.zr[m]).astype(bf16)
            r.grouped[l, m, here] = block
            queries, keys, values = (block[:, i * cols : (i + 1) * cols] for i in range(3))
            scores = nt(queries, by_head(keys, heads)) * scale
            same = same_item(index_cut(0, l, m, c * CLUSTER, CLUSTER))
            probs = []
            log_row = jnp.zeros((1, 128), f32)
            for h in range(heads):
                cut = slice(h * CLUSTER, (h + 1) * CLUSTER)
                prob, centred, total = softmax_parts(scores[:, cut], same)
                inner = jnp.sum(jnp.where(same, prob * centred, 0.0), axis=-1, keepdims=True)
                entropy = jnp.mean(jnp.log(total) - inner, axis=0, keepdims=True)
                log_row = jnp.where(lane == h, entropy, log_row)
                probs.append(prob.astype(bf16))
            r.entropy[l, m, pl.ds(c, 1)] = log_row
            mixed = nn(jnp.concatenate(probs, axis=1), by_head(values, heads))
            r.dmt[m, here] = mixed.astype(bf16)

        loop(rows // CLUSTER, cluster)

        def home(kk):
            cc = z_chunk(kk)
            here = rows_at(cc, chunk_rows)
            one_hot = place_rows(index_row(2, l, m), cc * chunk_rows, chunk_rows)
            block = nn(one_hot, r.dmt[m]).astype(bf16)
            r.dmr[m, here] = block
            z_send(1, m, cc, block[:, rest_m:], *z_home(m))

        loop(chunks, home)

    def heads_copy(l, m, k):
        peer = lax.rem(t + k, n_t)
        return remote(
            r.ms.at[m, rows_at(peer, own)], r.mt.at[l, m, t],
            (r.ta_s.at[m, k - 1], r.ta_r.at[m, k - 1]), {"tensor": peer},
        )

    def out_project(l, m):
        z_take(1, m, *z_home(m))
        for k in (2, 1, 3):
            heads_copy(l, m, k).start()
        r.mt[l, m, t] = r.ms[m, mine]

    def middle(l, m):
        sum_mid(m)

    def first_norm(l, m):
        need_weight(l, 1)
        for k in range(1, n_t):
            heads_copy(l, m, k).wait()
        total = r.xp[l, m, mine].astype(f32) + par(l, 1)
        for s in range(n_t):
            total = total + nn(r.mt[l, m, s], r.wo[l, s])
        normed, inverse = normalise(total)
        hidden = normed * par(l, 2) + par(l, 3)
        r.n1[l, m] = normed.astype(bf16)
        r.inv1[l, m] = jnp.broadcast_to(inverse, (own, 128))
        r.hid[m] = hidden
        r.hfull[l, m, mine] = hidden.astype(bf16)
        gather_start(0, m, r.hfull.at[l, m])

    def hidden_on(l, m):
        asked.add((l, m, 0))
        gather_on(0, m, r.hfull.at[l, m])

    def b_hidden_on(l, m):
        asked.add((l, m, 2))
        gather_on(2, m, r.db.at[m])

    def feed(l, m):
        need_weight(l, 2)
        need_weight(l, 3)

        def part(role):
            gather_step(0, m, role, r.hfull.at[l, m], (l, m, 0) in asked)
            here = role_rows(role)
            up = nn(r.hfull[l, m, here], r.wu[l]) + par(l, 4)
            square = up * up
            tanh = jnp.tanh(0.7978845608028654 * up * (1.0 + 0.044715 * square))
            half = 0.5 * (1.0 + tanh)
            slope = 0.7978845608028654 * (1.0 + 3 * 0.044715 * square)
            r.gp[l, m, here] = (half + 0.5 * up * (1.0 - tanh * tanh) * slope).astype(bf16)
            active = (up * half).astype(bf16)
            r.act[l, m, here] = active
            sum_put(m, role, nn(active, r.wd[l]))

        loop(n_t, part)

    def second_norm(l, m):
        gather_sent(0, m, r.hfull.at[l, m])
        total = sum_take(m) + par(l, 5)
        normed, inverse = normalise(r.hid[m] + total)
        r.n2[l, m] = normed.astype(bf16)
        r.inv2[l, m] = jnp.broadcast_to(inverse, (own, 128))
        r.ag[m, mine] = (normed * par(l, 6) + par(l, 7)).astype(bf16)
        gather_start(1, m, r.ag.at[m])

    def out_on(l, m):
        gather_on(1, m, r.ag.at[m])

    def to_tokens(l, m, dst, buf):
        def chunk(cc):
            one_hot = place_rows(index_row(1, l, m), cc * 128, 128)
            dst[m, rows_at(cc, 128)] = nn(one_hot, buf[m]).astype(bf16)

        loop(rows // 128, chunk)

    def out_tokens(l, m):
        gather_rest(1, m, r.ag.at[m])
        if l == 1:
            out_wait(0, 0, m, r.x.at[m], r.acts)
        to_tokens(l, m, r.x, r.ag)
        out_start(0, l, m, r.x.at[m], r.acts)

    def add_vec(l, index, value):
        r.vec[l, index : index + 1, : value.shape[1]] += value

    def b_second_norm(l, m):
        if l == 1:
            load(2 + m).wait()
        numbers = lax.broadcasted_iota(jnp.int32, (rows, own), 0)
        pick = (numbers == index_cut(1, l, m, t * own, own)).astype(bf16)
        up = tn(pick, r.g[m])
        normed = r.n2[l, m].astype(f32)
        down = norm_backward(up, normed, r.inv2[l, m][:, :1], par(l, 6))
        r.hid[m] = down
        low = down.astype(bf16)
        r.db[m, mine] = low
        gather_start(2, m, r.db.at[m])
        add_vec(l, 0, column_sum(up * normed))
        add_vec(l, 1, column_sum(up))
        add_vec(l, 2, column_sum(low))

    def b_feed(l, m):
        def part(role):
            gather_step(2, m, role, r.db.at[m], (l, m, 2) in asked)
            here = role_rows(role)
            low = (nt(r.db[m, here], r.wd[l]) * r.gp[l, m, here].astype(f32)).astype(bf16)
            r.gp[l, m, here] = low
            sum_put(m, role, nt(low, r.wu[l]))

        loop(n_t, part)

    def grad_slabs(ref, value, lanes):
        ref[:, :, lanes] = value.reshape(n_z, width // n_z, value.shape[1]).astype(bf16)

    def feed_weights(l, m):
        for i in range(2):
            gather_sent(2, i, r.db.at[i])
            add_vec(l, 6, column_sum(r.gp[l, i]))

        def block(c):
            cut = rows_at(c, 256)
            up = tn(r.hfull[l, 0], r.gp[l, 0, :, cut]) + tn(r.hfull[l, 1], r.gp[l, 1, :, cut])
            grad_slabs(r.gs_feed, up, cut)
            down = tn(r.db[0], r.act[l, 0, :, cut]) + tn(r.db[1], r.act[l, 1, :, cut])
            grad_slabs(r.gs_feed, down, pl.ds(pl.multiple_of(width + c * 256, 256), 256))

        loop(width // 256, block)
        grads_send(0, l, r.gs_feed, r.gr_feed)

    def b_first_norm(l, m):
        up = r.hid[m] + sum_take(m)
        normed = r.n1[l, m].astype(f32)
        down = norm_backward(up, normed, r.inv1[l, m][:, :1], par(l, 2))
        r.dres[m] = down
        low = down.astype(bf16)
        r.da[m] = low

        def part(kk):
            k = lax.rem(kk + 1, n_t)
            peer = lax.rem(t + k, n_t)
            block = nt(low, r.wo[l, peer]).astype(bf16)

            @pl.when(k > 0)
            def _():
                r.ms[m, rows_at(peer, own)] = block
                rows_copy(m, k).start()

            @pl.when(k == 0)
            def _():
                r.dmt[m, mine] = block

        loop(n_t, part)
        add_vec(l, 3, column_sum(up * normed))
        add_vec(l, 4, column_sum(up))
        add_vec(l, 5, column_sum(low))

    def rows_copy(m, k):
        peer = lax.rem(t + k, n_t)
        return remote(
            r.ms.at[m, rows_at(peer, own)], r.dmt.at[m, mine], (r.tb_s.at[m, k - 1], r.tb_r.at[m, k - 1]),
            {"tensor": peer},
        )

    def out_back(l, m):
        for k in range(1, n_t):
            rows_copy(m, k).wait()

        def chunk(kk):
            cc = z_chunk(kk)
            z_send(2, m, cc, r.dmt[m, rows_at(cc, chunk_rows), rest_m:], *z_back(m))

        loop(chunks, chunk)

    def out_weights(l, m):
        for s in range(n_t):
            value = tn(r.da[0], r.mt[l, 0, s]) + tn(r.da[1], r.mt[l, 1, s])
            r.gs_out[s] = value.reshape(n_z, width // n_z, cols).astype(bf16)

        @pl.when(core != l)
        def _():
            for k in range(n_t):
                out_core_copy(lax.rem(t + 1 + k, n_t)).start()

    def b_attend(l, m):
        z_take(2, m, *z_back(m))

        def cluster(c):
            here = rows_at(c, CLUSTER)
            numbers = lax.broadcasted_iota(jnp.int32, (rows, CLUSTER), 0)
            pick = (numbers == index_cut(2, l, m, c * CLUSTER, CLUSTER)).astype(bf16)
            dmix = tn(pick, r.dmr[m]).astype(bf16)
            block = r.grouped[l, m, here]
            queries, keys, values = (block[:, i * cols : (i + 1) * cols] for i in range(3))
            keys_by_head = by_head(keys, heads)
            scores = nt(queries, keys_by_head) * scale
            same = same_item(index_cut(0, l, m, c * CLUSTER, CLUSTER))
            dprob = nt(dmix, by_head(values, heads))
            probs, dscores = [], []
            for h in range(heads):
                cut = slice(h * CLUSTER, (h + 1) * CLUSTER)
                prob = softmax_parts(scores[:, cut], same)[0]
                outer = prob * dprob[:, cut]
                dscore = outer - prob * jnp.sum(outer, axis=-1, keepdims=True)
                probs.append(prob.astype(bf16))
                dscores.append(dscore.astype(bf16))
            prob_all = jnp.concatenate(probs, axis=1)
            dscore_all = jnp.concatenate(dscores, axis=1)
            dqueries = nn(dscore_all, keys_by_head) * scale
            dkeys = fold_heads(tn(dscore_all, queries), heads) * scale
            dvalues = fold_heads(tn(prob_all, dmix), heads)
            r.grouped[l, m, here] = jnp.concatenate([dqueries, dkeys, dvalues], axis=1).astype(bf16)

        loop(rows // CLUSTER, cluster)

        def home(kk):
            cc = z_chunk(kk)
            here = rows_at(cc, chunk_rows)
            one_hot = place_rows(index_row(2, l, m), cc * chunk_rows, chunk_rows)
            block = nn(one_hot, r.grouped[l, m]).astype(bf16)
            r.zs[m, here] = block[:, :rest_z]
            z_send(3, m, cc, block[:, rest_z:], *z_big(m))

        loop(chunks, home)

    def in_project(l, m):
        z_take(3, m, *z_big(m))

        def part(kk):
            role = 3 - kk
            sum_put(m, role, nn(r.zr[m, role_rows(role)], r.wa[l]))

        loop(n_t, part)

    def in_weights(l, m):
        for i in range(2):
            add_vec(l, 7, column_sum(r.zr[i]))
        for first in range(0, 3 * cols, 256):
            cut = slice(first, min(first + 256, 3 * cols))
            value = tn(r.xp[l, 0], r.zr[0, :, cut]) + tn(r.xp[l, 1], r.zr[1, :, cut])
            grad_slabs(r.gs_attn, value, cut)
        grads_send(1, l, r.gs_attn, r.gr_attn)

    def layer_input(l, m):
        r.ag[m, mine] = (r.dres[m] + sum_take(m)).astype(bf16)
        gather_start(4, m, r.ag.at[m])

    def b_out_on(l, m):
        gather_on(4, m, r.ag.at[m])

    def b_tokens(l, m):
        gather_rest(4, m, r.ag.at[m])
        if l == 0:
            out_wait(1, 1, m, r.g.at[m], r.grads)
        to_tokens(l, m, r.g, r.ag)
        out_start(1, l, m, r.g.at[m], r.grads)

    def grad_core_copy(kind, k, src, dst):
        return remote(src.at[k], dst.at[k], (r.gc_s.at[kind, k], r.gc_r.at[kind, k]), other)

    def grad_z_copy(kind, k, src, dst, lanes=slice(None)):
        peer = lax.rem(z + k, n_z)
        return remote(
            src.at[peer, :, lanes], dst.at[k - 1, :, lanes], (r.gz_s.at[kind, k - 1], r.gz_r.at[kind, k - 1]),
            {"dp": peer},
        )

    def grads_send(kind, l, src, dst):
        @pl.when(core != l)
        def _():
            loop(n_z, lambda k: grad_core_copy(kind, lax.rem(z + 1 + k, n_z), src, dst).start())

    def grads_add(kind, src, came, k, wait, lanes):
        peer = lax.rem(z + k, n_z)
        if wait:
            grad_core_copy(kind, peer, src, came).wait_recv()
        total = src[peer, :, lanes].astype(f32) + came[peer, :, lanes].astype(f32)
        src[peer, :, lanes] = total.astype(bf16)

    def grads_part(kind, sem, l, src, came, dst, part, wait, lanes):
        @pl.when(core == l)
        def _():
            first, last = part * (n_z - 1) // 3, (part + 1) * (n_z - 1) // 3

            def one(i):
                grads_add(kind, src, came, first + 1 + i, wait, lanes)
                grad_z_copy(sem, first + 1 + i, src, dst, lanes).start()

            loop(last - first, one)

    def grads_end(kind, sems, l, src, came, dst, outs):
        @pl.when(core == l)
        def _():
            lanes = src.shape[2] // len(sems)
            for i in range(len(sems)):
                grads_add(kind, src, came, 0, i == 0, slice(i * lanes, (i + 1) * lanes))
            cuts, first = [], 0
            for out in outs:
                cuts.append(slice(first, first + out.shape[-1]))
                first += out.shape[-1]
            for out, cut in zip(outs, cuts):
                out[...] = src[z, :, cut].astype(f32)

            def one(k):
                for i, sem in enumerate(sems):
                    grad_z_copy(sem, k + 1, src, dst, slice(i * lanes, (i + 1) * lanes)).wait()
                for out, cut in zip(outs, cuts):
                    out[...] += dst[k, :, cut].astype(f32)

            loop(n_z - 1, one)

        @pl.when(core != l)
        def _():
            loop(n_z, lambda k: grad_core_copy(kind, k, src, came).wait_send())

    def line_copy(half, c, slot, step):
        lanes = slice(half * width, (half + 1) * width)
        return remote(
            r.gs_feed.at[c, :, lanes], r.gz_feed.at[slot, :, lanes],
            (r.line_s.at[half, c], r.line_r.at[half, slot]), {"dp": z + step},
        )

    def line_add(half, c, slot, came):
        lanes = slice(half * width, (half + 1) * width)
        grads_add(0, r.gs_feed, r.gr_feed, c - z, half == 0, lanes)

        @pl.when(came)
        def _():
            line_copy(half, c, slot, 0).wait_recv()
            total = r.gs_feed[c, :, lanes].astype(f32) + r.gz_feed[slot, :, lanes].astype(f32)
            r.gs_feed[c, :, lanes] = total.astype(bf16)

    def line_part(half, part, l):
        @pl.when(core == l)
        def _():
            first, last = part * (n_z - 1) // 3, (part + 1) * (n_z - 1) // 3

            def one(i):
                far = n_z - 1 - first - i

                @pl.when(z + far < n_z)
                def _():
                    line_add(half, z + far, z + far, z > 0)
                    line_copy(half, z + far, z + far, 1).start()

                @pl.when(z - far >= 0)
                def _():
                    line_add(half, z - far, z - far, z < n_z - 1)
                    slot = jnp.where(far == 1, n_z, z - far)
                    line_copy(half, z - far, slot, -1).start()

            loop(last - first, one)

    def line_end(l):
        @pl.when(core == l)
        def _():
            for half, out in enumerate((r.g_up, r.g_down)):
                lanes = slice(half * width, (half + 1) * width)
                line_add(half, z, z, z > 0)
                out[...] = r.gs_feed[z, :, lanes].astype(f32)

                @pl.when(z < n_z - 1)
                def _():
                    line_copy(half, z, n_z, 0).wait_recv()
                    out[...] += r.gz_feed[n_z, :, lanes].astype(f32)

                def sent(k):
                    line_copy(half, lax.rem(z + 1 + k, n_z), 0, 0).wait_send()

                loop(n_z - 1, sent)

        @pl.when(core != l)
        def _():
            loop(n_z, lambda k: grad_core_copy(0, k, r.gs_feed, r.gr_feed).wait_send())

    def feed_part(i):
        return lambda l, m: line_part(i % 2, i // 2, l)

    def attn_part(i):
        return lambda l, m: grads_part(
            1, 2, l, r.gs_attn, r.gr_attn, r.gz_attn, i, True, slice(None)
        )

    feed_0, feed_1, feed_2, feed_3, feed_4, feed_5 = (feed_part(i) for i in range(6))
    attn_0, attn_1, attn_2 = (attn_part(i) for i in range(3))

    def feed_end(l, m):
        line_end(l)

    def attn_end(l, m):
        grads_end(1, (2,), l, r.gs_attn, r.gr_attn, r.gz_attn, tuple(r.g_attn.at[i] for i in range(3)))

    def out_core_copy(s):
        return remote(r.gs_out.at[s], r.gr_out.at[s], (r.oc_s.at[s], r.oc_r.at[s]), other)

    def out_t_copy(k):
        peer = lax.rem(t + k, n_t)
        return remote(
            r.gs_out.at[peer], r.gt_out.at[k - 1], (r.ot_s.at[k - 1], r.ot_r.at[k - 1]),
            {"tensor": peer},
        )

    def out_z_copy(k):
        peer = lax.rem(z + k, n_z)
        return remote(
            r.gs_out.at[t, peer], r.gz_out.at[k - 1], (r.gz_s.at[3, k - 1], r.gz_r.at[3, k - 1]),
            {"dp": peer},
        )

    def out_sum_t(l, m):
        @pl.when(core == l)
        def _():
            for kk in range(n_t):
                k = (kk + 1) % n_t
                s = lax.rem(t + k, n_t)
                out_core_copy(s).wait_recv()
                r.gs_out[s] = (r.gs_out[s].astype(f32) + r.gr_out[s].astype(f32)).astype(bf16)
                if k > 0:
                    out_t_copy(k).start()

    def out_sum_z(l, m):
        @pl.when(core == l)
        def _():
            for k in range(1, n_t):
                out_t_copy(k).wait()
            total = r.gs_out[t].astype(f32)
            for k in range(1, n_t):
                total = total + r.gt_out[k - 1].astype(f32)
            r.gs_out[t] = total.astype(bf16)
            loop(n_z - 1, lambda k: out_z_copy(k + 1).start())

        @pl.when(core != l)
        def _():
            for s in range(n_t):
                out_core_copy(s).wait_send()

    def out_end(l, m):
        @pl.when(core == l)
        def _():
            r.g_out[...] = r.gs_out[t, z].astype(f32)

            def one(k):
                out_z_copy(k + 1).wait()
                r.g_out[...] += r.gz_out[k].astype(f32)

            loop(n_z - 1, one)

    def vec_copy(l):
        return remote(r.vec.at[l], r.vec_came, (r.vc_s.at[0], r.vc_r.at[0]), other)

    def vec_t_copy(k):
        return remote(
            r.vec_t.at[t], r.vec_t.at[t], (r.vt_s.at[k - 1], r.vt_r.at[k - 1]),
            {"tensor": lax.rem(t + k, n_t)},
        )

    def vec_z_copy(k):
        return remote(
            r.vec_z.at[z], r.vec_z.at[z], (r.vz_s.at[k - 1], r.vz_r.at[k - 1]),
            {"dp": lax.rem(z + k, n_z)},
        )

    def entropy_copy(l, m):
        return remote(
            r.entropy.at[l, m], r.ent.at[core * 2 + m], (r.en_s.at[m], r.en_r.at[m]), other
        )

    def vec_start(l, m):
        @pl.when(core != l)
        def _():
            vec_copy(l).start()
            for i in range(2):
                entropy_copy(l, i).start()

    def vec_sum_t(l, m):
        @pl.when(core == l)
        def _():
            for i in range(2):
                r.ent[core * 2 + i] = r.entropy[l, i]
            vec_copy(l).wait_recv()
            r.vec_t[t] = r.vec[l] + r.vec_came[...]
            for k in range(1, n_t):
                vec_t_copy(k).start()

    def vec_sum_z(l, m):
        @pl.when(core == l)
        def _():
            for k in range(1, n_t):
                vec_t_copy(k).wait()
            total = r.vec_t[0]
            for k in range(1, n_t):
                total = total + r.vec_t[k]
            lane_rows = lax.broadcasted_iota(jnp.int32, total.shape, 0)
            r.vec_z[z] = jnp.where(lane_rows < 6, total, r.vec_t[t])
            loop(n_z - 1, lambda k: vec_z_copy(k + 1).start())

    def vec_end(l, m):
        @pl.when(core == l)
        def _():
            loop(n_z - 1, lambda k: vec_z_copy(k + 1).wait())
            r.vec_out[...] = r.vec_z[0]

            def one(k):
                r.vec_out[...] += r.vec_z[k + 1]

            loop(n_z - 1, one)

        @pl.when(core != l)
        def _():
            vec_copy(l).wait_send()
            for i in range(2):
                entropy_copy(l, i).wait_send()

    def finish():
        for m in range(2):
            out_wait(0, 1, m, r.x.at[m], r.acts)
            out_wait(1, 0, m, r.g.at[m], r.grads)
            for kind, out, src in ((0, r.acts, r.x), (1, r.grads, r.g)):
                out_away(kind, m, src.at[m], out).wait_recv()
            entropy_copy(0, m).wait_recv()
        for i in range(6):
            swap(i).wait_send()
        for k in range(1, n_t):
            wo_copy(k).wait_send()
            wo_on_copy(k).wait_send()

    schedule = (
        (project, 0, 1), (attend, 0, 1), (out_weight_on, 0, 0), (out_project, 0, 1), (project, 0, 0),
        (first_norm, 0, 1), (feed, 0, 1), (attend, 0, 0), (middle, 0, 1), (out_project, 0, 0),
        (second_norm, 0, 1), (out_on, 0, 1), (first_norm, 0, 0), (out_tokens, 0, 1), (hidden_on, 0, 0),
        (project, 1, 1), (feed, 0, 0), (middle, 0, 0), (attend, 1, 1), (second_norm, 0, 0),
        (out_project, 1, 1), (out_on, 0, 0), (first_norm, 1, 1), (out_tokens, 0, 0), (project, 1, 0),
        (hidden_on, 1, 1), (feed, 1, 1), (middle, 1, 1), (attend, 1, 0), (second_norm, 1, 1),
        (b_second_norm, 1, 1), (out_on, 1, 1), (out_project, 1, 0), (b_feed, 1, 1), (first_norm, 1, 0),
        (out_tokens, 1, 1), (middle, 1, 1), (hidden_on, 1, 0), (feed, 1, 0), (b_first_norm, 1, 1),
        (middle, 1, 0), (out_back, 1, 1), (second_norm, 1, 0), (b_second_norm, 1, 0), (b_attend, 1, 1),
        (b_hidden_on, 1, 0), (out_on, 1, 0), (b_feed, 1, 0), (in_project, 1, 1), (feed_weights, 1, 1),
        (middle, 1, 0), (middle, 1, 1), (b_first_norm, 1, 0), (out_weights, 1, 1), (layer_input, 1, 1),
        (out_back, 1, 0), (b_out_on, 1, 1), (b_tokens, 1, 1), (b_second_norm, 0, 1), (feed_0, 1, 1),
        (feed_1, 1, 1), (b_attend, 1, 0), (b_hidden_on, 0, 1), (b_feed, 0, 1), (out_sum_t, 1, 1),
        (out_tokens, 1, 0), (feed_2, 1, 1), (in_project, 1, 0), (middle, 0, 1), (middle, 1, 0),
        (in_weights, 1, 1), (feed_3, 1, 1), (feed_4, 1, 1), (b_first_norm, 0, 1), (layer_input, 1, 0),
        (out_sum_z, 1, 1), (out_back, 0, 1), (b_out_on, 1, 0), (vec_start, 1, 1), (feed_5, 1, 1),
        (attn_0, 1, 1), (out_end, 1, 1), (b_tokens, 1, 0), (b_second_norm, 0, 0), (b_attend, 0, 1),
        (b_hidden_on, 0, 0), (vec_sum_t, 1, 1), (feed_end, 1, 1), (b_feed, 0, 0), (attn_1, 1, 1),
        (feed_weights, 0, 1), (feed_0, 0, 1), (middle, 0, 0), (vec_sum_z, 1, 1), (feed_1, 0, 1),
        (in_project, 0, 1), (attn_2, 1, 1), (b_first_norm, 0, 0), (out_weights, 0, 1), (feed_2, 0, 1),
        (middle, 0, 1), (vec_end, 1, 1), (out_sum_t, 0, 1), (out_back, 0, 0), (feed_3, 0, 1),
        (b_attend, 0, 0), (layer_input, 0, 1), (feed_4, 0, 1), (out_sum_z, 0, 1), (attn_end, 1, 1),
        (in_project, 0, 0), (in_weights, 0, 1), (b_out_on, 0, 1), (vec_start, 0, 1), (attn_0, 0, 1),
        (attn_1, 0, 1), (attn_2, 0, 1), (vec_sum_t, 0, 1), (middle, 0, 0), (layer_input, 0, 0),
        (b_tokens, 0, 1), (feed_5, 0, 1), (b_out_on, 0, 0), (vec_sum_z, 0, 1), (out_end, 0, 1),
        (b_tokens, 0, 0), (attn_end, 0, 1), (feed_end, 0, 1), (vec_end, 0, 1),
    )
    start()
    for step, layer, micro in schedule:
        step(layer, micro)
    finish()


def run_layers(n_z, x, g, small, wa, wo, wu, wd):
    micros, rows, width = x.shape
    cols, hidden = wo.shape[0], wu.shape[1]
    n_t = lax.axis_size("tensor")
    own, slab = rows // n_t, width // n_z
    pair = (2, rows)
    both = (2, 2, rows)
    anywhere, vmem = pl.BlockSpec(memory_space=pl.ANY), pl.BlockSpec(memory_space=pltpu.VMEM)
    ins = dict(
        x_in=anywhere, g_in=anywhere, items_in=vmem, send_in=vmem, recv_in=vmem, qv_in=vmem,
        bo_in=vmem, norm1_in=vmem, bu_in=vmem, bd_in=vmem, norm2_in=vmem, wa_in=anywhere, wo_in=anywhere,
        wu_in=anywhere, wd_in=anywhere,
    )
    outs = dict(
        acts=(anywhere, x.shape, bf16), grads=(anywhere, x.shape, bf16),
        g_up=(vmem, (slab, width), f32), g_down=(vmem, (slab, width), f32),
        g_attn=(vmem, (3, slab, cols), f32),
        g_out=(vmem, (slab, cols), f32),
        vec_out=(vmem, (8, width), f32), ent=(vmem, (micros, max(8, rows // CLUSTER), 128), f32),
    )
    sem = pltpu.SemaphoreType.DMA
    scratch = dict(
        x=((*pair, width), bf16), g=((*pair, width), bf16),
        wa=((2, 3 * cols, width), bf16), wo=((2, n_t, cols, width), bf16),
        wu=((2, width, hidden), bf16), wd=((2, hidden, width), bf16),
        idx=((2, 12, rows // 128, 1, 128), jnp.int32), par=((2, 8, width), f32),
        xp=((*both, width), bf16), grouped=((*both, 3 * cols), bf16), ms=((*pair, cols), bf16),
        mt=((2, 2, n_t, own, cols), bf16),
        n1=((2, 2, own, width), bf16), inv1=((2, 2, own, 128), f32), hfull=((*both, width), bf16),
        act=((*both, hidden), bf16), gp=((*both, hidden), bf16),
        n2=((2, 2, own, width), bf16), inv2=((2, 2, own, 128), f32),
        entropy=((2, 2, max(8, rows // CLUSTER), 128), f32),
        zs=((*pair, 3 * cols - HEAD_DIM), bf16), zs_rest=((2, n_z, rows // n_z // 2, 128), bf16),
        zr_rest=((2, n_z, rows // n_z // 2, 128), bf16), ms_rest=((2, n_z, rows // n_z // 2, 128), bf16),
        mr_rest=((2, n_z, rows // n_z // 2, 128), bf16), zr=((*pair, 3 * cols), bf16),
        dmr=((*pair, cols), bf16),
        sum_src=((2, 6, own, width // 2), bf16), sum_dst=((2, 6, own, width // 2), bf16),
        sum_keep=((2, 2, own, width // 2), bf16), sum_own=((2, own, width), f32),
        hid=((2, own, width), f32), dres=((2, own, width), f32),
        ag=((*pair, width), bf16), db=((*pair, width), bf16), da=((2, own, width), bf16),
        dmt=((*pair, cols), bf16),
        gs_feed=((n_z, slab, 2 * width), bf16), gr_feed=((n_z, slab, 2 * width), bf16),
        gz_feed=((n_z + 1, slab, 2 * width), bf16),
        gs_attn=((n_z, slab, 3 * cols), bf16), gr_attn=((n_z, slab, 3 * cols), bf16),
        gz_attn=((n_z - 1, slab, 3 * cols), bf16),
        gs_out=((n_t, n_z, slab, cols), bf16), gr_out=((n_t, n_z, slab, cols), bf16),
        gt_out=((n_t - 1, n_z, slab, cols), bf16), gz_out=((n_z - 1, slab, cols), bf16),
        vec=((2, 8, width), f32), vec_came=((8, width), f32), vec_t=((n_t, 8, width), f32),
        vec_z=((n_z, 8, width), f32),
    )
    sems = dict(load_sem=(8,))
    for name, shape in dict(
        swap=(6,), z=(8, 2, n_z - 1), sum=(2, 6), gather=(5, 2, 6), out=(2, 2), gc=(2, n_z),
        gz=(4, n_z - 1), line=(2, n_z + 1), vc=(1,), vt=(n_t - 1,), vz=(n_z - 1,), en=(2,),
        wt=(n_t - 1,), wc=(n_t - 1,), ta=(2, n_t - 1), tb=(2, n_t - 1), oc=(n_t,), ot=(n_t - 1,),
    ).items():
        sems[name + "_s"] = shape
        sems[name + "_r"] = shape
    sems["out_l"] = (2, 2)
    names = [*ins, *outs, *scratch, *sems]
    return pl.pallas_call(
        functools.partial(layers_kernel, n_z, n_t, rows, width, cols, names),
        out_shape=[jax.ShapeDtypeStruct(shape, dtype) for _, shape, dtype in outs.values()],
        in_specs=list(ins.values()),
        out_specs=[spec for spec, _, _ in outs.values()],
        scratch_shapes=[
            *(pltpu.VMEM(shape, dtype) for shape, dtype in scratch.values()),
            *(sem(shape) for shape in sems.values()),
        ],
        compiler_params=pltpu.CompilerParams(
            collective_id=0, has_side_effects=True, vmem_limit_bytes=VMEM_LIMIT
        ),
        name="layers",
    )(x, g, *small, wa, wo, wu, wd)


def outputs_kernel(
    items, acts, grads, g_up, g_down, g_attn, g_out, vec, ent,
    acts_out, grads_out, ent_out, occ_out, attn_out, qv_out, out_out, out_b, norm1, up_out, up_b, down_out,
    down_b, norm2,
):
    acts_out[...] = acts[...]
    grads_out[...] = grads[...].astype(f32)

    @pl.when(pl.program_id(0) == 0)
    def _():
        heads, micros, clusters = ent_out.shape
        cols = qv_out.shape[1]
        for m in range(micros):
            ent_out[:, m, :] = ent[m].T[:heads, :clusters]
        lane = lax.broadcasted_iota(jnp.int32, (items.shape[0], ITEMS), 1)
        for c in range(clusters):
            row = jnp.zeros(lane.shape, f32)
            labels = items[:, c * CLUSTER : (c + 1) * CLUSTER]
            for i in range(ITEMS):
                count = jnp.sum((labels == i).astype(f32), axis=1, keepdims=True)
                row = jnp.where(lane == i, count, row)
            occ_out[:, c, :] = row
        attn_out[...] = g_attn[...]
        out_out[...] = g_out[...].T
        up_out[...] = g_up[...]
        down_out[...] = g_down[...]
        qv_out[0:1] = vec[7:8, :cols]
        qv_out[1:2] = vec[7:8, 2 * cols : 3 * cols]
        norm2[...] = vec[0:2]
        down_b[...] = vec[2:3]
        norm1[...] = vec[3:5]
        out_b[...] = vec[5:6]
        up_b[...] = vec[6:7]


def finish_outputs(items, acts, grads, g_up, g_down, g_attn, g_out, vec, ent):
    micros, rows, width = acts.shape
    clusters, (slab, cols) = rows // CLUSTER, g_out.shape
    part = pl.BlockSpec((2, rows, width), lambda i: (i, 0, 0))
    whole = pl.BlockSpec(memory_space=pltpu.VMEM)
    shapes = [
        (acts.shape, bf16), (acts.shape, f32), ((cols // HEAD_DIM, micros, clusters), f32),
        ((micros, clusters, ITEMS), f32), (g_attn.shape, f32), ((2, cols), f32), ((cols, slab), f32),
        ((1, width), f32), ((2, width), f32), (g_up.shape, f32), ((1, width), f32), (g_down.shape, f32),
        ((1, width), f32), ((2, width), f32),
    ]

    small = (g_up, g_down, g_attn, g_out, vec, ent)
    return pl.pallas_call(
        outputs_kernel,
        grid=(micros // 2,),
        out_shape=[jax.ShapeDtypeStruct(shape, dtype) for shape, dtype in shapes],
        in_specs=[whole, part, part, *([whole] * len(small))],
        out_specs=[part, part, *([whole] * (len(shapes) - 2))],
        compiler_params=pltpu.CompilerParams(vmem_limit_bytes=VMEM_LIMIT),
        name="outputs",
    )(items, acts, grads, *small)


def shards(
    inputs, out_grad, items, send_order, recv_order,
    attn_weight, qv_bias, out_weight, out_bias, norm_first,
    up_weight, up_bias, down_weight, down_bias, norm_second,
):
    micros, rows, width = inputs.shape
    n_z = lax.axis_size("dp")
    cols = attn_weight.shape[3]
    small = (
        items[0], send_order[0], recv_order[0], qv_bias[0], out_bias, norm_first[0], up_bias,
        down_bias, norm_second[0],
    )
    wa = jnp.transpose(attn_weight[0], (1, 2, 0)).reshape(3 * cols, width)
    acts, grads, g_up, g_down, g_attn, g_out, vec, ent = run_layers(
        n_z, inputs, out_grad, small, wa, out_weight[0], up_weight[0], down_weight[0]
    )
    (
        acts, grads, entropy, occupancy, attn, qv, out_w, out_b, norm1, up, up_b, down, down_b, norm2,
    ) = finish_outputs(items[0], acts, grads, g_up, g_down, g_attn, g_out, vec, ent)
    results = (
        acts, grads, jnp.transpose(entropy, (1, 2, 0)), occupancy, jnp.transpose(attn, (1, 0, 2)), qv, out_w, out_b[0], norm1, up,
        up_b[0], down.T, down_b[0], norm2,
    )
    return tuple(value[None] for value in results)


def solution(mesh):
    return jax.shard_map(
        shards,
        mesh=mesh,
        in_specs=(
            P(None, "dp", None),
            P(None, "dp", None),
            P("section", None, "dp"),
            P("section", None, "dp", None),
            P("section", None, "dp", None),
            P("section", None, None, "tensor"),
            P("section", None, "tensor"),
            P("section", "tensor", None),
            P("section", None),
            P("section", None, None),
            P("section", None, "tensor"),
            P("section", "tensor"),
            P("section", "tensor", None),
            P("section", None),
            P("section", None, None),
        ),
        out_specs=(
            P("section", None, "dp", None),
            P("section", None, "dp", None),
            P("section", None, "dp", "tensor"),
            P("section", None, "dp", None),
            P("section", "dp", None, "tensor"),
            P("section", None, "tensor"),
            P("section", "tensor", "dp"),
            P("section", None),
            P("section", None, None),
            P("section", "dp", "tensor"),
            P("section", "tensor"),
            P("section", "tensor", "dp"),
            P("section", None),
            P("section", None, None),
        ),
        check_vma=False,
    )
```
